32 devices in a mesh: dp: 8 (over z, x), half: 2 (over core), tensor: 2 (over y).
Axes of the slice: x: 2, y: 2, z: 4, core: 2. Of those that a mesh axis runs over, the one named last changes fastest.
Arguments:
- inputs: bfloat16 [16, 1024, 768], P('dp', 'half'), as said below
- cotangent: bfloat16 [16, 1024, 768], P('dp', ('half', 'tensor')), may hold values from -6 to 6
- src_lengths: int32 [16], P('dp'), may hold values from 304 to 512
- tgt_mask: int32 [16, 512], P('dp'), may hold values 0 or 1
- timesteps: int32 [16], P('dp'), may hold values from 0 to 1999
- importance: float32 [2000], replicated, may hold values from 0.25 to 4
- w_qkv: bfloat16 [3, 768, 768], P(None, None, ('tensor', 'half')), as said below
- b_qv: float32 [2, 768], P(None, ('tensor', 'half')), may hold values from -3 to 3
- w_out: bfloat16 [768, 768], P(('tensor', 'half')), as said below
- b_out: float32 [768], replicated, may hold values from -3 to 3
- gain_one: float32 [768], replicated, may hold values from 0.5 to 1.5
- shift_one: float32 [768], replicated, may hold values from -2 to 2
- w_up: bfloat16 [768, 3072], P(None, ('tensor', 'half')), as said below
- b_up: float32 [3072], P(('tensor', 'half')), may hold values from -3 to 3
- w_down: bfloat16 [3072, 768], P(('tensor', 'half')), as said below
- b_down: float32 [768], replicated, may hold values from -3 to 3
- gain_two: float32 [768], replicated, may hold values from 0.5 to 1.5
- shift_two: float32 [768], replicated, may hold values from -2 to 2
- w_time1: float32 [128, 512], replicated, may hold values from -0.75 to 0.75
- time_bias1: float32 [512], replicated, may hold values from -3 to 3
- w_time2: float32 [512, 768], replicated, may hold values from -0.25 to 0.25
- time_bias2: float32 [768], replicated, may hold values from -3 to 3
Outputs:
- outputs: bfloat16 [16, 1024, 768], P('dp', ('half', 'tensor'))
- grad_inputs: float32 [16, 1024, 768], P('dp', ('half', 'tensor'))
- grad_w_qkv: float32 [3, 768, 768], P(None, None, ('tensor', 'half'))
- grad_b_qv: float32 [2, 768], P(None, ('tensor', 'half'))
- grad_w_out: float32 [768, 768], P(('tensor', 'half'))
- grad_b_out: float32 [768], replicated
- grad_gain_one: float32 [768], replicated
- grad_shift_one: float32 [768], replicated
- grad_w_up: float32 [768, 3072], P(None, ('tensor', 'half'))
- grad_b_up: float32 [3072], P(('tensor', 'half'))
- grad_w_down: float32 [3072, 768], P(('tensor', 'half'))
- grad_b_down: float32 [768], replicated
- grad_gain_two: float32 [768], replicated
- grad_shift_two: float32 [768], replicated
- grad_w_time1: float32 [128, 512], replicated
- grad_time_bias1: float32 [512], replicated
- grad_w_time2: float32 [512, 768], replicated
- grad_time_bias2: float32 [768], replicated
The draws below stay inside these ranges and needn't reach their ends.
Inputs may be any that keep to these rules, and one draw needn't show every extreme that they name: `inputs`: entries of order one. `w_qkv`: entries of about 768 ** -0.5. `w_out`: entries of about max(6, 1) ** -0.5. `w_up`: entries of about 768 ** -0.5. `w_down`: entries of about (1536) ** -0.5.
All inputs are finite; a program needn't handle non-finite values. No bound on the sum of `tgt_mask` on one device may be relied on, other than what follows from the above.
Results may differ from the reference program's by a relative error of at most 0.02.
Values may be sent and summed in bfloat16 or wider, within the bound.
No kernel may reach another device: no remote copies, remote signals or barrier semaphores. Data moves between devices by JAX's collectives and lax.ppermute only.
A program may use at most 192 MiB of HBM per device.

```python
import math
import jax
import jax.numpy as jnp
from jax import lax

D = 768
HEAD = 64
FF = 3072
TDIM = 128
THID = 512
TSTEPS = 2000
SEQLEN = 1024
SEQS = 16
HALF = 512


def drawn_law(key, shape, scale):
    return jax.random.truncated_normal(key, -4.0, 4.0, shape, jnp.float32) * scale


def draw_inputs(key, part):
    key = jax.random.fold_in(key, 11)
    shape = (SEQS, SEQLEN, D)
    values = drawn_law(key, shape, 1.0)
    return values.astype(jnp.bfloat16)


def draw_w_qkv(key, part):
    key = jax.random.fold_in(key, 12)
    shape = (3, D, D)
    scale = D ** (-0.5)
    values = drawn_law(key, shape, scale)
    return values.astype(jnp.bfloat16)


def draw_w_out(key, part):
    key = jax.random.fold_in(key, 13)
    shape = (D, D)
    scale = max(D // 128, 1) ** (-0.5)
    values = drawn_law(key, shape, scale)
    return values.astype(jnp.bfloat16)


def draw_w_up(key, part):
    key = jax.random.fold_in(key, 14)
    shape = (D, FF)
    scale = D ** (-0.5)
    values = drawn_law(key, shape, scale)
    return values.astype(jnp.bfloat16)


def draw_w_down(key, part):
    key = jax.random.fold_in(key, 15)
    shape = (FF, D)
    scale = (FF // 2) ** (-0.5)
    values = drawn_law(key, shape, scale)
    return values.astype(jnp.bfloat16)


def place_ends(values, rng, low, top_value):
    longest = values.shape.index(max(values.shape))
    spots = []
    for shift in (0, 1):
        where = [jax.random.randint(jax.random.fold_in(rng, axis), (), 0, length) for axis, length in enumerate(values.shape)]
        where[longest] = (where[longest] + shift) % values.shape[longest]
        spots.append(tuple(where))
    return values.at[spots[0]].set(low).at[spots[1]].set(top_value)


def levels(stream_key, extent, split, smallest, largest):
    def one(position, shards_of):
        heights = jax.random.uniform(jax.random.fold_in(jax.random.fold_in(stream_key, 6), position), (shards_of,), jnp.float32, smallest / len(split), largest / len(split))
        return jnp.repeat(jnp.exp(heights), extent[position] // shards_of).reshape((-1,) + (1,) * (len(extent) - position - 1))

    factor_of = one(*split[0])
    for cut in split[1:]:
        factor_of = factor_of * one(*cut)
    return factor_of


def normal_values(stream_key, dims, scale, most, shards=(), kind=jnp.bfloat16):
    values = scale * jax.random.normal(stream_key, dims, jnp.float32)
    if shards:
        values = values * levels(stream_key, dims, shards, -0.22, 0.18)
    return jnp.clip(values, -most, most).astype(kind)


def setup_inputs(seed: int = 0) -> dict:
    arg_keys = jax.random.split(jax.random.key(seed), 23)
    return {
        "inputs": draw_inputs(jax.random.fold_in(arg_keys[22], 71), 0),
        "cotangent": normal_values(arg_keys[1], (SEQS, SEQLEN, D), 1.0, 6.0, ((0, 8), (1, 4))),
        "src_lengths": place_ends(jax.random.randint(arg_keys[2], (SEQS,), HALF * 19 // 32, HALF + 1), jax.random.fold_in(arg_keys[2], 1), HALF * 19 // 32, HALF).astype(jnp.int32),
        "tgt_mask": place_ends((jax.random.randint(arg_keys[3], (SEQS, HALF), 0, 8) < 7).astype(jnp.int32), jax.random.fold_in(arg_keys[3], 1), 0, 1),
        "timesteps": place_ends(jax.random.randint(arg_keys[4], (SEQS,), 0, TSTEPS), jax.random.fold_in(arg_keys[4], 1), 0, TSTEPS - 1).astype(jnp.int32),
        "importance": jnp.clip(jnp.exp(jax.random.uniform(arg_keys[5], (TSTEPS,), jnp.float32, math.log(0.25), math.log(4.0))), 0.25, 4.0),
        "w_qkv": draw_w_qkv(jax.random.fold_in(arg_keys[22], 71), 0),
        "b_qv": normal_values(arg_keys[7], (2, D), 0.5, 3.0, ((1, 4),), jnp.float32),
        "w_out": draw_w_out(jax.random.fold_in(arg_keys[22], 71), 0),
        "b_out": normal_values(arg_keys[9], (D,), 0.5, 3.0, (), jnp.float32),
        "gain_one": jnp.clip(1.0 + 0.1 * jax.random.normal(arg_keys[10], (D,), jnp.float32), 0.5, 1.5),
        "shift_one": normal_values(arg_keys[11], (D,), 0.3, 2.0, (), jnp.float32),
        "w_up": draw_w_up(jax.random.fold_in(arg_keys[22], 71), 0),
        "b_up": normal_values(arg_keys[13], (FF,), 0.5, 3.0, ((0, 4),), jnp.float32),
        "w_down": draw_w_down(jax.random.fold_in(arg_keys[22], 71), 0),
        "b_down": normal_values(arg_keys[15], (D,), 0.5, 3.0, (), jnp.float32),
        "gain_two": jnp.clip(1.0 + 0.1 * jax.random.normal(arg_keys[16], (D,), jnp.float32), 0.5, 1.5),
        "shift_two": normal_values(arg_keys[17], (D,), 0.3, 2.0, (), jnp.float32),
        "w_time1": normal_values(arg_keys[18], (TDIM, THID), (TDIM // 2) ** -0.5, 0.75, (), jnp.float32),
        "time_bias1": normal_values(arg_keys[19], (THID,), 0.5, 3.0, (), jnp.float32),
        "w_time2": normal_values(arg_keys[20], (THID, D), THID ** -0.5, 0.25, (), jnp.float32),
        "time_bias2": normal_values(arg_keys[21], (D,), 0.5, 3.0, (), jnp.float32),
    }


@jax.custom_vjp
def low(v):
    return lax.optimization_barrier(v.astype(jnp.bfloat16)).astype(jnp.float32)

@jax.custom_vjp
def low_back(v):
    return v

def low_keep(v):
    return (low(v), None)

def low_pass(kept, grad):
    return (grad,)

def back_keep(v):
    return (v, None)

def back_low(kept, grad):
    return (low(grad),)
low.defvjp(low_keep, low_pass)
low_back.defvjp(back_keep, back_low)

def matmul(left, right):
    return jnp.matmul(left, right, precision=lax.Precision.HIGHEST)

def sinusoid(step_ids, feature_count):
    halfway = feature_count // 2
    frequency = jnp.exp(-math.log(10000.0) * jnp.arange(halfway, dtype=jnp.float32) / halfway)
    angles = step_ids.astype(jnp.float32)[:, None] * frequency[None, :]
    return jnp.concatenate([jnp.cos(angles), jnp.sin(angles)], axis=1)

def layer_norm(values, norm_gain, norm_shift):
    centre = values - lax.optimization_barrier(jnp.mean(values, axis=-1, keepdims=True))
    spread = lax.optimization_barrier(jnp.mean(centre * centre, axis=-1, keepdims=True))
    return centre * lax.rsqrt(spread + 1e-05) * norm_gain + norm_shift

def forward(tokens, features, allowed, w_qkv, b_qv, w_out, b_out, gain_one, shift_one, w_up, b_up, w_down, b_down, gain_two, shift_two, w_time1, time_bias1, w_time2, time_bias2):
    hidden_time = jax.nn.silu(matmul(features, w_time1) + time_bias1)
    time_vec = matmul(hidden_time, w_time2) + time_bias2
    start = tokens + time_vec[:, None, :]
    lower_rows_start = low(start)
    queries = low(low_back(matmul(lower_rows_start, w_qkv[0]) + b_qv[0]))
    key_rows = low(low_back(matmul(lower_rows_start, w_qkv[1])))
    value_rows = low(low_back(matmul(lower_rows_start, w_qkv[2]) + b_qv[1]))
    batch_count, row_count, feature_count = tokens.shape
    head_count = feature_count // HEAD
    shaped = (batch_count, row_count, head_count, HEAD)
    scores = jnp.einsum('gqhe,gkhe->ghqk', queries.reshape(shaped), key_rows.reshape(shaped), precision=lax.Precision.HIGHEST) * HEAD ** (-0.5)
    scores = low_back(jnp.where(allowed[:, None, None, :], scores, -1000000000.0))
    chances = low(jax.nn.softmax(scores, axis=-1))
    attended = jnp.einsum('ghqk,gkhe->gqhe', chances, value_rows.reshape(shaped), precision=lax.Precision.HIGHEST)
    attended = low(low_back(attended.reshape(batch_count, row_count, feature_count)))
    branch = low_back(matmul(attended, w_out) + b_out)
    normed = layer_norm(start + branch, gain_one, shift_one)
    upward = low_back(matmul(low(normed), w_up) + b_up)
    activated = low(jax.nn.gelu(upward, approximate=False))
    mixed = low_back(matmul(activated, w_down) + b_down)
    return layer_norm(normed + mixed, gain_two, shift_two)

def reference(inputs, cotangent, src_lengths, tgt_mask, timesteps, importance, w_qkv, b_qv, w_out, b_out, gain_one, shift_one, w_up, b_up, w_down, b_down, gain_two, shift_two, w_time1, time_bias1, w_time2, time_bias2):
    floats = (w_qkv.astype(jnp.float32), b_qv, w_out.astype(jnp.float32), b_out, gain_one, shift_one, w_up.astype(jnp.float32), b_up, w_down.astype(jnp.float32), b_down, gain_two, shift_two, w_time1, time_bias1, w_time2, time_bias2)
    total_seqs, row_count, feature_count = inputs.shape
    group_size = math.gcd(total_seqs, 4)
    group_count = total_seqs // group_size
    positions = jnp.arange(row_count // 2, dtype=jnp.int32)
    source_live = positions[None, :] < src_lengths[:, None]
    allowed = jnp.concatenate([source_live, tgt_mask == 1], axis=1)
    features = sinusoid(timesteps, w_time1.shape[0])
    row_weight = importance[timesteps]

    def regroup(array):
        return array.reshape((group_count, group_size) + array.shape[1:])

    def one_group(carry, pieces):
        tokens, cotan, feats, live, weights = pieces

        def local_forward(tokens_float, *params):
            return forward(tokens_float, feats, live, *params)
        result, pullback = jax.vjp(local_forward, tokens.astype(jnp.float32), *floats)
        grads = pullback(cotan.astype(jnp.float32) * weights[:, None, None])
        new_carry = tuple((total + piece for total, piece in zip(carry, grads[1:])))
        return (new_carry, (result.astype(jnp.bfloat16), grads[0]))
    initial = tuple((jnp.zeros(param.shape, jnp.float32) for param in floats))
    sums, (results, input_grads) = lax.scan(one_group, initial, (regroup(inputs), regroup(cotangent), regroup(features), regroup(allowed), regroup(row_weight)))
    return (results.reshape(inputs.shape), input_grads.reshape(inputs.shape), sums[0], sums[1], sums[2], sums[3], sums[4], sums[5], sums[6], sums[7], sums[8], sums[9], sums[10], sums[11], sums[12], sums[13], sums[14], sums[15])
```

```python
import math

import jax
import jax.numpy as jnp
from jax import lax
from jax.experimental import pallas as pl
from jax.experimental.pallas import tpu as pltpu
from jax.sharding import PartitionSpec as P

HEAD = 64
F32 = jnp.float32
BF16 = jnp.bfloat16
HIGHEST = lax.Precision.HIGHEST
LOG2E = math.log2(math.e)
MASKED = -1e9
MIB = 1024 * 1024

NT = (((1,), (1,)), ((), ()))
NN = (((1,), (0,)), ((), ()))
TN = (((0,), (0,)), ((), ()))


def mm(left, right, dims=NN):
    return lax.dot_general(left, right, dims, preferred_element_type=F32)


def flip(value, axis, bit=0):
    return lax.ppermute(value, axis, [(i, i ^ (1 << bit)) for i in range(lax.axis_size(axis))])


def across(value):
    return lax.ppermute(value, ("half", "tensor"), [(i, 3 - i) for i in range(4)])


def params(limit, *semantics):
    return pltpu.CompilerParams(vmem_limit_bytes=limit * MIB, dimension_semantics=semantics)


def project_kernel(x_ref, tv_ref, w_ref, bq_ref, bv_ref, q_ref, k_ref, v_ref, low_ref):
    low = (x_ref[0].astype(F32) + tv_ref[0]).astype(BF16)
    low_ref[0] = low
    q_ref[0] = ((mm(low, w_ref[0]) + bq_ref[...]) * (LOG2E / math.sqrt(HEAD))).astype(BF16)
    k_ref[0] = mm(low, w_ref[1]).astype(BF16)
    v_ref[0] = (mm(low, w_ref[2]) + bv_ref[...]).astype(BF16)


def project(rows, time_vec, weights, bias_q, bias_v):
    seqs, count, width = rows.shape
    head_width = weights.shape[2]
    block = pl.BlockSpec((1, count, width), lambda s: (s, 0, 0))
    narrow = pl.BlockSpec((1, count, head_width), lambda s: (s, 0, 0))
    bias = pl.BlockSpec((1, head_width), lambda s: (0, 0))
    return pl.pallas_call(
        project_kernel,
        grid=(seqs,),
        in_specs=[
            block,
            pl.BlockSpec((1, 1, width), lambda s: (s, 0, 0)),
            pl.BlockSpec(weights.shape, lambda s: (0, 0, 0)),
            bias,
            bias,
        ],
        out_specs=[narrow, narrow, narrow, block],
        out_shape=[jax.ShapeDtypeStruct((seqs, count, head_width), BF16)] * 3
        + [jax.ShapeDtypeStruct(rows.shape, BF16)],
        compiler_params=params(40, "arbitrary"),
        name="project",
    )(rows, time_vec[:, None, :], weights, bias_q[None], bias_v[None])


def attend_kernel(heads, qn_ref, qf_ref, kn_ref, kf_ref, vn_ref, vf_ref, mask_ref, on_ref, of_ref, sum_ref, exp_ref):
    rows = qn_ref.shape[1]
    ones = jnp.ones((rows, HEAD), BF16)
    keys_all = jnp.concatenate([kn_ref[0], kf_ref[0]], axis=0)
    values_all = jnp.concatenate([vn_ref[0], vf_ref[0]], axis=0)
    many = jnp.ones((keys_all.shape[0], HEAD), BF16)
    for block, (q_ref, o_ref) in enumerate(((qn_ref, on_ref), (qf_ref, of_ref))):
        outs = []
        for head in range(heads):
            lanes = slice(head * HEAD, (head + 1) * HEAD)
            query = jnp.concatenate([q_ref[0, :, lanes], ones], axis=1)
            keys = jnp.concatenate([keys_all[:, lanes], mask_ref[0]], axis=1)
            scores = mm(query, keys, NT)
            power = jnp.exp2(scores - jnp.max(scores, axis=1, keepdims=True)).astype(BF16)
            exp_ref[0, block, head] = power
            values = jnp.concatenate([values_all[:, lanes], many], axis=1)
            total = mm(power, values)
            sum_ref[0, block, head] = total
            outs.append(total[:, :HEAD] / total[:, HEAD:])
        o_ref[0] = jnp.concatenate(outs, axis=1).astype(BF16)


def attend(part, queries, keys, values, mask):
    seqs, half_rows, head_width = queries[0].shape
    rows = half_rows // 2
    heads = head_width // HEAD
    q_spec = pl.BlockSpec((1, rows, head_width), lambda s: (s, part, 0))
    k_spec = pl.BlockSpec((1, half_rows, head_width), lambda s: (s, 0, 0))
    o_spec = pl.BlockSpec((1, rows, head_width), lambda s: (s, 0, 0))
    return pl.pallas_call(
        lambda *refs: attend_kernel(heads, *refs),
        grid=(seqs,),
        in_specs=[q_spec, q_spec, k_spec, k_spec, k_spec, k_spec, pl.BlockSpec((1, 2 * half_rows, HEAD), lambda s: (s, 0, 0))],
        out_specs=[
            o_spec,
            o_spec,
            pl.BlockSpec((1, 2, heads, rows, 2 * HEAD), lambda s: (s, 0, 0, 0, 0)),
            pl.BlockSpec((1, 2, heads, rows, 2 * half_rows), lambda s: (s, 0, 0, 0, 0)),
        ],
        out_shape=[
            jax.ShapeDtypeStruct((seqs, rows, head_width), BF16),
            jax.ShapeDtypeStruct((seqs, rows, head_width), BF16),
            jax.ShapeDtypeStruct((seqs, 2, heads, rows, 2 * HEAD), F32),
            jax.ShapeDtypeStruct((seqs, 2, heads, rows, 2 * half_rows), BF16),
        ],
        compiler_params=params(48, "arbitrary"),
        name="attend",
    )(*queries, *queries[:0], *keys, *values, mask)


def attend_back_kernel(heads, first, *refs):
    if first:
        gn_ref, gf_ref, sum_ref, exp_ref, qn_ref, qf_ref, kn_ref, kf_ref, vn_ref, vf_ref, dqn_ref, dqf_ref, dk_ref, dv_ref = refs
    else:
        gn_ref, gf_ref, sum_ref, exp_ref, qn_ref, qf_ref, kn_ref, kf_ref, vn_ref, vf_ref, k0_ref, v0_ref, dqn_ref, dqf_ref, dk_ref, dv_ref = refs
    keys_all = jnp.concatenate([kn_ref[0], kf_ref[0]], axis=0)
    values_all = jnp.concatenate([vn_ref[0], vf_ref[0]], axis=0)
    grad_q = [[], []]
    for head in range(heads):
        lanes = slice(head * HEAD, (head + 1) * HEAD)
        keys, values = keys_all[:, lanes], values_all[:, lanes]
        grad_k = grad_v = None
        for block, (q_ref, g_ref) in enumerate(((qn_ref, gn_ref), (qf_ref, gf_ref))):
            totals = sum_ref[0, block, head]
            inverse = 1.0 / totals[:, HEAD:]
            grad = (g_ref[0, :, lanes].astype(F32) * inverse).astype(BF16)
            inner = jnp.sum(grad.astype(F32) * (totals[:, :HEAD] * inverse), axis=1, keepdims=True)
            power = exp_ref[0, block, head]
            grad_power = mm(grad, values, NT)
            grad_scores = power * (grad_power - inner).astype(BF16)
            grad_q[block].append(mm(grad_scores, keys) * (1.0 / math.sqrt(HEAD)))
            part_k = mm(q_ref[0, :, lanes], grad_scores, TN)
            part_v = mm(grad, power, TN)
            grad_k = part_k if grad_k is None else grad_k + part_k
            grad_v = part_v if grad_v is None else grad_v + part_v
        grad_k = grad_k * (1.0 / LOG2E)
        if not first:
            grad_k = grad_k + k0_ref[0, lanes]
            grad_v = grad_v + v0_ref[0, lanes]
        dk_ref[0, lanes] = grad_k.astype(dk_ref.dtype)
        dv_ref[0, lanes] = grad_v.astype(dv_ref.dtype)
    dqn_ref[0] = jnp.concatenate(grad_q[0], axis=1).astype(BF16)
    dqf_ref[0] = jnp.concatenate(grad_q[1], axis=1).astype(BF16)


def attend_back(part, grads, sums, powers, queries, keys, values, before=()):
    seqs, half_rows, head_width = queries[0].shape
    rows = half_rows // 2
    heads = head_width // HEAD
    first = not before
    q_spec = pl.BlockSpec((1, rows, head_width), lambda s: (s, part, 0))
    k_spec = pl.BlockSpec((1, half_rows, head_width), lambda s: (s, 0, 0))
    o_spec = pl.BlockSpec((1, rows, head_width), lambda s: (s, 0, 0))
    t_spec = pl.BlockSpec((1, head_width, 2 * half_rows), lambda s: (s, 0, 0))
    out_type = F32 if first else BF16
    return pl.pallas_call(
        lambda *refs: attend_back_kernel(heads, first, *refs),
        grid=(seqs,),
        in_specs=[
            o_spec,
            o_spec,
            pl.BlockSpec((1, 2, heads, rows, 2 * HEAD), lambda s: (s, 0, 0, 0, 0)),
            pl.BlockSpec((1, 2, heads, rows, 2 * half_rows), lambda s: (s, 0, 0, 0, 0)),
            q_spec,
            q_spec,
            k_spec,
            k_spec,
            k_spec,
            k_spec,
        ]
        + [t_spec] * len(before),
        out_specs=[o_spec, o_spec, t_spec, t_spec],
        out_shape=[jax.ShapeDtypeStruct((seqs, rows, head_width), BF16)] * 2
        + [jax.ShapeDtypeStruct((seqs, head_width, 2 * half_rows), out_type)] * 2,
        compiler_params=params(48, "arbitrary"),
        name="attend_back",
    )(*grads, sums, powers, *queries, *keys, *values, *before)


def normalize(values):
    centre = values - jnp.mean(values, axis=-1, keepdims=True)
    scale = lax.rsqrt(jnp.mean(centre * centre, axis=-1, keepdims=True) + 1e-05)
    return centre * scale, scale


def normalize_back(grad, unit, scale):
    return scale * (
        grad
        - jnp.mean(grad, axis=-1, keepdims=True)
        - unit * jnp.mean(grad * unit, axis=-1, keepdims=True)
    )


def sinusoid(step_ids, feature_count):
    halfway = feature_count // 2
    frequency = jnp.exp(-math.log(10000.0) * jnp.arange(halfway, dtype=F32) / halfway)
    angles = step_ids.astype(F32)[:, None] * frequency[None, :]
    return jnp.concatenate([jnp.cos(angles), jnp.sin(angles)], axis=1)


def dp_bits():
    return list(range(lax.axis_size("dp").bit_length() - 1))


def bit_of(bit):
    return (lax.axis_index("dp") >> bit) & 1


def scatter_step(value, axis, bit, mine):
    rows = value.shape[0] // 2
    sent = lax.dynamic_slice_in_dim(value, (1 - mine) * rows, rows, 0)
    kept = lax.dynamic_slice_in_dim(value, mine * rows, rows, 0)
    return (kept.astype(F32) + flip(sent, axis, bit).astype(F32)).astype(BF16)


def gather_step(value, axis, bit, mine):
    other = flip(value, axis, bit)
    return jnp.where(mine == 0, jnp.concatenate([value, other]), jnp.concatenate([other, value]))


def dp_sum(value, order):
    for bit in order:
        value = scatter_step(value, "dp", bit, bit_of(bit))
    for bit in reversed(order):
        value = gather_step(value, "dp", bit, bit_of(bit))
    return value


def per_device(
    inputs,
    cotangent,
    src_lengths,
    tgt_mask,
    timesteps,
    importance,
    w_qkv,
    b_qv,
    w_out,
    b_out,
    gain_one,
    shift_one,
    w_up,
    b_up,
    w_down,
    b_down,
    gain_two,
    shift_two,
    w_time1,
    time_bias1,
    w_time2,
    time_bias2,
):
    half = lax.axis_index("half")
    tensor = lax.axis_index("tensor")
    seqs, half_rows, width = inputs.shape
    rows = half_rows // lax.axis_size("tensor")
    hidden = w_up.shape[1]
    bits = dp_bits()

    def own_first(array):
        return jnp.concatenate(
            [
                lax.dynamic_slice_in_dim(array, tensor * rows, rows, 1),
                lax.dynamic_slice_in_dim(array, (1 - tensor) * rows, rows, 1),
            ],
            axis=1,
        )

    near = own_first(inputs)
    far = flip(near, "half")

    def whole(shard):
        one = flip(shard, "tensor")
        return [shard, one, flip(shard, "half"), flip(one, "half")]

    def whole_in_parts(shard):
        rows_of = shard.shape[0] // 2
        mine = bit_of(0)
        part = flip(lax.dynamic_slice_in_dim(shard, mine * rows_of, rows_of, 0), "tensor")
        one = gather_step(part, "dp", 0, mine)
        return [shard, one, flip(shard, "half"), flip(one, "half")]

    outs_w = whole(w_out)
    ups_b = whole(b_up)
    ups_w = whole_in_parts(w_up)
    downs_w = whole_in_parts(w_down)

    features = sinusoid(timesteps, w_time1.shape[0])
    time_sum = jnp.dot(features, w_time1, precision=HIGHEST) + time_bias1
    time_vec = jnp.dot(jax.nn.silu(time_sum), w_time2, precision=HIGHEST) + time_bias2

    positions = jnp.arange(half_rows, dtype=jnp.int32)
    source_live = positions[None, :] < src_lengths[:, None]
    target_live = tgt_mask == 1
    near_live = own_first(jnp.where(half == 0, source_live, target_live))
    far_live = own_first(jnp.where(half == 0, target_live, source_live))
    allowed = jnp.concatenate([near_live, far_live], axis=1)
    mask = jnp.where(
        (jnp.arange(HEAD) == 0)[None, None, :] & ~allowed[:, :, None], MASKED, 0.0
    ).astype(BF16)

    q_near, k_near, v_near, low_near = project(near, time_vec, w_qkv, b_qv[0], b_qv[1])
    q_far, k_far, v_far, low_far = project(far, time_vec, w_qkv, b_qv[0], b_qv[1])
    queries, keys, values = (q_near, q_far), (k_near, k_far), (v_near, v_far)

    att_y, att_d, sums_a, powers_a = attend(1, queries, keys, values, mask)
    got_y, got_d = flip(att_y, "tensor"), across(att_d)
    att_own, att_h, sums_b, powers_b = attend(0, queries, keys, values, mask)
    got_h = flip(att_h, "half")
    flat = seqs * rows
    atts = [a.reshape(flat, -1) for a in (att_own, got_y, got_h, got_d)]

    start = (near[:, :rows].astype(F32) + time_vec[:, None, :]).reshape(flat, width)
    branch = sum(mm(a, w) for a, w in zip(atts, outs_w))
    unit_one, scale_one = normalize(start + (branch + b_out))
    normed = unit_one * gain_one + shift_one
    normed_low = normed.astype(BF16)
    acts, slopes = [], []
    mixed = b_down
    for up, bias, down in zip(ups_w, ups_b, downs_w):
        upward = mm(normed_low, up) + bias
        below = 0.5 * (1.0 + lax.erf(upward * math.sqrt(0.5)))
        density = jnp.exp(-0.5 * upward * upward) * (1.0 / math.sqrt(2.0 * math.pi))
        acts.append((upward * below).astype(BF16))
        slopes.append((below + upward * density).astype(BF16))
        mixed = mixed + mm(acts[-1], down)
    unit_two, scale_two = normalize(normed + mixed)
    outputs = (unit_two * gain_two + shift_two).astype(BF16).reshape(seqs, rows, width)
    table_index = jnp.arange(importance.shape[0], dtype=jnp.int32)
    row_weight = jnp.sum(
        jnp.where(table_index[None, :] == timesteps[:, None], importance[None, :], 0.0), axis=1
    )
    grad_result = (cotangent.astype(F32) * row_weight[:, None, None]).reshape(flat, width)
    grad_gain_two = jnp.sum(grad_result * unit_two, axis=0)
    grad_shift_two = jnp.sum(grad_result, axis=0)
    grad_sum = normalize_back(grad_result * gain_two, unit_two, scale_two)
    grad_mixed = grad_sum.astype(BF16)
    grad_b_down = jnp.sum(grad_mixed.astype(F32), axis=0)
    grad_ups = [
        (mm(grad_mixed, down, NT) * slope.astype(F32)).astype(BF16)
        for down, slope in zip(downs_w, slopes)
    ]
    grad_b_ups = [jnp.sum(g.astype(F32), axis=0) for g in grad_ups]
    grad_normed = grad_sum + sum(mm(g, up, NT) for g, up in zip(grad_ups, ups_w))
    grad_gain_one = jnp.sum(grad_normed * unit_one, axis=0)
    grad_shift_one = jnp.sum(grad_normed, axis=0)
    grad_pre = normalize_back(grad_normed * gain_one, unit_one, scale_one)
    grad_branch = grad_pre.astype(BF16)
    grad_b_out = jnp.sum(grad_branch.astype(F32), axis=0)
    grad_atts = [
        mm(grad_branch, w, NT).astype(BF16).reshape(seqs, rows, -1) for w in outs_w
    ]

    def pair_sum(lefts, right_own, right_far, order, transposed):
        got = [flip(v, "half") for v in lefts[2:]]
        pieces = []
        for own, other in zip(lefts[:2], got):
            left = jnp.concatenate([own, other])
            right = jnp.concatenate([right_own, right_far])
            pieces.append((mm(right, left, TN) if transposed else mm(left, right, TN)).astype(BF16))
        total = (pieces[0].astype(F32) + flip(pieces[1], "tensor").astype(F32)).astype(BF16)
        return dp_sum(total, order).astype(F32)

    order = bits
    grad_w_down = pair_sum(acts, grad_mixed, flip(grad_mixed, "half"), order, False)
    grad_w_up = pair_sum(grad_ups, normed_low, flip(normed_low, "half"), order, True)
    grad_w_out = pair_sum(atts, grad_branch, flip(grad_branch, "half"), order, False)

    back_y, back_h, back_d = flip(grad_atts[1], "tensor"), flip(grad_atts[2], "half"), across(grad_atts[3])
    dq_own, dq_h, dk, dv = attend_back(
        0, (grad_atts[0], back_h), sums_b, powers_b, queries, keys, values
    )
    dq_y, dq_d, dk, dv = attend_back(
        1, (back_y, back_d), sums_a, powers_a, queries, keys, values, (dk, dv)
    )
    dq = jnp.concatenate([dq_own, dq_y, dq_h, dq_d], axis=1)
    low = jnp.concatenate([low_near, low_far], axis=1)
    gradient = jnp.concatenate([jnp.swapaxes(dq, 1, 2), dk, dv], axis=1)
    grad_w_qkv = jnp.einsum("scr,srd->cd", gradient, low, preferred_element_type=F32).astype(BF16)
    grad_w_qkv = dp_sum(grad_w_qkv, order).astype(F32)
    head_width = w_qkv.shape[2]
    grad_w_qkv = jnp.swapaxes(grad_w_qkv.reshape(3, head_width, width), 1, 2)

    w_cat = jnp.swapaxes(w_qkv, 1, 2).reshape(3 * head_width, width)
    part = jnp.einsum("scr,cd->srd", gradient, w_cat, preferred_element_type=F32).astype(BF16)
    over_half = part[:, :half_rows].astype(F32) + flip(part[:, half_rows:], "half").astype(F32)
    over_tensor = over_half[:, :rows] + flip(over_half[:, rows:].astype(BF16), "tensor").astype(F32)
    grad_pre = grad_pre.reshape(seqs, rows, width)
    grad_inputs = grad_pre + over_tensor

    column_sums = jnp.sum(gradient.astype(F32), axis=2)
    grad_time = jnp.sum(grad_pre, axis=1) + jnp.dot(column_sums, w_cat.astype(F32), precision=HIGHEST)
    shared = jnp.stack(
        [grad_b_out, grad_gain_one, grad_shift_one, grad_b_down, grad_gain_two, grad_shift_two]
    )
    shared = jnp.concatenate([shared, grad_time])
    up_two = jnp.stack(grad_b_ups[:2]).reshape(2, -1)
    up_far = jnp.stack(grad_b_ups[2:]).reshape(2, -1)
    got = flip(jnp.concatenate([shared, up_far.reshape(-1, width)]), "half")
    shared = shared + got[: shared.shape[0]]
    up_two = up_two + got[shared.shape[0] :].reshape(2, -1)
    got = flip(jnp.concatenate([shared, up_two[1].reshape(-1, width)]), "tensor")
    shared = shared + got[: shared.shape[0]]
    up_own = up_two[0] + got[shared.shape[0] :].reshape(-1)
    bias_sums = jnp.sum(column_sums, axis=0).reshape(3, head_width)
    grad_b_qv = jnp.stack([bias_sums[0], bias_sums[2]])
    reduced = jnp.concatenate([shared[:6].reshape(-1), up_own, grad_b_qv.reshape(-1)])
    reduced = reduced.reshape(-1, HEAD * 2)
    times = jnp.concatenate([shared[6:], time_sum, features], axis=1).reshape(seqs, 1, -1)
    times = times.reshape(-1, HEAD * 2)
    count = reduced.shape[0]
    for bit in bits:
        got = flip(jnp.concatenate([reduced, times]), "dp", bit)
        reduced = reduced + got[:count]
        times = jnp.concatenate([times, got[count:]])
    reduced = reduced.reshape(-1)
    times = times.reshape(-1, shared.shape[1] + time_sum.shape[1] + features.shape[1])
    all_grad, all_sum, all_features = jnp.split(times, [width, width + time_sum.shape[1]], axis=1)
    gate = jax.nn.sigmoid(all_sum)
    all_hidden = all_sum * gate
    grad_w_time2 = lax.dot_general(all_hidden, all_grad, TN, precision=HIGHEST)
    grad_hidden = lax.dot_general(all_grad, w_time2, NT, precision=HIGHEST)
    grad_hidden = grad_hidden * (gate * (1.0 + all_sum * (1.0 - gate)))
    grad_w_time1 = lax.dot_general(all_features, grad_hidden, TN, precision=HIGHEST)
    vectors = reduced[: 6 * width].reshape(6, width)
    grad_b_up = reduced[6 * width : 6 * width + hidden]
    grad_b_qv = reduced[6 * width + hidden :].reshape(2, head_width)
    return (
        outputs,
        grad_inputs,
        grad_w_qkv,
        grad_b_qv,
        grad_w_out,
        vectors[0],
        vectors[1],
        vectors[2],
        grad_w_up,
        grad_b_up,
        grad_w_down,
        vectors[3],
        vectors[4],
        vectors[5],
        grad_w_time1,
        jnp.sum(grad_hidden, axis=0),
        grad_w_time2,
        jnp.sum(all_grad, axis=0),
    )


def solution(mesh):
    in_specs = (
        P("dp", "half", None),
        P("dp", ("half", "tensor"), None),
        P("dp"),
        P("dp", None),
        P("dp"),
        P(),
        P(None, None, ("tensor", "half")),
        P(None, ("tensor", "half")),
        P(("tensor", "half"), None),
        P(),
        P(),
        P(),
        P(None, ("tensor", "half")),
        P(("tensor", "half")),
        P(("tensor", "half"), None),
        P(),
        P(),
        P(),
        P(),
        P(),
        P(),
        P(),
    )
    out_specs = (
        P("dp", ("half", "tensor"), None),
        P("dp", ("half", "tensor"), None),
        P(None, None, ("tensor", "half")),
        P(None, ("tensor", "half")),
        P(("tensor", "half"), None),
        P(),
        P(),
        P(),
        P(None, ("tensor", "half")),
        P(("tensor", "half")),
        P(("tensor", "half"), None),
        P(),
        P(),
        P(),
        P(),
        P(),
        P(),
        P(),
    )
    return jax.shard_map(
        per_device, mesh=mesh, in_specs=in_specs, out_specs=out_specs, check_vma=False
    )
```

```python
import math

import jax
import jax.numpy as jnp
from jax import lax
from jax.experimental import pallas as pl
from jax.experimental.pallas import tpu as pltpu
from jax.sharding import PartitionSpec as P

HEAD = 64
F32 = jnp.float32
BF16 = jnp.bfloat16
HIGHEST = lax.Precision.HIGHEST
LOG2E = math.log2(math.e)
MASKED = -1e9
MIB = 1024 * 1024
GRANTS = {"rows_part": 38, "attend": 24, "attend_back": 24, "qkv_grad": 14, "weight_grad": 14}
ANY = pl.BlockSpec(memory_space=pl.ANY)
HBM = pl.BlockSpec(memory_space=pltpu.HBM)

NT = (((1,), (1,)), ((), ()))
NN = (((1,), (0,)), ((), ()))
TN = (((0,), (0,)), ((), ()))


def mm(left, right, dims=NN):
    return lax.dot_general(left, right, dims, preferred_element_type=F32)


def bit_of(dim):
    if dim == "y":
        return lax.axis_index("tensor")
    if dim == "core":
        return lax.axis_index("half")
    return (lax.axis_index("dp") >> dim) & 1


def swap(value, *dims):
    axes = ("dp", "half", "tensor")
    sizes = [lax.axis_size(a) for a in axes]
    pairs = []
    for d in range(sizes[0]):
        for h in range(2):
            for t in range(2):
                dim = dims[h % len(dims)]
                if dim == "y":
                    to = (d, h, 1 - t)
                elif dim == "core":
                    to = (d, 1 - h, t)
                else:
                    to = (d ^ (1 << dim), h, t)
                pairs.append(((d * 2 + h) * 2 + t, (to[0] * 2 + to[1]) * 2 + to[2]))
    return lax.ppermute(value, axes, pairs)


def place(*dims):
    if len(dims) == 1:
        return bit_of(dims[0])
    return jnp.where(lax.axis_index("half") == 0, bit_of(dims[0]), bit_of(dims[1]))


class Order:
    token = None


def call(kernel, name, in_specs, args, out_specs, out_shape, grid=(), scalars=None, scratch_shapes=(), aliases=None, after=(), pins=()):
    tokens = (() if Order.token is None else (Order.token,)) + tuple(after)
    first = len(in_specs) + (scalars is not None)

    def body(*refs):
        kernel(*refs[:first], *refs[first + len(tokens) :])

    in_specs = list(in_specs) + [ANY] * len(tokens)
    args = [pltpu.with_memory_space_constraint(a, pltpu.HBM) if i in pins else a for i, a in enumerate(args)]
    if scalars is None:
        rest = dict(grid=grid, in_specs=in_specs, out_specs=out_specs, scratch_shapes=scratch_shapes)
    else:
        rest = dict(
            grid_spec=pltpu.PrefetchScalarGridSpec(
                num_scalar_prefetch=1,
                grid=grid,
                in_specs=in_specs,
                out_specs=out_specs,
                scratch_shapes=scratch_shapes,
            )
        )
        args = (jnp.stack(scalars).astype(jnp.int32), *args)
    out = pl.pallas_call(
        body,
        out_shape=out_shape,
        compiler_params=pltpu.CompilerParams(vmem_limit_bytes=GRANTS.get(name, 12) * MIB),
        cost_estimate=cost(name),
        input_output_aliases=aliases or {},
        name=name,
        **rest,
    )(*args, *tokens)
    Order.token = out[0] if isinstance(out, (list, tuple)) else out
    return out


def hold(*values):
    return call(
        lambda *refs: None,
        "hold",
        [ANY] * len(values),
        values,
        [ANY] * len(values),
        [like(v.shape, v.dtype) for v in values],
        aliases={i: i for i in range(len(values))},
    )


def like(shape, dtype):
    return jax.ShapeDtypeStruct(shape, dtype)


TIMES = {"project": 2.5, "attend": 6, "rows_part": 24, "attend_back": 9, "weight_grad": 6, "out_grad": 2.4, "qkv_grad": 5.5, "input_grad": 2.7, "hold": 0}


def cost(name):
    return pl.CostEstimate(flops=int(TIMES.get(name, 1) * 1.15e9), bytes_accessed=1024, transcendentals=0)


VMEM = pl.BlockSpec(memory_space=pltpu.VMEM)
SMEM = pl.BlockSpec(memory_space=pltpu.SMEM)


def project_kernel(order_ref, x_ref, tv_ref, w_ref, bq_ref, bv_ref, q_ref, k_ref, v_ref, low_ref):
    low = (x_ref[0].astype(F32) + tv_ref[0]).astype(BF16)
    low_ref[0] = low
    q_ref[0] = ((mm(low, w_ref[0], NT) + bq_ref[...]) * (LOG2E / math.sqrt(HEAD))).astype(BF16)
    k_ref[0] = mm(low, w_ref[1], NT).astype(BF16)
    v_ref[0] = (mm(low, w_ref[2], NT) + bv_ref[...]).astype(BF16)


def project(rows, time_vec, weights, bias_q, bias_v, tensor, after=()):
    seqs, count, width = rows.shape
    head_width = weights.shape[1]
    step = count // 2
    narrow = pl.BlockSpec((1, step, head_width), lambda s, i, t: (s, i, 0))
    bias = pl.BlockSpec((1, head_width), lambda s, i, t: (0, 0))
    return call(
        project_kernel,
        "project",
        [
            pl.BlockSpec((1, step, width), lambda s, i, t: (s, i ^ t[0], 0)),
            pl.BlockSpec((1, 1, width), lambda s, i, t: (s, 0, 0)),
            pl.BlockSpec(weights.shape, lambda s, i, t: (0, 0, 0)),
            bias,
            bias,
        ],
        (rows, time_vec[:, None, :], weights, bias_q[None], bias_v[None]),
        [narrow, narrow, narrow, pl.BlockSpec((1, step, width), lambda s, i, t: (s, i, 0))],
        [like((seqs, count, head_width), BF16)] * 3 + [pltpu.HBM(rows.shape, BF16)],
        (seqs, 2),
        [tensor],
        after=after,
    )


def attend_kernel(heads, qn_ref, qf_ref, kn_ref, kf_ref, vn_ref, vf_ref, mask_ref, o_ref, sum_ref, exp_ref, held, sems):
    rows = qn_ref.shape[1]
    seq = pl.program_id(0)

    def store(s, head):
        return pltpu.make_async_copy(held.at[s, head], exp_ref.at[s, head], sems.at[s, head])

    keys = jnp.concatenate([kn_ref[0], kf_ref[0]], axis=0)
    values = jnp.concatenate([vn_ref[0], vf_ref[0]], axis=0)
    queries = jnp.concatenate([qn_ref[0], qf_ref[0]], axis=0)
    ones = jnp.ones((2 * rows, HEAD), BF16)
    many = jnp.ones((keys.shape[0], HEAD), BF16)

    def scores_of(head):
        lanes = slice(head * HEAD, (head + 1) * HEAD)
        return mm(
            jnp.concatenate([queries[:, lanes], ones], axis=1),
            jnp.concatenate([keys[:, lanes], mask_ref[0]], axis=1),
            NT,
        )

    outs = []
    scores = scores_of(0)
    for head in range(heads):
        later = scores_of(head + 1) if head + 1 < heads else None
        power = jnp.exp2(scores - jnp.max(scores, axis=1, keepdims=True)).astype(BF16)
        lanes = slice(head * HEAD, (head + 1) * HEAD)
        total = mm(power, jnp.concatenate([values[:, lanes], many], axis=1))
        held[seq, head] = power
        store(seq, head).start()
        inverse = 1.0 / total[:, HEAD:]
        out = (total[:, :HEAD] * inverse).astype(BF16)
        high = inverse.astype(BF16)
        rest = (inverse - high.astype(F32)).astype(BF16)
        sum_ref[0, head] = jnp.concatenate([out, high[:, : HEAD // 2], rest[:, HEAD // 2 :]], axis=1)
        outs.append(out)
        scores = later
    out = jnp.concatenate(outs, axis=1)
    o_ref[0, 0] = out[:rows]
    o_ref[1, 0] = out[rows:]

    @pl.when(seq == pl.num_programs(0) - 1)
    def _():
        for s in range(exp_ref.shape[0]):
            for head in range(heads):
                store(s, head).wait()


def attend(part, queries, keys, values, mask):
    seqs, half_rows, head_width = queries[0].shape
    rows = half_rows // 2
    heads = head_width // HEAD
    q_spec = pl.BlockSpec((1, rows, head_width), lambda s: (s, part, 0))
    k_spec = pl.BlockSpec((1, half_rows, head_width), lambda s: (s, 0, 0))
    return call(
        lambda *refs: attend_kernel(heads, *refs),
        "attend",
        [q_spec, q_spec, k_spec, k_spec, k_spec, k_spec]
        + [pl.BlockSpec((1, 2 * half_rows, HEAD), lambda s: (s, 0, 0))],
        (*queries, *keys, *values, mask),
        [
            pl.BlockSpec((2, 1, rows, head_width), lambda s: (0, s, 0, 0)),
            pl.BlockSpec((1, heads, 2 * rows, 2 * HEAD), lambda s: (s, 0, 0, 0)),
            HBM,
        ],
        [
            like((2, seqs, rows, head_width), BF16),
            pltpu.HBM((seqs, heads, 2 * rows, 2 * HEAD), BF16),
            pltpu.HBM((seqs, heads, 2 * rows, 2 * half_rows), BF16),
        ],
        (seqs,),
        None,
        [
            pltpu.VMEM((seqs, heads, 2 * rows, 2 * half_rows), BF16),
            pltpu.SemaphoreType.DMA((seqs, heads)),
        ],
    )


def attend_back_kernel(heads, first, gn_ref, gf_ref, sum_ref, exp_ref, qn_ref, qf_ref, kn_ref, kf_ref, vn_ref, vf_ref, *refs):
    before, (dq_ref, dk_ref, dv_ref, held, sems) = refs[:-5], refs[-5:]
    seq = pl.program_id(0)

    def load(s, head):
        return pltpu.make_async_copy(exp_ref.at[s, head], held.at[s, head], sems.at[s, head])

    @pl.when(seq == 0)
    def _():
        for s in range(exp_ref.shape[0]):
            for head in range(heads):
                load(s, head).start()

    rows = gn_ref.shape[2]
    keys = jnp.concatenate([kn_ref[0], kf_ref[0]], axis=0)
    values = jnp.concatenate([vn_ref[0], vf_ref[0]], axis=0)
    queries = jnp.concatenate([qn_ref[0], qf_ref[0]], axis=0)
    grads = jnp.concatenate([gn_ref[0, 0], gf_ref[0, 0]], axis=0)

    def prepare(head):
        lanes = slice(head * HEAD, (head + 1) * HEAD)
        kept = sum_ref[0, head].astype(F32)
        inverse = kept[:, HEAD : HEAD + 1] + kept[:, 3 * HEAD // 2 : 3 * HEAD // 2 + 1]
        grad = (grads[:, lanes].astype(F32) * inverse).astype(BF16)
        inner = jnp.sum(grad.astype(F32) * kept[:, :HEAD], axis=1, keepdims=True)
        return grad, inner, mm(grad, values[:, lanes], NT)

    grad_q = []
    ready = prepare(0)
    for head in range(heads):
        later = prepare(head + 1) if head + 1 < heads else None
        lanes = slice(head * HEAD, (head + 1) * HEAD)
        grad, inner, grad_power = ready
        load(seq, head).wait()
        power = held[seq, head]
        grad_scores = power * (grad_power - inner).astype(BF16)
        grad_q.append(mm(grad_scores, keys[:, lanes]) * (1.0 / math.sqrt(HEAD)))
        grad_k = mm(queries[:, lanes], grad_scores, TN) * (1.0 / LOG2E)
        grad_v = mm(grad, power, TN)
        if not first:
            grad_k = grad_k + before[0][0, lanes].astype(F32)
            grad_v = grad_v + before[1][0, lanes].astype(F32)
        dk_ref[0, lanes] = grad_k.astype(dk_ref.dtype)
        dv_ref[0, lanes] = grad_v.astype(dv_ref.dtype)
        ready = later
    grad_q = jnp.concatenate(grad_q, axis=1).astype(BF16)
    dq_ref[0, 0] = grad_q[:rows]
    dq_ref[1, 0] = grad_q[rows:]


def attend_back(part, grads, sums, powers, queries, keys, values, before=()):
    seqs, half_rows, head_width = queries[0].shape
    rows = half_rows // 2
    heads = head_width // HEAD
    first = not before
    q_spec = pl.BlockSpec((1, rows, head_width), lambda s: (s, part, 0))
    k_spec = pl.BlockSpec((1, half_rows, head_width), lambda s: (s, 0, 0))
    (near_grad, near_block), (far_grad, far_block) = grads
    t_spec = pl.BlockSpec((1, head_width, 2 * half_rows), lambda s: (s, 0, 0))
    return call(
        lambda *refs: attend_back_kernel(heads, first, *refs),
        "attend_back",
        [
            pl.BlockSpec((1, 1, rows, head_width), lambda s: (near_block, s, 0, 0)),
            pl.BlockSpec((1, 1, rows, head_width), lambda s: (far_block, s, 0, 0)),
            pl.BlockSpec((1, heads, 2 * rows, 2 * HEAD), lambda s: (s, 0, 0, 0)),
            HBM,
            q_spec,
            q_spec,
            k_spec,
            k_spec,
            k_spec,
            k_spec,
        ]
        + [t_spec] * len(before),
        (near_grad, far_grad, sums, powers, *queries, *keys, *values, *before),
        [pl.BlockSpec((2, 1, rows, head_width), lambda s: (0, s, 0, 0)), t_spec, t_spec],
        [like((2, seqs, rows, head_width), BF16)]
        + [like((seqs, head_width, 2 * half_rows), BF16)] * 2,
        (seqs,),
        None,
        [
            pltpu.VMEM((seqs, heads, 2 * rows, 2 * half_rows), BF16),
            pltpu.SemaphoreType.DMA((seqs, heads)),
        ],
        pins=tuple(range(10 + len(before))),
    )


def normalize(values):
    centre = values - jnp.mean(values, axis=-1, keepdims=True)
    scale = lax.rsqrt(jnp.mean(centre * centre, axis=-1, keepdims=True) + 1e-05)
    return centre * scale, scale


def normalize_back(grad, unit, scale):
    return scale * (
        grad
        - jnp.mean(grad, axis=-1, keepdims=True)
        - unit * jnp.mean(grad * unit, axis=-1, keepdims=True)
    )


def gelu_parts(values):
    size = jnp.abs(values)
    bell = jnp.exp2(values * values * (-0.5 * LOG2E))
    t = 1.0 / (1.0 + (0.3275911 * math.sqrt(0.5)) * size)
    tail = 0.5 * 1.061405429
    for factor in (-1.453152027, 1.421413741, -0.284496736, 0.254829592):
        tail = tail * t + 0.5 * factor
    tail = tail * t * bell
    below = jnp.where(values < 0.0, tail, 1.0 - tail)
    return values * below, below + values * (bell * (1.0 / math.sqrt(2.0 * math.pi)))


def staged(count, stages):
    depth = len(stages)

    def turn(now, parity, first, last):
        for k in range(first, last):
            stages[k](now - k, (parity - k) % 2)

    for now in range(depth - 1):
        turn(now, now % 2, 0, now + 1)

    def body(step, carry):
        for p in range(2):
            turn(2 * step + p + depth - 1, (p + depth - 1) % 2, 0, depth)
        return carry

    full = count - depth + 1
    lax.fori_loop(0, full // 2, body, 0)
    for now in range(count - full % 2, count):
        turn(now, now % 2, 0, depth)
    for now in range(count, count + depth - 1):
        turn(now, now % 2, now - count + 1, depth)


def rows_kernel(order_ref, near_ref, tv_ref, cot_ref, steps_ref, table_ref, bo_ref, g1_ref, s1_ref, bd_ref, g2_ref, s2_ref, bu0, bu1, bu2, bu3, *refs):
    atts, wos, wus, wds = refs[:4], refs[4:8], refs[8:12], refs[12:16]
    part_ref = refs[16]
    out_o, gpre_o, own_o, core_o, back_own_o, back_h_o, back_y_o = refs[17:24]
    wo, wu, wd, slopes, held_a, held_b, now_a, now_b, unit_one, scale_one, total = refs[24:35]
    out_v, gpre_v, low_v, act_v, mix_v, grad_v, branch_v, back_v = refs[35:43]
    bias_up = refs[43]
    sems, out_sems = refs[44:46]
    held, now = (held_a, held_b), (now_a, now_b)
    seqs, rows, width = cot_ref.shape
    loads = [
        [pltpu.make_async_copy(s, target.at[j], sems.at[group, j]) for j, s in enumerate(sources)]
        for group, (sources, target) in enumerate(((wos, wo), (wus, wu), (wds, wd)))
    ]
    for j in range(4):
        loads[0][j].start()
    for j in range(4):
        loads[1][j].start()
        loads[2][j].start()
    for j, ref in enumerate((bu0, bu1, bu2, bu3)):
        bias_up[j : j + 1] = ref[...]
    stores = []

    def store(source, target):
        copy = pltpu.make_async_copy(source, target, out_sems.at[len(stores)])
        copy.start()
        stores.append(copy)

    for copy in loads[0]:
        copy.wait()
    for s in range(seqs):
        here = pl.ds(s * rows, rows)
        pre = near_ref[s].astype(F32) + tv_ref[s : s + 1] + bo_ref[...]
        for j in range(4):
            pre = pre + mm(atts[j][0, s], wo[j])
        unit, scale = normalize(pre)
        unit_one[here] = unit
        scale_one[here] = scale
        normed = unit * g1_ref[...] + s1_ref[...]
        low_v[here] = normed.astype(BF16)
        total[here] = normed + bd_ref[...]
    store(low_v, own_o.at[5])
    store(low_v, core_o.at[5])
    for copy in loads[1] + loads[2]:
        copy.wait()

    def where(i):
        return i // seqs, pl.ds(lax.rem(i, seqs) * rows, rows)

    def upward(i, p):
        j, here = where(i)
        held[p][...] = mm(low_v[here], wu[j]) + bias_up[pl.ds(j, 1)]

    def gelu(i, p):
        j, here = where(i)
        act, slope = gelu_parts(held[p][...])
        act = act.astype(BF16)
        now[p][...] = act
        act_v[j, here] = act
        slopes[j, here] = slope.astype(BF16)

    def downward(i, p):
        j, here = where(i)
        total[here] += mm(now[p][...], wd[j])

    staged(4 * seqs, (upward, gelu, downward))
    store(act_v.at[2:4], core_o.at[0:2])
    store(act_v.at[0:2], own_o.at[0:2])

    sums = [0.0] * 3
    for s in range(seqs):
        here = pl.ds(s * rows, rows)
        unit, scale = normalize(total[here])
        out_v[s] = (unit * g2_ref[...] + s2_ref[...]).astype(BF16)
        grad = cot_ref[s].astype(F32) * table_ref[steps_ref[s]]
        sums[1] += jnp.sum(grad * unit, axis=0, keepdims=True)
        sums[2] += jnp.sum(grad, axis=0, keepdims=True)
        grad = normalize_back(grad * g2_ref[...], unit, scale)
        mixed = grad.astype(BF16)
        mix_v[here] = mixed
        total[here] = grad
        sums[0] += jnp.sum(mixed.astype(F32), axis=0, keepdims=True)
    store(out_v, out_o)
    store(mix_v, core_o.at[4])
    store(mix_v, own_o.at[4])
    part_ref[3:6] = jnp.concatenate(sums)
    part_ref[8:16] = jnp.zeros((8, width), F32)

    def back_down(i, p):
        j, here = where(i)
        held[p][...] = mm(mix_v[here], wd[j], NT)

    def back_gelu(i, p):
        j, here = where(i)
        grad = (held[p][...] * slopes[j, here].astype(F32)).astype(BF16)
        now[p][...] = grad
        grad_v[j, here] = grad
        part_ref[pl.ds(8 + j, 1)] += jnp.sum(grad.astype(F32), axis=0, keepdims=True)

    def back_up(i, p):
        j, here = where(i)
        total[here] += mm(now[p][...], wu[j], NT)

    staged(4 * seqs, (back_down, back_gelu, back_up))
    store(grad_v.at[2:4], core_o.at[2:4])
    store(grad_v.at[0:2], own_o.at[2:4])
    sums = [0.0] * 3
    for s in range(seqs):
        here = pl.ds(s * rows, rows)
        unit, grad = unit_one[here], total[here]
        sums[1] += jnp.sum(grad * unit, axis=0, keepdims=True)
        sums[2] += jnp.sum(grad, axis=0, keepdims=True)
        grad_pre = normalize_back(grad * g1_ref[...], unit, scale_one[here])
        gpre_v[here] = grad_pre
        branch = grad_pre.astype(BF16)
        branch_v[here] = branch
        sums[0] += jnp.sum(branch.astype(F32), axis=0, keepdims=True)
        part_ref[6 + s : 7 + s] = jnp.sum(grad_pre, axis=0, keepdims=True)
        for j in range(4):
            back_v[j, s] = mm(branch, wo[j], NT).astype(BF16)
    store(back_v.at[1], back_y_o.at[0])
    store(back_v.at[3], back_y_o.at[1])
    store(back_v.at[2], back_h_o.at[0])
    store(back_v.at[0], back_own_o.at[0])
    store(branch_v, core_o.at[6])
    store(branch_v, own_o.at[6])
    store(gpre_v, gpre_o)
    part_ref[0:3] = jnp.concatenate(sums)
    for copy in stores:
        copy.wait()


def rows_part(inputs, time_vec, cotangent, timesteps, importance, vectors, bias_up, atts, wos, wus, wds, tensor):
    seqs, rows, width = cotangent.shape
    flat, hidden, head_width = seqs * rows, wus[0].shape[1], wos[0].shape[0]
    kept = [
        like((seqs, rows, width), BF16),
        like((flat, width), F32),
        pltpu.HBM((7, flat, hidden), BF16),
        pltpu.HBM((7, flat, hidden), BF16),
        pltpu.HBM((1, seqs, rows, head_width), BF16),
        pltpu.HBM((1, seqs, rows, head_width), BF16),
        pltpu.HBM((2, seqs, rows, head_width), BF16),
    ]
    return call(
        rows_kernel,
        "rows_part",
        [pl.BlockSpec((seqs, rows, width), lambda i, t: (0, t[0], 0)), VMEM, VMEM, SMEM, SMEM]
        + [VMEM] * 6
        + [VMEM] * 4
        + [pl.BlockSpec((1, seqs, rows, head_width), lambda i, t, b=b: (b, 0, 0, 0)) for _, b in atts]
        + [HBM] * 12,
        (
            inputs,
            time_vec,
            cotangent,
            timesteps,
            importance,
            *[v[None] for v in vectors],
            *[v[None] for v in bias_up],
            *[a for a, _ in atts],
            *wos,
            *wus,
            *wds,
        ),
        [VMEM] + [HBM] * len(kept),
        [like((16, width), F32)] + kept,
        (1,),
        [tensor],
        [
            pltpu.VMEM((4,) + wos[0].shape, BF16),
            pltpu.VMEM((4,) + wus[0].shape, BF16),
            pltpu.VMEM((4,) + wds[0].shape, BF16),
            pltpu.VMEM((4, flat, hidden), BF16),
            pltpu.VMEM((rows, hidden), F32),
            pltpu.VMEM((rows, hidden), F32),
            pltpu.VMEM((rows, hidden), BF16),
            pltpu.VMEM((rows, hidden), BF16),
            pltpu.VMEM((flat, width), F32),
            pltpu.VMEM((flat, 1), F32),
            pltpu.VMEM((flat, width), F32),
            pltpu.VMEM((seqs, rows, width), BF16),
            pltpu.VMEM((flat, width), F32),
            pltpu.VMEM((flat, width), BF16),
            pltpu.VMEM((4, flat, hidden), BF16),
            pltpu.VMEM((flat, width), BF16),
            pltpu.VMEM((4, flat, hidden), BF16),
            pltpu.VMEM((flat, width), BF16),
            pltpu.VMEM((4, seqs, rows, head_width), BF16),
            pltpu.VMEM((4, hidden), F32),
            pltpu.SemaphoreType.DMA((3, 4)),
            pltpu.SemaphoreType.DMA((20,)),
        ],
        pins=tuple(range(19, 31)),
    )


def weight_grad_kernel(sides, place_ref, own_ref, far_ref, send_ref, keep_ref, left, right, out, sems, out_sems):
    _, rows, width = own_ref.shape
    step = width // 2
    y_first, mine, tensor = place_ref[0], place_ref[1], place_ref[2]
    loads = {}
    for chunk in range(2):
        for number, (target, (first, chunks)) in enumerate(zip((right, left), reversed(sides))):
            if chunk < target.shape[0]:
                loads[number, chunk] = [
                    pltpu.make_async_copy(
                        ref.at[first + chunk], target.at[chunk, pl.ds(source * rows, rows)], sems.at[number, chunk, source]
                    )
                    for source, ref in enumerate((own_ref, far_ref))
                ]
                for copy in loads[number, chunk]:
                    copy.start()
    for chunk in range(2):
        for number in range(2):
            for copy in loads.get((number, chunk), ()):
                copy.wait()
        for half in range(2):
            lanes = slice(half * step, (half + 1) * step)
            spot = 2 * chunk + half
            out[spot] = mm(left[min(chunk, left.shape[0] - 1), :, lanes], right[min(chunk, right.shape[0] - 1)], TN).astype(BF16)
            tens = tensor ^ chunk
            outer = jnp.where(y_first == 1, tens, half)
            inside = jnp.where(y_first == 1, half, tens)

            @pl.when(outer != mine)
            def _():
                pltpu.make_async_copy(out.at[spot], send_ref.at[pl.ds(inside * step, step)], out_sems.at[spot]).start()

            @pl.when(outer == mine)
            def _():
                pltpu.make_async_copy(out.at[spot], keep_ref.at[pl.ds(inside * step, step)], out_sems.at[spot]).start()

    for spot in range(4):
        pltpu.make_async_copy(out.at[spot], send_ref.at[pl.ds(0, step)], out_sems.at[spot]).wait()


def weight_grad(own, far, left, right, y_first, first):
    _, rows, width = own.shape
    step = width // 2
    return call(
        lambda *refs: weight_grad_kernel((left, right), *refs),
        "weight_grad",
        [ANY, ANY],
        (own, far),
        [ANY, ANY],
        [pltpu.HBM((2 * step, width), BF16)] * 2,
        (1,),
        [y_first, first, lax.axis_index("tensor")],
        [
            pltpu.VMEM((1 + left[1], 2 * rows, width), BF16),
            pltpu.VMEM((1 + right[1], 2 * rows, width), BF16),
            pltpu.VMEM((4, step, width), BF16),
            pltpu.SemaphoreType.DMA((2, 2, 2)),
            pltpu.SemaphoreType.DMA((4,)),
        ],
        pins=(0, 1),
    )


def out_grad_kernel(own_ref, far_ref, other_ref, other_far_ref, right_ref, right_far_ref, own_out, other_out):
    count = right_ref.shape[1]

    def product(near, far):
        return (
            mm(near[...].reshape(count, -1), right_ref[0], TN)
            + mm(far[...].reshape(count, -1), right_far_ref[0], TN)
        ).astype(BF16)

    other_out[...] = product(other_ref, other_far_ref)
    own_out[...] = product(own_ref, far_ref)


def out_grad(sides, own, far, place_of):
    _, rows, width = own.shape
    head_width = sides[0][0].shape[3]
    shape = (head_width, width)
    right = pl.BlockSpec((1, rows, width), lambda i: (place_of, 0, 0))
    return call(
        out_grad_kernel,
        "out_grad",
        [pl.BlockSpec((1,) + a.shape[1:], lambda i, b=b: (b, 0, 0, 0)) for a, b in sides] + [right, right],
        (*[a for a, _ in sides], own, far),
        [VMEM, VMEM],
        [like(shape, BF16)] * 2,
        (1,),
        pins=tuple(range(6)),
    )


SHARED = 16


def padded(count):
    return -(-(SHARED + 2 * count) // 16) * 16


def put_vectors(ref, first, value):
    rows = value.shape[0]
    high = value.astype(BF16)
    low = (value - high.astype(F32)).astype(BF16)
    ref[first : first + rows] = high
    ref[first + rows : first + 2 * rows] = low
    return high.astype(F32) + low.astype(F32)


def get_vectors(ref, first, rows):
    return ref[first : first + rows].astype(F32) + ref[first + rows : first + 2 * rows].astype(F32)


def qkv_grad_kernel(place_ref, dqs_b, dqs_a, dk_ref, dv_ref, near_ref, far_ref, w_ref, out_ref, got_ref, parts_ref, feat_ref, send_ref, keep_ref, vec_ref):
    seqs, half_rows, _ = near_ref.shape
    rows = half_rows // 2
    width = dk_ref.shape[1]
    blocks = ((dqs_b, 0, near_ref, 0), (dqs_a, 0, near_ref, rows), (dqs_b, 1, far_ref, 0), (dqs_a, 1, far_ref, rows))

    def put(half, first, value):
        @pl.when(place_ref[0] == half)
        def _():
            keep_ref[first : first + width] = value

        @pl.when(place_ref[0] != half)
        def _():
            send_ref[first : first + width] = value

    for c, ref in ((1, dk_ref), (2, dv_ref)):
        grad = sum(
            mm(ref[s, :, :half_rows], near_ref[s]) + mm(ref[s, :, half_rows:], far_ref[s])
            for s in range(seqs)
        )
        put(1, (c - 1) * width, grad.astype(BF16))
    grad_q = sum(
        mm(dq[b, s], low[s, first : first + rows], TN)
        for dq, b, low, first in blocks
        for s in range(seqs)
    )
    put(0, 0, (out_ref[...].astype(F32) + got_ref[...].astype(F32)).astype(BF16))
    put(0, width, grad_q.astype(BF16))
    vec_ref[...] = jnp.zeros_like(vec_ref)
    vec_ref[0:6] = parts_ref[0:6]
    vec_ref[6:10] = parts_ref[8:12]
    ones = jnp.ones((8, rows), BF16)
    many = jnp.ones((8, 2 * half_rows), BF16)
    bias = [0.0] * 3
    for s in range(seqs):
        sums = [
            sum(mm(ones, dq[b, s]) for dq, b, _, _ in blocks),
            mm(many, dk_ref[s], NT),
            mm(many, dv_ref[s], NT),
        ]
        back = 0.0
        for c in range(3):
            bias[c] = bias[c] + sums[c][0:1]
            high = sums[c].astype(BF16)
            rest = (sums[c] - high.astype(F32)).astype(BF16)
            back = back + mm(high, w_ref[c]) + mm(rest, w_ref[c])
        vec_ref[SHARED + s : SHARED + s + 1] = parts_ref[6 + s : 7 + s] + back[0:1]
    empty = jnp.zeros((1, vec_ref.shape[1] - 2 * width), F32)
    vec_ref[10:11] = jnp.concatenate([bias[0], bias[2], empty], axis=1)
    vec_ref[SHARED + seqs : SHARED + 2 * seqs] = feat_ref[...]
    vec_ref[...] = put_vectors(send_ref, 2 * width, vec_ref[...])


def qkv_grad(dqs_b, dqs_a, dk, dv, near, far, weights, out_own, out_got, parts, feats, mine):
    seqs, _, width = near.shape
    head_width = weights.shape[1]
    return call(
        qkv_grad_kernel,
        "qkv_grad",
        [VMEM] * 11,
        (dqs_b, dqs_a, dk, dv, near, far, weights, out_own, out_got, parts, feats),
        [VMEM] * 3,
        [
            like((2 * head_width + 2 * padded(seqs), width), BF16),
            like((2 * head_width, width), BF16),
            like((padded(seqs), width), F32),
        ],
        (1,),
        [mine],
    )


def input_grad_kernel(dqs_b, dqs_a, dk_ref, dv_ref, w_ref, own_ref, y_ref, far_ref):
    seqs, width, columns = dk_ref.shape
    half_rows = columns // 2
    rows = half_rows // 2
    for half in (1, 0):
        for s in range(seqs):
            lanes = slice(half * half_rows, (half + 1) * half_rows)
            part = mm(dk_ref[s, :, lanes], w_ref[1], TN) + mm(dv_ref[s, :, lanes], w_ref[2], TN)
            own = part[:rows] + mm(dqs_b[half, s], w_ref[0])
            other = part[rows:] + mm(dqs_a[half, s], w_ref[0])
            if half == 0:
                own_ref[s] = own
                y_ref[s] = other.astype(BF16)
            else:
                far_ref[0, s] = own.astype(BF16)
                far_ref[1, s] = other.astype(BF16)


def input_grad(dqs_b, dqs_a, dk, dv, weights):
    seqs, head_width, columns = dk.shape
    width, rows = weights.shape[2], columns // 4
    return call(
        input_grad_kernel,
        "input_grad",
        [VMEM] * 5,
        (dqs_b, dqs_a, dk, dv, weights),
        [VMEM] * 3,
        [
            like((seqs, rows, width), F32),
            like((seqs, rows, width), BF16),
            like((2, seqs, rows, width), BF16),
        ],
    )


def input_cross_kernel(y_ref, got_ref, out_ref):
    out_ref[...] = (y_ref[...].astype(F32) + got_ref[0].astype(F32)).astype(BF16)


def input_cross(part, got):
    seqs, rows, width = part.shape
    block = pl.BlockSpec((1, rows, width), lambda s: (s, 0, 0))
    return call(
        input_cross_kernel,
        "input_cross",
        [block, pl.BlockSpec((1, 1, rows, width), lambda s: (1, s, 0, 0))],
        (part, got),
        block,
        like(part.shape, BF16),
        (seqs,),
    )


def input_total_kernel(pre_ref, own_ref, got_ref, cross_ref, out_ref):
    out_ref[0] = pre_ref[...] + (own_ref[0] + got_ref[0, 0].astype(F32)) + cross_ref[0].astype(F32)


def input_total(pre, own, got, cross):
    seqs, rows, width = own.shape
    block = pl.BlockSpec((1, rows, width), lambda s: (s, 0, 0))
    return call(
        input_total_kernel,
        "input_total",
        [pl.BlockSpec((rows, width), lambda s: (s, 0)), block, pl.BlockSpec((1, 1, rows, width), lambda s: (0, s, 0, 0)), block],
        (pre, own, got, cross),
        block,
        like(own.shape, F32),
        (seqs,),
    )


def sinusoid(step_ids, feature_count):
    halfway = feature_count // 2
    frequency = jnp.exp(-math.log(10000.0) * jnp.arange(halfway, dtype=F32) / halfway)
    angles = step_ids.astype(F32)[:, None] * frequency[None, :]
    return jnp.concatenate([jnp.cos(angles), jnp.sin(angles)], axis=1)


def halved(value, mine):
    rows = value.shape[0] // 2
    return (
        lax.dynamic_slice_in_dim(value, (1 - mine) * rows, rows, 0),
        lax.dynamic_slice_in_dim(value, mine * rows, rows, 0),
    )


def split_kernel(mine_ref, keep_send, got_send, keep_keep, got_keep, send_ref, keep_ref):
    send_ref[...] = (keep_send[...].astype(F32) + got_send[...].astype(F32)).astype(BF16)
    keep_ref[...] = (keep_keep[...].astype(F32) + got_keep[...].astype(F32)).astype(BF16)


def add_split(keep, got, mine):
    rows, width = keep.shape
    blocks = 2 if rows % 64 == 0 else 1
    step = rows // 2 // blocks
    send = pl.BlockSpec((step, width), lambda i, m: ((1 - m[0]) * blocks + i, 0))
    stay = pl.BlockSpec((step, width), lambda i, m: (m[0] * blocks + i, 0))
    out = pl.BlockSpec((step, width), lambda i, m: (i, 0))
    if step % 8:
        total = (keep.astype(F32) + got.astype(F32)).astype(BF16)
        return halved(total, mine)
    return call(
        split_kernel,
        "add_split",
        [send, send, stay, stay],
        (keep, got, keep, got),
        [out, out],
        [like((rows // 2, width), BF16)] * 2,
        (blocks,),
        [mine],
    )


def add_kernel(left, right, out_ref):
    out_ref[...] = (left[...].astype(F32) + right[...].astype(F32)).astype(BF16)


def add(left, right):
    return call(add_kernel, "add", [VMEM, VMEM], (left, right), VMEM, like(left.shape, BF16))


def join_kernel(mine_ref, value_ref, got_ref, out_ref):
    @pl.when(pl.program_id(0) == mine_ref[0])
    def _():
        out_ref[...] = value_ref[...].astype(out_ref.dtype)

    @pl.when(pl.program_id(0) != mine_ref[0])
    def _():
        out_ref[...] = got_ref[...].astype(out_ref.dtype)


def join(value, got, mine, dtype=BF16):
    rows, width = value.shape
    if rows % 8:
        out = jnp.where(mine == 0, jnp.concatenate([value, got]), jnp.concatenate([got, value]))
        return out.astype(dtype)
    whole = pl.BlockSpec((rows, width), lambda i, m: (0, 0))
    return call(
        join_kernel,
        "join",
        [whole, whole],
        (value, got),
        pl.BlockSpec((rows, width), lambda i, m: (i, 0)),
        like((2 * rows, width), dtype),
        (2,),
        [mine],
    )


def joined_vectors(count, mine, value, got, inner=None):
    pieces = [value[:SHARED] + got[:SHARED]]
    for first in (SHARED, SHARED + count):
        own, other = value[first : first + count], got[first : first + count]
        low, high = jnp.where(mine == 0, own, other), jnp.where(mine == 0, other, own)
        if inner is not None:
            middle = count // 2
            a, b = low[middle:], high[:middle]
            low = jnp.concatenate([low[:middle], jnp.where(inner == 1, b, a)])
            high = jnp.concatenate([jnp.where(inner == 1, a, b), high[middle:]])
        pieces += [low, high]
    rest = padded(2 * count) - SHARED - 4 * count
    return jnp.concatenate(pieces + [jnp.zeros((rest, value.shape[1]), F32)] * (rest > 0))


def small_join_kernel(mine_ref, value_ref, got_ref, out_ref, qkv_ref):
    first = mine_ref[0] == 0
    low = jnp.where(first, value_ref[...], got_ref[...]).astype(F32)
    high = jnp.where(first, got_ref[...], value_ref[...]).astype(F32)
    count = out_ref.shape[0]
    out_ref[...] = low[:count]
    qkv_ref[:count] = low[count:]
    qkv_ref[count:] = high


def small_join(value, got, mine):
    rows, width = value.shape
    return call(
        small_join_kernel,
        "small_join",
        [VMEM, VMEM],
        (value, got),
        [VMEM, VMEM],
        [like((rows // 2, width), F32), like((rows // 2 * 3, width), F32)],
        (1,),
        [mine],
    )


def vector_kernel(count, mine_ref, value_ref, got_ref, out_ref):
    out_ref[...] = joined_vectors(count, mine_ref[0], value_ref[...], got_ref[...])


def vector_step(value, got, mine, count):
    return call(
        lambda *refs: vector_kernel(count, *refs),
        "vector_step",
        [VMEM, VMEM],
        (value, got),
        VMEM,
        like((padded(2 * count), value.shape[1]), F32),
        (1,),
        [mine],
    )


def small_kernel(count, last, mine_ref, keep_ref, got_ref, vec_ref, *outs):
    rows = keep_ref.shape[0]
    place_before, mine = mine_ref[0], mine_ref[1]
    vectors = joined_vectors(
        count, place_before, vec_ref[...], get_vectors(got_ref, rows, vec_ref.shape[0]), mine_ref[2] if last else None
    )

    def total(first, size):
        here = pl.ds(pl.multiple_of(first, 16), size)
        return (keep_ref[here].astype(F32) + got_ref[here].astype(F32)).astype(BF16)

    if last:
        outs[0][0:rows] = total(0, rows)
        outs[-1][...] = put_vectors(outs[0], rows, vectors)
    else:
        size = rows // 2
        outs[0][0:size] = total((1 - mine) * size, size)
        outs[-1][...] = put_vectors(outs[0], size, vectors)
        outs[1][...] = total(mine * size, size)


def small_step(keep, got, vectors, count, place_before, mine, last):
    rows, width = keep.shape
    after = padded(2 * count)
    size = rows if last else rows // 2
    out = call(
        lambda *refs: small_kernel(count, last, *refs),
        "small_step",
        [VMEM] * 3,
        (keep, got, vectors),
        [VMEM] * (2 if last else 3),
        [like((size + 2 * after, width), BF16)]
        + ([] if last else [like((size, width), BF16)])
        + [like((after, width), F32)],
        (1,),
        [place_before, mine, lax.axis_index("half")],
    )
    return (out[0], None, out[1]) if last else out


def small_end_kernel(count, mine_ref, value_ref, got_ref, vec_ref, out_ref, vec_out):
    rows = out_ref.shape[0]
    vec_out[...] = joined_vectors(count, mine_ref[0], vec_ref[...], get_vectors(got_ref, rows, vec_ref.shape[0]))
    out_ref[...] = (value_ref[0:rows].astype(F32) + got_ref[0:rows].astype(F32)).astype(BF16)


def small_end(value, got, vectors, count, mine):
    rows = value.shape[0] - 2 * vectors.shape[0]
    width = value.shape[1]
    return call(
        lambda *refs: small_end_kernel(count, *refs),
        "small_end",
        [VMEM] * 3,
        (value, got, vectors),
        [VMEM] * 2,
        [like((rows, width), BF16), like((padded(2 * count), width), F32)],
        (1,),
        [mine],
    )


def fold_kernel(first, second, chunks, value_ref, got_ref, out_ref):
    out_ref[...] = value_ref[...]
    out_ref[0:6] = value_ref[0:6] + got_ref[0:6]
    out_ref[6 : 6 + chunks] = value_ref[6 : 6 + chunks] + got_ref[6 + chunks : 6 + 2 * chunks]
    out_ref[first:second] = value_ref[first:second] + got_ref[first:second]


def fold(value, got, count, chunks):
    return call(
        lambda *refs: fold_kernel(SHARED, SHARED + count, chunks, *refs),
        "fold",
        [VMEM, VMEM],
        (value, got),
        VMEM,
        like(value.shape, F32),
    )


def per_device(
    inputs,
    cotangent,
    src_lengths,
    tgt_mask,
    timesteps,
    importance,
    w_qkv,
    b_qv,
    w_out,
    b_out,
    gain_one,
    shift_one,
    w_up,
    b_up,
    w_down,
    b_down,
    gain_two,
    shift_two,
    w_time1,
    time_bias1,
    w_time2,
    time_bias2,
):
    Order.token = None
    half = lax.axis_index("half")
    tensor = lax.axis_index("tensor")
    seqs, half_rows, width = inputs.shape
    rows = half_rows // lax.axis_size("tensor")
    hidden = w_up.shape[1]
    head_width = w_qkv.shape[2]
    bits = lax.axis_size("dp").bit_length() - 1

    far = swap(inputs, "core")

    spread = [(0, 1), (1, 0)]

    def quarter(shard):
        _, value = halved(shard, place(*spread[1]))
        _, value = halved(value, place(*spread[0]))
        return value

    up_one = swap(quarter(w_up), "y")
    out_one = swap(w_out, "y")
    down_one = swap(quarter(w_down), "y")
    bias_one = swap(b_up, "y")

    features = sinusoid(timesteps, w_time1.shape[0])
    time_sum = jnp.dot(features, w_time1, precision=HIGHEST) + time_bias1
    time_vec = jnp.dot(jax.nn.silu(time_sum), w_time2, precision=HIGHEST) + time_bias2

    feats = jnp.concatenate([time_sum, features], axis=1)
    feats = jnp.pad(feats, ((0, 0), (0, width - feats.shape[1])))

    def own_first(array):
        return jnp.concatenate(
            [
                lax.dynamic_slice_in_dim(array, tensor * rows, rows, 1),
                lax.dynamic_slice_in_dim(array, (1 - tensor) * rows, rows, 1),
            ],
            axis=1,
        )

    positions = jnp.arange(half_rows, dtype=jnp.int32)
    source_live = positions[None, :] < src_lengths[:, None]
    target_live = tgt_mask == 1
    near_live = own_first(jnp.where(half == 0, source_live, target_live))
    far_live = own_first(jnp.where(half == 0, target_live, source_live))
    allowed = jnp.concatenate([near_live, far_live], axis=1)
    mask = jnp.where(
        (jnp.arange(HEAD) == 0)[None, None, :] & ~allowed[:, :, None], MASKED, 0.0
    ).astype(BF16)

    w_turned = jnp.swapaxes(w_qkv, 1, 2)
    q_near, k_near, v_near, low_near = project(inputs, time_vec, w_turned, b_qv[0], b_qv[1], tensor, (feats, mask))
    far, bias_one = hold(far, bias_one)
    up_core, bias_core, bias_two = swap(w_up, "core"), swap(b_up, "core"), swap(bias_one, "core")
    q_far, k_far, v_far, low_far = project(far, time_vec, w_turned, b_qv[0], b_qv[1], tensor)
    queries, keys, values = (q_near, q_far), (k_near, k_far), (v_near, v_far)

    up_one, up_core, bias_core, bias_two = hold(up_one, up_core, bias_core, bias_two)
    up_got = swap(up_one, *spread[0])
    down_core = swap(w_down, "core")
    att_y, sums_a, powers_a = attend(1, queries, keys, values, mask)
    got_y = swap(att_y, "y")
    out_one, down_core = hold(out_one, down_core)
    out_core = swap(out_one, "core")
    up_one = join(up_one, up_got, place(*spread[0]))
    up_got = swap(up_one, *spread[1])
    down_one, out_core = hold(down_one, out_core)
    down_got = swap(down_one, *spread[0])
    att_own, sums_b, powers_b = attend(0, queries, keys, values, mask)
    got_h = swap(att_own, "core")
    got_y, got_h = hold(got_y, got_h)
    got_far, out_two = swap(got_y, "core"), swap(w_out, "core")
    down_one = join(down_one, down_got, place(*spread[0]))
    down_got = swap(down_one, *spread[1])
    up_one = join(up_one, up_got, place(*spread[1]))
    up_three = swap(up_one, "core")
    got_far, out_two, up_three = hold(got_far, out_two, up_three)
    down_one = join(down_one, down_got, place(*spread[1]))
    outs_w = [w_out, out_one, out_two, out_core]
    ups_w = [w_up, up_one, up_core, up_three]
    downs_w = [w_down, down_one, down_core, swap(down_one, "core")]
    ups_b = [b_up, bias_one, bias_core, bias_two]
    atts = ((att_own, 0), (got_y, 0), (got_h, 1), (got_far, 1))

    (
        parts,
        outputs,
        grad_pre,
        own,
        core,
        back_own,
        back_h,
        back_y,
    ) = rows_part(
        inputs,
        time_vec,
        cotangent,
        timesteps,
        importance,
        (b_out, gain_one, shift_one, b_down, gain_two, shift_two),
        ups_b,
        atts,
        outs_w,
        ups_w,
        downs_w,
        tensor,
    )
    back_h = swap(back_h, "core")
    back_y = swap(back_y, "y")
    back_h, core = hold(back_h, core)
    far_rows = swap(core, "core")

    down_steps = up_steps = [(0, "y"), ("y", 0), (1,)]
    small_steps = [(0, 1), (1, 0)]
    dqs_b, dk, dv = attend_back(0, ((back_own, 0), (back_h, 0)), sums_b, powers_b, queries, keys, values)
    down_send, down_keep = weight_grad(own, far_rows, (0, True), (4, False), half, place(*down_steps[0]))
    down_got = swap(down_send, *down_steps[0])
    (back_y,) = hold(back_y)
    back_d = swap(back_y, "core")
    up_send, up_keep = weight_grad(own, far_rows, (5, False), (2, True), half, place(*up_steps[0]))
    up_got = swap(up_send, *up_steps[0])
    out_own, out_other = out_grad(((att_own, 0), (att_own, 1), (got_y, 0), (got_y, 1)), own, far_rows, 6)
    out_got = swap(out_other, "y")
    def step(keep, got, steps, turn):
        send, keep = add_split(keep, got, place(*steps[turn]))
        return keep, swap(send, *steps[turn])

    def collect(value, got, dims, dtype=BF16):
        return join(value, got, place(*dims), dtype)

    down_keep, down_got = step(down_keep, down_got, down_steps, 1)
    dqs_a, dk, dv = attend_back(1, ((back_y, 0), (back_d, 1)), sums_a, powers_a, queries, keys, values, (dk, dv))
    up_keep, up_got = step(up_keep, up_got, up_steps, 1)
    down_keep, down_got = step(down_keep, down_got, down_steps, 2)
    small_send, small_keep, vectors = qkv_grad(
        dqs_b, dqs_a, dk, dv, low_near, low_far, w_turned, out_own, out_got, parts, feats, place(*small_steps[0])
    )
    small_got = swap(small_send, *small_steps[0])
    dx_own, dx_y, dx_far = input_grad(dqs_b, dqs_a, dk, dv, w_turned)
    up_keep, up_got = step(up_keep, up_got, up_steps, 2)
    down = add(down_keep, down_got)
    down_got = swap(down, 2)
    (dx_far,) = hold(dx_far)
    dx_got = swap(dx_far, "core")
    count = seqs
    small_send, small_keep, vectors = small_step(
        small_keep, small_got, vectors, count, place(*small_steps[0]), place(*small_steps[1]), False
    )
    small_got = swap(small_send, *small_steps[1])
    count *= 2
    up = add(up_keep, up_got)
    up_got = swap(up, 2)
    dx_cross = swap(input_cross(dx_y, dx_got), "y")
    small_send, _, vectors = small_step(
        small_keep, small_got, vectors, count, place(*small_steps[1]), place(2), True
    )
    small_got = swap(small_send, 2)
    count *= 2
    down = add(down, down_got)
    if bits > 3:
        up = add(up, up_got)
        small, vectors = small_end(small_send, small_got, vectors, count, place(2))
        count *= 2
        for bit in range(3, bits):
            down, up, small = (add(v, swap(v, bit)) for v in (down, up, small))
            vectors = vector_step(vectors, swap(vectors, bit), bit_of(bit), count)
            count *= 2
    down_steps = up_steps = [(0,), (1,)]
    down_got = swap(down, *down_steps[1])
    if bits == 3:
        up = add(up, up_got)
    up_got = swap(up, *up_steps[1])
    down = collect(down, down_got, down_steps[1])
    down_got = swap(down, *down_steps[0])
    if bits == 3:
        small, vectors = small_end(small_send, small_got, vectors, count, place(2))
        count *= 2
    small_got = swap(small, *small_steps[1])
    vectors_got = swap(vectors, "core")
    up = collect(up, up_got, up_steps[1])
    up_got = swap(up, *up_steps[0])
    small = collect(small, small_got, small_steps[1])
    small_got = swap(small, *small_steps[0])
    vectors = fold(vectors, vectors_got, count, 2)
    vectors_got = swap(vectors, "y")
    grad_inputs = input_total(grad_pre, dx_own, dx_got, dx_cross)
    grad_w_down = collect(down, down_got, down_steps[0], F32)
    vectors = fold(vectors, vectors_got, count, 1)
    grad_w_up = collect(up, up_got, up_steps[0], F32)
    grad_w_out, qkv = small_join(small, small_got, place(*small_steps[0]))
    grad_w_qkv = jnp.swapaxes(qkv.reshape(3, head_width, width), 1, 2)

    all_grad = vectors[SHARED : SHARED + count]
    all_sum = vectors[SHARED + count : SHARED + 2 * count, : time_sum.shape[1]]
    all_features = vectors[SHARED + count : SHARED + 2 * count, time_sum.shape[1] : time_sum.shape[1] + features.shape[1]]
    gate_of = jax.nn.sigmoid(all_sum)
    all_hidden = all_sum * gate_of
    grad_w_time2 = lax.dot_general(all_hidden, all_grad, TN, precision=HIGHEST)
    grad_hidden = lax.dot_general(all_grad, w_time2, NT, precision=HIGHEST)
    grad_hidden = grad_hidden * (gate_of * (1.0 + all_sum * (1.0 - gate_of)))
    grad_w_time1 = lax.dot_general(all_features, grad_hidden, TN, precision=HIGHEST)
    return (
        outputs,
        grad_inputs,
        grad_w_qkv,
        vectors[10, : 2 * head_width].reshape(2, head_width),
        grad_w_out,
        vectors[0],
        vectors[1],
        vectors[2],
        grad_w_up,
        vectors[6, :hidden],
        grad_w_down,
        vectors[3],
        vectors[4],
        vectors[5],
        grad_w_time1,
        jnp.sum(grad_hidden, axis=0),
        grad_w_time2,
        jnp.sum(all_grad, axis=0),
    )


def solution(mesh):
    in_specs = (
        P("dp", "half", None),
        P("dp", ("half", "tensor"), None),
        P("dp"),
        P("dp", None),
        P("dp"),
        P(),
        P(None, None, ("tensor", "half")),
        P(None, ("tensor", "half")),
        P(("tensor", "half"), None),
        P(),
        P(),
        P(),
        P(None, ("tensor", "half")),
        P(("tensor", "half")),
        P(("tensor", "half"), None),
        P(),
        P(),
        P(),
        P(),
        P(),
        P(),
        P(),
    )
    out_specs = (
        P("dp", ("half", "tensor"), None),
        P("dp", ("half", "tensor"), None),
        P(None, None, ("tensor", "half")),
        P(None, ("tensor", "half")),
        P(("tensor", "half"), None),
        P(),
        P(),
        P(),
        P(None, ("tensor", "half")),
        P(("tensor", "half")),
        P(("tensor", "half"), None),
        P(),
        P(),
        P(),
        P(),
        P(),
        P(),
        P(),
    )
    return jax.shard_map(
        per_device, mesh=mesh, in_specs=in_specs, out_specs=out_specs, check_vma=False
    )
```

```python
import math

import jax
import jax.numpy as jnp
from jax import lax
from jax.experimental import pallas as pl
from jax.experimental.pallas import tpu as pltpu
from jax.sharding import PartitionSpec as P

HEAD = 64
F32 = jnp.float32
BF16 = jnp.bfloat16
HIGHEST = lax.Precision.HIGHEST
LOG2E = math.log2(math.e)
MASKED = -1e9
MIB = 1024 * 1024
GRANTS = {"rows_part": 38, "attend": 24, "attend_back": 24, "qkv_grad": 14, "weight_grad": 14}
ANY = pl.BlockSpec(memory_space=pl.ANY)
HBM = pl.BlockSpec(memory_space=pltpu.HBM)

NT = (((1,), (1,)), ((), ()))
NN = (((1,), (0,)), ((), ()))
TN = (((0,), (0,)), ((), ()))


def mm(left, right, dims=NN):
    return lax.dot_general(left, right, dims, preferred_element_type=F32)


def bit_of(dim):
    if dim == "y":
        return lax.axis_index("tensor")
    if dim == "core":
        return lax.axis_index("half")
    return (lax.axis_index("dp") >> dim) & 1


def swap(value, *dims):
    axes = ("dp", "half", "tensor")
    sizes = [lax.axis_size(a) for a in axes]
    pairs = []
    for d in range(sizes[0]):
        for h in range(2):
            for t in range(2):
                dim = dims[h % len(dims)]
                if dim == "y":
                    to = (d, h, 1 - t)
                elif dim == "core":
                    to = (d, 1 - h, t)
                else:
                    to = (d ^ (1 << dim), h, t)
                pairs.append(((d * 2 + h) * 2 + t, (to[0] * 2 + to[1]) * 2 + to[2]))
    return lax.ppermute(value, axes, pairs)


def place(*dims):
    if len(dims) == 1:
        return bit_of(dims[0])
    return jnp.where(lax.axis_index("half") == 0, bit_of(dims[0]), bit_of(dims[1]))


class Order:
    token = None
    pinned = False


def call(kernel, name, in_specs, args, out_specs, out_shape, grid=(), scalars=None, scratch_shapes=(), aliases=None, after=(), pins=()):
    tokens = (() if Order.token is None else (Order.token,)) + tuple(after)
    if Order.pinned:
        tokens = (pltpu.with_memory_space_constraint(tokens[0], pltpu.HBM), *tokens[1:])
    first = len(in_specs) + (scalars is not None)

    def body(*refs):
        kernel(*refs[:first], *refs[first + len(tokens) :])

    in_specs = list(in_specs) + [ANY] * len(tokens)
    args = [pltpu.with_memory_space_constraint(a, pltpu.HBM) if i in pins else a for i, a in enumerate(args)]
    if scalars is None:
        rest = dict(grid=grid, in_specs=in_specs, out_specs=out_specs, scratch_shapes=scratch_shapes)
    else:
        rest = dict(
            grid_spec=pltpu.PrefetchScalarGridSpec(
                num_scalar_prefetch=1,
                grid=grid,
                in_specs=in_specs,
                out_specs=out_specs,
                scratch_shapes=scratch_shapes,
            )
        )
        args = (jnp.stack(scalars).astype(jnp.int32), *args)
    out = pl.pallas_call(
        body,
        out_shape=out_shape,
        compiler_params=pltpu.CompilerParams(vmem_limit_bytes=GRANTS.get(name, 12) * MIB),
        cost_estimate=cost(name),
        input_output_aliases=aliases or {},
        name=name,
        **rest,
    )(*args, *tokens)
    several = isinstance(out, (list, tuple))
    Order.token = out[0] if several else out
    Order.pinned = not isinstance(out_shape[0] if several else out_shape, jax.ShapeDtypeStruct)
    return out


def hold(*values):
    return call(
        lambda *refs: None,
        "hold",
        [ANY] * len(values),
        values,
        [ANY] * len(values),
        [like(v.shape, v.dtype) for v in values],
        aliases={i: i for i in range(len(values))},
    )


def like(shape, dtype):
    return jax.ShapeDtypeStruct(shape, dtype)


TIMES = {'project': 1.0, 'rows_part': 24, 'attend': 1.0, 'attend_back': 9, 'weight_grad': 6, 'out_grad': 2.4}


def cost(name):
    return pl.CostEstimate(flops=int(TIMES.get(name, 0) * 1.15e9), bytes_accessed=1024, transcendentals=0)


VMEM = pl.BlockSpec(memory_space=pltpu.VMEM)
SMEM = pl.BlockSpec(memory_space=pltpu.SMEM)


def project_kernel(order_ref, x_ref, tv_ref, w_ref, bq_ref, bv_ref, q_ref, k_ref, v_ref, low_ref):
    low = (x_ref[0].astype(F32) + tv_ref[0]).astype(BF16)
    low_ref[0] = low
    q_ref[0] = ((mm(low, w_ref[0], NT) + bq_ref[...]) * (LOG2E / math.sqrt(HEAD))).astype(BF16)
    k_ref[0] = mm(low, w_ref[1], NT).astype(BF16)
    v_ref[0] = (mm(low, w_ref[2], NT) + bv_ref[...]).astype(BF16)


def project(rows, time_vec, weights, bias_q, bias_v, tensor, after=()):
    seqs, count, width = rows.shape
    head_width = weights.shape[1]
    step = count // 2
    narrow = pl.BlockSpec((1, step, head_width), lambda s, i, t: (s, i, 0))
    bias = pl.BlockSpec((1, head_width), lambda s, i, t: (0, 0))
    return call(
        project_kernel,
        "project",
        [
            pl.BlockSpec((1, step, width), lambda s, i, t: (s, i ^ t[0], 0)),
            pl.BlockSpec((1, 1, width), lambda s, i, t: (s, 0, 0)),
            pl.BlockSpec(weights.shape, lambda s, i, t: (0, 0, 0)),
            bias,
            bias,
        ],
        (rows, time_vec[:, None, :], weights, bias_q[None], bias_v[None]),
        [narrow, narrow, narrow, pl.BlockSpec((1, step, width), lambda s, i, t: (s, i, 0))],
        [like((seqs, count, head_width), BF16)] * 3 + [pltpu.HBM(rows.shape, BF16)],
        (seqs, 2),
        [tensor],
        after=after,
        pins=(0, 2),
    )


def attend_kernel(heads, qn_ref, qf_ref, kn_ref, kf_ref, vn_ref, vf_ref, mask_ref, o_ref, sum_ref, exp_ref, held, sems):
    rows = qn_ref.shape[1]
    seq = pl.program_id(0)

    def store(s, head):
        return pltpu.make_async_copy(held.at[s, head], exp_ref.at[s, head], sems.at[s, head])

    keys = jnp.concatenate([kn_ref[0], kf_ref[0]], axis=0)
    values = jnp.concatenate([vn_ref[0], vf_ref[0]], axis=0)
    queries = jnp.concatenate([qn_ref[0], qf_ref[0]], axis=0)
    ones = jnp.ones((2 * rows, HEAD), BF16)
    many = jnp.ones((keys.shape[0], HEAD), BF16)

    def scores_of(head):
        lanes = slice(head * HEAD, (head + 1) * HEAD)
        return mm(
            jnp.concatenate([queries[:, lanes], ones], axis=1),
            jnp.concatenate([keys[:, lanes], mask_ref[0]], axis=1),
            NT,
        )

    outs = []
    scores = scores_of(0)
    for head in range(heads):
        later = scores_of(head + 1) if head + 1 < heads else None
        power = jnp.exp2(scores - jnp.max(scores, axis=1, keepdims=True)).astype(BF16)
        lanes = slice(head * HEAD, (head + 1) * HEAD)
        total = mm(power, jnp.concatenate([values[:, lanes], many], axis=1))
        held[seq, head] = power
        store(seq, head).start()
        inverse = 1.0 / total[:, HEAD:]
        out = (total[:, :HEAD] * inverse).astype(BF16)
        high = inverse.astype(BF16)
        rest = (inverse - high.astype(F32)).astype(BF16)
        sum_ref[0, head] = jnp.concatenate([out, high[:, : HEAD // 2], rest[:, HEAD // 2 :]], axis=1)
        outs.append(out)
        scores = later
    out = jnp.concatenate(outs, axis=1)
    o_ref[0, 0] = out[:rows]
    o_ref[1, 0] = out[rows:]

    @pl.when(seq == pl.num_programs(0) - 1)
    def _():
        for s in range(exp_ref.shape[0]):
            for head in range(heads):
                store(s, head).wait()


def attend(part, queries, keys, values, mask):
    seqs, half_rows, head_width = queries[0].shape
    rows = half_rows // 2
    heads = head_width // HEAD
    q_spec = pl.BlockSpec((1, rows, head_width), lambda s: (s, part, 0))
    k_spec = pl.BlockSpec((1, half_rows, head_width), lambda s: (s, 0, 0))
    return call(
        lambda *refs: attend_kernel(heads, *refs),
        "attend",
        [q_spec, q_spec, k_spec, k_spec, k_spec, k_spec]
        + [pl.BlockSpec((1, 2 * half_rows, HEAD), lambda s: (s, 0, 0))],
        (*queries, *keys, *values, mask),
        [
            pl.BlockSpec((2, 1, rows, head_width), lambda s: (0, s, 0, 0)),
            pl.BlockSpec((1, heads, 2 * rows, 2 * HEAD), lambda s: (s, 0, 0, 0)),
            HBM,
        ],
        [
            like((2, seqs, rows, head_width), BF16),
            pltpu.HBM((seqs, heads, 2 * rows, 2 * HEAD), BF16),
            pltpu.HBM((seqs, heads, 2 * rows, 2 * half_rows), BF16),
        ],
        (seqs,),
        None,
        [
            pltpu.VMEM((seqs, heads, 2 * rows, 2 * half_rows), BF16),
            pltpu.SemaphoreType.DMA((seqs, heads)),
        ],
    )


def attend_back_kernel(part, blocks, first, gn_hbm, gf_hbm, sum_hbm, exp_hbm, qn_hbm, qf_hbm, kn_hbm, kf_hbm, vn_hbm, vf_hbm, *refs):
    before, (dq_ref, dk_ref, dv_ref) = refs[: 0 if first else 2], refs[-10:-7]
    grads, sums, held, queries, keys, values, sems = refs[-7:]
    seqs, heads, rows = sums.shape[0], sums.shape[1], sums.shape[2] // 2
    half_rows = keys.shape[1] // 2
    near, far = pl.ds(0, rows), pl.ds(rows, rows)
    near_keys, far_keys = pl.ds(0, half_rows), pl.ds(half_rows, half_rows)

    def copies(s):
        pairs = [
            (gn_hbm.at[blocks[0], s], grads.at[s, near]),
            (gf_hbm.at[blocks[1], s], grads.at[s, far]),
            (sum_hbm.at[s], sums.at[s]),
            (vn_hbm.at[s], values.at[s, near_keys]),
            (vf_hbm.at[s], values.at[s, far_keys]),
            (exp_hbm.at[s, 0], held.at[s, 0]),
            (kn_hbm.at[s], keys.at[s, near_keys]),
            (kf_hbm.at[s], keys.at[s, far_keys]),
            (qn_hbm.at[s, pl.ds(part * rows, rows)], queries.at[s, near]),
            (qf_hbm.at[s, pl.ds(part * rows, rows)], queries.at[s, far]),
        ] + [(exp_hbm.at[s, head], held.at[s, head]) for head in range(1, heads)]
        return [pltpu.make_async_copy(a, b, sems.at[s, i]) for i, (a, b) in enumerate(pairs)]

    loads = [copies(s) for s in range(seqs)]
    for s in range(seqs):
        for copy in loads[s]:
            copy.start()

    def prepare(unit):
        s, head = divmod(unit, heads)
        if head == 0:
            for copy in loads[s][:5]:
                copy.wait()
        lanes = slice(head * HEAD, (head + 1) * HEAD)
        kept = sums[s, head].astype(F32)
        inverse = kept[:, HEAD : HEAD + 1] + kept[:, 3 * HEAD // 2 : 3 * HEAD // 2 + 1]
        grad = (grads[s, :, lanes].astype(F32) * inverse).astype(BF16)
        inner = jnp.sum(grad.astype(F32) * kept[:, :HEAD], axis=1, keepdims=True)
        return grad, inner, mm(grad, values[s, :, lanes], NT)

    grad_q = []
    ready = prepare(0)
    for unit in range(seqs * heads):
        s, head = divmod(unit, heads)
        later = prepare(unit + 1) if unit + 1 < seqs * heads else None
        for copy in loads[s][5:10] if head == 0 else loads[s][9 + head : 10 + head]:
            copy.wait()
        lanes = slice(head * HEAD, (head + 1) * HEAD)
        grad, inner, grad_power = ready
        power = held[s, head]
        grad_scores = power * (grad_power - inner).astype(BF16)
        grad_q.append(mm(grad_scores, keys[s, :, lanes]) * (1.0 / math.sqrt(HEAD)))
        grad_k = mm(queries[s, :, lanes], grad_scores, TN) * (1.0 / LOG2E)
        grad_v = mm(grad, power, TN)
        if not first:
            grad_k = grad_k + before[0][s, lanes].astype(F32)
            grad_v = grad_v + before[1][s, lanes].astype(F32)
        dk_ref[s, lanes] = grad_k.astype(BF16)
        dv_ref[s, lanes] = grad_v.astype(BF16)
        if head == heads - 1:
            whole = jnp.concatenate(grad_q, axis=1).astype(BF16)
            dq_ref[0, s] = whole[:rows]
            dq_ref[1, s] = whole[rows:]
            grad_q = []
        ready = later


def attend_back(part, grads, sums, powers, queries, keys, values, before=()):
    seqs, half_rows, head_width = queries[0].shape
    rows = half_rows // 2
    heads = head_width // HEAD
    (near_grad, near_block), (far_grad, far_block) = grads
    return call(
        lambda *refs: attend_back_kernel(part, (near_block, far_block), not before, *refs),
        "attend_back",
        [ANY] * 10 + [VMEM] * len(before),
        (near_grad, far_grad, sums, powers, *queries, *keys, *values, *before),
        [VMEM] * 3,
        [like((2, seqs, rows, head_width), BF16)] + [like((seqs, head_width, 2 * half_rows), BF16)] * 2,
        (1,),
        None,
        [
            pltpu.VMEM((seqs, 2 * rows, head_width), BF16),
            pltpu.VMEM((seqs, heads, 2 * rows, 2 * HEAD), BF16),
            pltpu.VMEM((seqs, heads, 2 * rows, 2 * half_rows), BF16),
            pltpu.VMEM((seqs, 2 * rows, head_width), BF16),
            pltpu.VMEM((seqs, 2 * half_rows, head_width), BF16),
            pltpu.VMEM((seqs, 2 * half_rows, head_width), BF16),
            pltpu.SemaphoreType.DMA((seqs, 16)),
        ],
        pins=tuple(range(2, 10)),
    )


def normalize(values):
    centre = values - jnp.mean(values, axis=-1, keepdims=True)
    scale = lax.rsqrt(jnp.mean(centre * centre, axis=-1, keepdims=True) + 1e-05)
    return centre * scale, scale


def normalize_back(grad, unit, scale):
    return scale * (
        grad
        - jnp.mean(grad, axis=-1, keepdims=True)
        - unit * jnp.mean(grad * unit, axis=-1, keepdims=True)
    )


def gelu_parts(values):
    size = jnp.abs(values)
    bell = jnp.exp2(values * values * (-0.5 * LOG2E))
    t = 1.0 / (1.0 + (0.3275911 * math.sqrt(0.5)) * size)
    tail = 0.5 * 1.061405429
    for factor in (-1.453152027, 1.421413741, -0.284496736, 0.254829592):
        tail = tail * t + 0.5 * factor
    tail = tail * t * bell
    below = jnp.where(values < 0.0, tail, 1.0 - tail)
    return values * below, below + values * (bell * (1.0 / math.sqrt(2.0 * math.pi)))


def staged(count, stages):
    depth = len(stages)

    def turn(now, parity, first, last):
        for k in range(first, last):
            stages[k](now - k, (parity - k) % 2)

    for now in range(depth - 1):
        turn(now, now % 2, 0, now + 1)

    def body(step, carry):
        for p in range(2):
            turn(2 * step + p + depth - 1, (p + depth - 1) % 2, 0, depth)
        return carry

    full = count - depth + 1
    lax.fori_loop(0, full // 2, body, 0)
    for now in range(count - full % 2, count):
        turn(now, now % 2, 0, depth)
    for now in range(count, count + depth - 1):
        turn(now, now % 2, now - count + 1, depth)


def rows_kernel(order_ref, near_ref, tv_ref, cot_ref, steps_ref, table_ref, bo_ref, g1_ref, s1_ref, bd_ref, g2_ref, s2_ref, bu0, bu1, bu2, bu3, *refs):
    atts, wos, wus, wds = refs[:4], refs[4:8], refs[8:12], refs[12:16]
    part_ref = refs[16]
    out_o, gpre_o, own_o, core_o, back_own_o, back_h_o, back_y_o = refs[17:24]
    wo, wu, wd, slopes, held_a, held_b, now_a, now_b, unit_one, scale_one, total = refs[24:35]
    out_v, gpre_v, low_v, act_v, mix_v, grad_v, branch_v, back_v = refs[35:43]
    bias_up = refs[43]
    sems, out_sems = refs[44:46]
    held, now = (held_a, held_b), (now_a, now_b)
    seqs, rows, width = cot_ref.shape
    loads = [
        [pltpu.make_async_copy(s, target.at[j], sems.at[group, j]) for j, s in enumerate(sources)]
        for group, (sources, target) in enumerate(((wos, wo), (wus, wu), (wds, wd)))
    ]
    for j in range(4):
        loads[0][j].start()
    for j in range(4):
        loads[1][j].start()
        loads[2][j].start()
    for j, ref in enumerate((bu0, bu1, bu2, bu3)):
        bias_up[j : j + 1] = ref[...]
    stores = []

    def store(source, target):
        copy = pltpu.make_async_copy(source, target, out_sems.at[len(stores)])
        copy.start()
        stores.append(copy)

    for copy in loads[0]:
        copy.wait()
    for s in range(seqs):
        here = pl.ds(s * rows, rows)
        pre = near_ref[s].astype(F32) + tv_ref[s : s + 1] + bo_ref[...]
        for j in range(4):
            pre = pre + mm(atts[j][0, s], wo[j])
        unit, scale = normalize(pre)
        unit_one[here] = unit
        scale_one[here] = scale
        normed = unit * g1_ref[...] + s1_ref[...]
        low_v[here] = normed.astype(BF16)
        total[here] = normed + bd_ref[...]
    store(low_v, own_o.at[5])
    store(low_v, core_o.at[5])
    for copy in loads[1] + loads[2]:
        copy.wait()

    def where(i):
        return i // seqs, pl.ds(lax.rem(i, seqs) * rows, rows)

    def upward(i, p):
        j, here = where(i)
        held[p][...] = mm(low_v[here], wu[j]) + bias_up[pl.ds(j, 1)]

    def gelu(i, p):
        j, here = where(i)
        act, slope = gelu_parts(held[p][...])
        act = act.astype(BF16)
        now[p][...] = act
        act_v[j, here] = act
        slopes[j, here] = slope.astype(BF16)

    def downward(i, p):
        j, here = where(i)
        total[here] += mm(now[p][...], wd[j])

    staged(4 * seqs, (upward, gelu, downward))
    store(act_v.at[2:4], core_o.at[0:2])
    store(act_v.at[0:2], own_o.at[0:2])

    sums = [0.0] * 3
    for s in range(seqs):
        here = pl.ds(s * rows, rows)
        unit, scale = normalize(total[here])
        out_v[s] = (unit * g2_ref[...] + s2_ref[...]).astype(BF16)
        grad = cot_ref[s].astype(F32) * table_ref[steps_ref[s]]
        sums[1] += jnp.sum(grad * unit, axis=0, keepdims=True)
        sums[2] += jnp.sum(grad, axis=0, keepdims=True)
        grad = normalize_back(grad * g2_ref[...], unit, scale)
        mixed = grad.astype(BF16)
        mix_v[here] = mixed
        total[here] = grad
        sums[0] += jnp.sum(mixed.astype(F32), axis=0, keepdims=True)
    store(out_v, out_o)
    store(mix_v, core_o.at[4])
    store(mix_v, own_o.at[4])
    part_ref[3:6] = jnp.concatenate(sums)
    part_ref[8:16] = jnp.zeros((8, width), F32)

    def back_down(i, p):
        j, here = where(i)
        held[p][...] = mm(mix_v[here], wd[j], NT)

    def back_gelu(i, p):
        j, here = where(i)
        grad = (held[p][...] * slopes[j, here].astype(F32)).astype(BF16)
        now[p][...] = grad
        grad_v[j, here] = grad
        part_ref[pl.ds(8 + j, 1)] += jnp.sum(grad.astype(F32), axis=0, keepdims=True)

    def back_up(i, p):
        j, here = where(i)
        total[here] += mm(now[p][...], wu[j], NT)

    staged(4 * seqs, (back_down, back_gelu, back_up))
    store(grad_v.at[2:4], core_o.at[2:4])
    store(grad_v.at[0:2], own_o.at[2:4])
    sums = [0.0] * 3
    for s in range(seqs):
        here = pl.ds(s * rows, rows)
        unit, grad = unit_one[here], total[here]
        sums[1] += jnp.sum(grad * unit, axis=0, keepdims=True)
        sums[2] += jnp.sum(grad, axis=0, keepdims=True)
        grad_pre = normalize_back(grad * g1_ref[...], unit, scale_one[here])
        gpre_v[here] = grad_pre
        branch = grad_pre.astype(BF16)
        branch_v[here] = branch
        sums[0] += jnp.sum(branch.astype(F32), axis=0, keepdims=True)
        part_ref[6 + s : 7 + s] = jnp.sum(grad_pre, axis=0, keepdims=True)
        for j in range(4):
            back_v[j, s] = mm(branch, wo[j], NT).astype(BF16)
    store(back_v.at[1], back_y_o.at[0])
    store(back_v.at[3], back_y_o.at[1])
    store(back_v.at[2], back_h_o.at[0])
    store(back_v.at[0], back_own_o.at[0])
    store(branch_v, core_o.at[6])
    store(branch_v, own_o.at[6])
    store(gpre_v, gpre_o)
    part_ref[0:3] = jnp.concatenate(sums)
    for copy in stores:
        copy.wait()


def rows_part(inputs, time_vec, cotangent, timesteps, importance, vectors, bias_up, atts, wos, wus, wds, tensor):
    seqs, rows, width = cotangent.shape
    flat, hidden, head_width = seqs * rows, wus[0].shape[1], wos[0].shape[0]
    kept = [
        like((seqs, rows, width), BF16),
        like((flat, width), F32),
        pltpu.HBM((7, flat, hidden), BF16),
        pltpu.HBM((7, flat, hidden), BF16),
        pltpu.HBM((1, seqs, rows, head_width), BF16),
        pltpu.HBM((1, seqs, rows, head_width), BF16),
        pltpu.HBM((2, seqs, rows, head_width), BF16),
    ]
    return call(
        rows_kernel,
        "rows_part",
        [pl.BlockSpec((seqs, rows, width), lambda i, t: (0, t[0], 0)), VMEM, VMEM, SMEM, SMEM]
        + [VMEM] * 6
        + [VMEM] * 4
        + [pl.BlockSpec((1, seqs, rows, head_width), lambda i, t, b=b: (b, 0, 0, 0)) for _, b in atts]
        + [HBM] * 12,
        (
            inputs,
            time_vec,
            cotangent,
            timesteps,
            importance,
            *[v[None] for v in vectors],
            *[v[None] for v in bias_up],
            *[a for a, _ in atts],
            *wos,
            *wus,
            *wds,
        ),
        [VMEM] + [HBM] * len(kept),
        [like((16, width), F32)] + kept,
        (1,),
        [tensor],
        [
            pltpu.VMEM((4,) + wos[0].shape, BF16),
            pltpu.VMEM((4,) + wus[0].shape, BF16),
            pltpu.VMEM((4,) + wds[0].shape, BF16),
            pltpu.VMEM((4, flat, hidden), BF16),
            pltpu.VMEM((rows, hidden), F32),
            pltpu.VMEM((rows, hidden), F32),
            pltpu.VMEM((rows, hidden), BF16),
            pltpu.VMEM((rows, hidden), BF16),
            pltpu.VMEM((flat, width), F32),
            pltpu.VMEM((flat, 1), F32),
            pltpu.VMEM((flat, width), F32),
            pltpu.VMEM((seqs, rows, width), BF16),
            pltpu.VMEM((flat, width), F32),
            pltpu.VMEM((flat, width), BF16),
            pltpu.VMEM((4, flat, hidden), BF16),
            pltpu.VMEM((flat, width), BF16),
            pltpu.VMEM((4, flat, hidden), BF16),
            pltpu.VMEM((flat, width), BF16),
            pltpu.VMEM((4, seqs, rows, head_width), BF16),
            pltpu.VMEM((4, hidden), F32),
            pltpu.SemaphoreType.DMA((3, 4)),
            pltpu.SemaphoreType.DMA((20,)),
        ],
        pins=tuple(range(19, 30)),
    )


def weight_grad_kernel(sides, place_ref, own_ref, far_ref, send_ref, keep_ref, left, right, out, sems, out_sems):
    _, rows, width = own_ref.shape
    step = width // 2
    y_first, mine, tensor = place_ref[0], place_ref[1], place_ref[2]
    loads = {}
    for chunk in range(2):
        for number, (target, (first, chunks)) in enumerate(zip((right, left), reversed(sides))):
            if chunk < target.shape[0]:
                loads[number, chunk] = [
                    pltpu.make_async_copy(
                        ref.at[first + chunk], target.at[chunk, pl.ds(source * rows, rows)], sems.at[number, chunk, source]
                    )
                    for source, ref in enumerate((own_ref, far_ref))
                ]
                for copy in loads[number, chunk]:
                    copy.start()
    for chunk in range(2):
        for number in range(2):
            for copy in loads.get((number, chunk), ()):
                copy.wait()
        for half in range(2):
            lanes = slice(half * step, (half + 1) * step)
            spot = 2 * chunk + half
            out[spot] = mm(left[min(chunk, left.shape[0] - 1), :, lanes], right[min(chunk, right.shape[0] - 1)], TN).astype(BF16)
            tens = tensor ^ chunk
            outer = jnp.where(y_first == 1, tens, half)
            inside = jnp.where(y_first == 1, half, tens)

            @pl.when(outer != mine)
            def _():
                pltpu.make_async_copy(out.at[spot], send_ref.at[pl.ds(inside * step, step)], out_sems.at[spot]).start()

            @pl.when(outer == mine)
            def _():
                pltpu.make_async_copy(out.at[spot], keep_ref.at[pl.ds(inside * step, step)], out_sems.at[spot]).start()

    for spot in range(4):
        pltpu.make_async_copy(out.at[spot], send_ref.at[pl.ds(0, step)], out_sems.at[spot]).wait()


def weight_grad(own, far, left, right, y_first, first):
    _, rows, width = own.shape
    step = width // 2
    return call(
        lambda *refs: weight_grad_kernel((left, right), *refs),
        "weight_grad",
        [ANY, ANY],
        (own, far),
        [ANY, ANY],
        [pltpu.HBM((2 * step, width), BF16)] * 2,
        (1,),
        [y_first, first, lax.axis_index("tensor")],
        [
            pltpu.VMEM((1 + left[1], 2 * rows, width), BF16),
            pltpu.VMEM((1 + right[1], 2 * rows, width), BF16),
            pltpu.VMEM((4, step, width), BF16),
            pltpu.SemaphoreType.DMA((2, 2, 2)),
            pltpu.SemaphoreType.DMA((4,)),
        ],
        pins=(0, 1),
    )


def out_grad_kernel(own_ref, far_ref, other_ref, other_far_ref, right_ref, right_far_ref, own_out, other_out):
    count = right_ref.shape[1]

    def product(near, far):
        return (
            mm(near[...].reshape(count, -1), right_ref[0], TN)
            + mm(far[...].reshape(count, -1), right_far_ref[0], TN)
        ).astype(BF16)

    other_out[...] = product(other_ref, other_far_ref)
    own_out[...] = product(own_ref, far_ref)


def out_grad(sides, own, far, place_of):
    _, rows, width = own.shape
    head_width = sides[0][0].shape[3]
    shape = (head_width, width)
    right = pl.BlockSpec((1, rows, width), lambda i: (place_of, 0, 0))
    return call(
        out_grad_kernel,
        "out_grad",
        [pl.BlockSpec((1,) + a.shape[1:], lambda i, b=b: (b, 0, 0, 0)) for a, b in sides] + [right, right],
        (*[a for a, _ in sides], own, far),
        [VMEM, VMEM],
        [like(shape, BF16)] * 2,
        (1,),
        pins=tuple(range(6)),
    )


SHARED = 16


def padded(count):
    return -(-(SHARED + 2 * count) // 16) * 16


def put_vectors(ref, first, value):
    rows = value.shape[0]
    high = value.astype(BF16)
    low = (value - high.astype(F32)).astype(BF16)
    ref[first : first + rows] = high
    ref[first + rows : first + 2 * rows] = low
    return high.astype(F32) + low.astype(F32)


def get_vectors(ref, first, rows):
    return ref[first : first + rows].astype(F32) + ref[first + rows : first + 2 * rows].astype(F32)


def qkv_grad_kernel(place_ref, dqs_b, dqs_a, dk_ref, dv_ref, near_ref, far_ref, w_ref, out_ref, got_ref, parts_ref, feat_ref, send_ref, keep_ref, vec_ref):
    seqs, half_rows, _ = near_ref.shape
    rows = half_rows // 2
    width = dk_ref.shape[1]
    blocks = ((dqs_b, 0, near_ref, 0), (dqs_a, 0, near_ref, rows), (dqs_b, 1, far_ref, 0), (dqs_a, 1, far_ref, rows))

    def put(half, first, value):
        @pl.when(place_ref[0] == half)
        def _():
            keep_ref[first : first + width] = value

        @pl.when(place_ref[0] != half)
        def _():
            send_ref[first : first + width] = value

    for c, ref in ((1, dk_ref), (2, dv_ref)):
        grad = sum(
            mm(ref[s, :, :half_rows], near_ref[s]) + mm(ref[s, :, half_rows:], far_ref[s])
            for s in range(seqs)
        )
        put(1, (c - 1) * width, grad.astype(BF16))
    grad_q = sum(
        mm(dq[b, s], low[s, first : first + rows], TN)
        for dq, b, low, first in blocks
        for s in range(seqs)
    )
    put(0, 0, (out_ref[...].astype(F32) + got_ref[...].astype(F32)).astype(BF16))
    put(0, width, grad_q.astype(BF16))
    vec_ref[...] = jnp.zeros_like(vec_ref)
    vec_ref[0:6] = parts_ref[0:6]
    vec_ref[6:10] = parts_ref[8:12]
    ones = jnp.ones((8, rows), BF16)
    many = jnp.ones((8, 2 * half_rows), BF16)
    bias = [0.0] * 3
    for s in range(seqs):
        sums = [
            sum(mm(ones, dq[b, s]) for dq, b, _, _ in blocks),
            mm(many, dk_ref[s], NT),
            mm(many, dv_ref[s], NT),
        ]
        back = 0.0
        for c in range(3):
            bias[c] = bias[c] + sums[c][0:1]
            high = sums[c].astype(BF16)
            rest = (sums[c] - high.astype(F32)).astype(BF16)
            back = back + mm(high, w_ref[c]) + mm(rest, w_ref[c])
        vec_ref[SHARED + s : SHARED + s + 1] = parts_ref[6 + s : 7 + s] + back[0:1]
    empty = jnp.zeros((1, vec_ref.shape[1] - 2 * width), F32)
    vec_ref[10:11] = jnp.concatenate([bias[0], bias[2], empty], axis=1)
    vec_ref[SHARED + seqs : SHARED + 2 * seqs] = feat_ref[...]
    vec_ref[...] = put_vectors(send_ref, 2 * width, vec_ref[...])


def qkv_grad(dqs_b, dqs_a, dk, dv, near, far, weights, out_own, out_got, parts, feats, mine):
    seqs, _, width = near.shape
    head_width = weights.shape[1]
    return call(
        qkv_grad_kernel,
        "qkv_grad",
        [VMEM] * 11,
        (dqs_b, dqs_a, dk, dv, near, far, weights, out_own, out_got, parts, feats),
        [VMEM] * 3,
        [
            like((2 * head_width + 2 * padded(seqs), width), BF16),
            pltpu.HBM((2 * head_width, width), BF16),
            like((padded(seqs), width), F32),
        ],
        (1,),
        [mine],
    )


def input_grad_kernel(dqs_b, dqs_a, dk_ref, dv_ref, w_ref, own_ref, y_ref, far_ref):
    seqs, width, columns = dk_ref.shape
    half_rows = columns // 2
    rows = half_rows // 2
    for half in (1, 0):
        for s in range(seqs):
            lanes = slice(half * half_rows, (half + 1) * half_rows)
            part = mm(dk_ref[s, :, lanes], w_ref[1], TN) + mm(dv_ref[s, :, lanes], w_ref[2], TN)
            own = part[:rows] + mm(dqs_b[half, s], w_ref[0])
            other = part[rows:] + mm(dqs_a[half, s], w_ref[0])
            if half == 0:
                own_ref[s] = own
                y_ref[s] = other.astype(BF16)
            else:
                far_ref[0, s] = own.astype(BF16)
                far_ref[1, s] = other.astype(BF16)


def input_grad(dqs_b, dqs_a, dk, dv, weights):
    seqs, head_width, columns = dk.shape
    width, rows = weights.shape[2], columns // 4
    return call(
        input_grad_kernel,
        "input_grad",
        [VMEM] * 5,
        (dqs_b, dqs_a, dk, dv, weights),
        [VMEM] * 3,
        [
            like((seqs, rows, width), F32),
            like((seqs, rows, width), BF16),
            like((2, seqs, rows, width), BF16),
        ],
    )


def input_cross_kernel(y_ref, got_ref, out_ref):
    out_ref[...] = (y_ref[...].astype(F32) + got_ref[0].astype(F32)).astype(BF16)


def input_cross(part, got):
    seqs, rows, width = part.shape
    block = pl.BlockSpec((1, rows, width), lambda s: (s, 0, 0))
    return call(
        input_cross_kernel,
        "input_cross",
        [block, pl.BlockSpec((1, 1, rows, width), lambda s: (1, s, 0, 0))],
        (part, got),
        block,
        like(part.shape, BF16),
        (seqs,),
    )


def input_total_kernel(pre_ref, own_ref, got_ref, cross_ref, out_ref):
    out_ref[0] = pre_ref[...] + (own_ref[0] + got_ref[0, 0].astype(F32)) + cross_ref[0].astype(F32)


def input_total(pre, own, got, cross):
    seqs, rows, width = own.shape
    block = pl.BlockSpec((1, rows, width), lambda s: (s, 0, 0))
    return call(
        input_total_kernel,
        "input_total",
        [pl.BlockSpec((rows, width), lambda s: (s, 0)), block, pl.BlockSpec((1, 1, rows, width), lambda s: (0, s, 0, 0)), block],
        (pre, own, got, cross),
        block,
        pltpu.HBM(own.shape, F32),
        (seqs,),
    )


def sinusoid(step_ids, feature_count):
    halfway = feature_count // 2
    frequency = jnp.exp(-math.log(10000.0) * jnp.arange(halfway, dtype=F32) / halfway)
    angles = step_ids.astype(F32)[:, None] * frequency[None, :]
    return jnp.concatenate([jnp.cos(angles), jnp.sin(angles)], axis=1)


def halved(value, mine):
    rows = value.shape[0] // 2
    return (
        lax.dynamic_slice_in_dim(value, (1 - mine) * rows, rows, 0),
        lax.dynamic_slice_in_dim(value, mine * rows, rows, 0),
    )


def split_kernel(mine_ref, keep_send, got_send, keep_keep, got_keep, send_ref, keep_ref):
    send_ref[...] = (keep_send[...].astype(F32) + got_send[...].astype(F32)).astype(BF16)
    keep_ref[...] = (keep_keep[...].astype(F32) + got_keep[...].astype(F32)).astype(BF16)


def add_split(keep, got, mine):
    rows, width = keep.shape
    blocks = 2 if rows % 64 == 0 else 1
    step = rows // 2 // blocks
    send = pl.BlockSpec((step, width), lambda i, m: ((1 - m[0]) * blocks + i, 0))
    stay = pl.BlockSpec((step, width), lambda i, m: (m[0] * blocks + i, 0))
    out = pl.BlockSpec((step, width), lambda i, m: (i, 0))
    if step % 8:
        total = (keep.astype(F32) + got.astype(F32)).astype(BF16)
        return halved(total, mine)
    return call(
        split_kernel,
        "add_split",
        [send, send, stay, stay],
        (keep, got, keep, got),
        [out, out],
        [like((rows // 2, width), BF16)] * 2,
        (blocks,),
        [mine],
    )


def add_kernel(left, right, out_ref):
    out_ref[...] = (left[...].astype(F32) + right[...].astype(F32)).astype(BF16)


def add(left, right):
    return call(add_kernel, "add", [VMEM, VMEM], (left, right), VMEM, like(left.shape, BF16))


def join_kernel(mine_ref, value_ref, got_ref, out_ref):
    @pl.when(pl.program_id(0) == mine_ref[0])
    def _():
        out_ref[...] = value_ref[...].astype(out_ref.dtype)

    @pl.when(pl.program_id(0) != mine_ref[0])
    def _():
        out_ref[...] = got_ref[...].astype(out_ref.dtype)


def join(value, got, mine, dtype=BF16):
    rows, width = value.shape
    if rows % 8:
        out = jnp.where(mine == 0, jnp.concatenate([value, got]), jnp.concatenate([got, value]))
        return out.astype(dtype)
    whole = pl.BlockSpec((rows, width), lambda i, m: (0, 0))
    return call(
        join_kernel,
        "join",
        [whole, whole],
        (value, got),
        pl.BlockSpec((rows, width), lambda i, m: (i, 0)),
        (pltpu.HBM if dtype == F32 else like)((2 * rows, width), dtype),
        (2,),
        [mine],
    )


def joined_vectors(count, mine, value, got, inner=None):
    pieces = [value[:SHARED] + got[:SHARED]]
    for first in (SHARED, SHARED + count):
        own, other = value[first : first + count], got[first : first + count]
        low, high = jnp.where(mine == 0, own, other), jnp.where(mine == 0, other, own)
        if inner is not None:
            middle = count // 2
            a, b = low[middle:], high[:middle]
            low = jnp.concatenate([low[:middle], jnp.where(inner == 1, b, a)])
            high = jnp.concatenate([jnp.where(inner == 1, a, b), high[middle:]])
        pieces += [low, high]
    rest = padded(2 * count) - SHARED - 4 * count
    return jnp.concatenate(pieces + [jnp.zeros((rest, value.shape[1]), F32)] * (rest > 0))


def small_join_kernel(mine_ref, value_ref, got_ref, out_ref, qkv_ref):
    first = mine_ref[0] == 0
    low = jnp.where(first, value_ref[...], got_ref[...]).astype(F32)
    high = jnp.where(first, got_ref[...], value_ref[...]).astype(F32)
    count = out_ref.shape[0]
    out_ref[...] = low[:count]
    qkv_ref[:count] = low[count:]
    qkv_ref[count:] = high


def joined_vectors(count, mine, value, got, inner=None):
    pieces = [value[:SHARED] + got[:SHARED]]
    for first in (SHARED, SHARED + count):
        own, other = value[first : first + count], got[first : first + count]
        low, high = jnp.where(mine == 0, own, other), jnp.where(mine == 0, other, own)
        if inner is not None:
            middle = count // 2
            a, b = low[middle:], high[:middle]
            low = jnp.concatenate([low[:middle], jnp.where(inner == 1, b, a)])
            high = jnp.concatenate([jnp.where(inner == 1, a, b), high[middle:]])
        pieces += [low, high]
    rest = padded(2 * count) - SHARED - 4 * count
    return jnp.concatenate(pieces + [jnp.zeros((rest, value.shape[1]), F32)] * (rest > 0))


def small_join_kernel(mine_ref, value_ref, got_ref, out_ref, qkv_ref):
    first = mine_ref[0] == 0
    low = jnp.where(first, value_ref[...], got_ref[...]).astype(F32)
    high = jnp.where(first, got_ref[...], value_ref[...]).astype(F32)
    count = out_ref.shape[0]
    out_ref[...] = low[:count]
    qkv_ref[:count] = low[count:]
    qkv_ref[count:] = high


def small_join(value, got, mine):
    rows, width = value.shape
    return call(
        small_join_kernel,
        "small_join",
        [VMEM, VMEM],
        (value, got),
        [VMEM, VMEM],
        [like((rows // 2, width), F32), like((rows // 2 * 3, width), F32)],
        (1,),
        [mine],
    )


def vector_kernel(count, mine_ref, value_ref, got_ref, out_ref):
    out_ref[...] = joined_vectors(count, mine_ref[0], value_ref[...], got_ref[...])


def vector_step(value, got, mine, count):
    return call(
        lambda *refs: vector_kernel(count, *refs),
        "vector_step",
        [VMEM, VMEM],
        (value, got),
        VMEM,
        like((padded(2 * count), value.shape[1]), F32),
        (1,),
        [mine],
    )


def small_kernel(count, last, mine_ref, keep_ref, got_ref, vec_ref, *outs):
    rows = keep_ref.shape[0]
    place_before, mine = mine_ref[0], mine_ref[1]
    vectors = joined_vectors(
        count, place_before, vec_ref[...], get_vectors(got_ref, rows, vec_ref.shape[0]), mine_ref[2] if last else None
    )

    def total(first, size):
        here = pl.ds(pl.multiple_of(first, 16), size)
        return (keep_ref[here].astype(F32) + got_ref[here].astype(F32)).astype(BF16)

    if last:
        outs[0][0:rows] = total(0, rows)
        outs[-1][...] = put_vectors(outs[0], rows, vectors)
    else:
        size = rows // 2
        outs[0][0:size] = total((1 - mine) * size, size)
        outs[-1][...] = put_vectors(outs[0], size, vectors)
        outs[1][...] = total(mine * size, size)


def small_step(keep, got, vectors, count, place_before, mine, last):
    rows, width = keep.shape
    after = padded(2 * count)
    size = rows if last else rows // 2
    out = call(
        lambda *refs: small_kernel(count, last, *refs),
        "small_step",
        [VMEM] * 3,
        (keep, got, vectors),
        [VMEM] * (2 if last else 3),
        [like((size + 2 * after, width), BF16)]
        + ([] if last else [like((size, width), BF16)])
        + [like((after, width), F32)],
        (1,),
        [place_before, mine, lax.axis_index("half")],
    )
    return (out[0], None, out[1]) if last else out


def small_end_kernel(count, mine_ref, value_ref, got_ref, vec_ref, out_ref, vec_out):
    rows = out_ref.shape[0]
    vec_out[...] = joined_vectors(count, mine_ref[0], vec_ref[...], get_vectors(got_ref, rows, vec_ref.shape[0]))
    out_ref[...] = (value_ref[0:rows].astype(F32) + got_ref[0:rows].astype(F32)).astype(BF16)


def small_end(value, got, vectors, count, mine):
    rows = value.shape[0] - 2 * vectors.shape[0]
    width = value.shape[1]
    return call(
        lambda *refs: small_end_kernel(count, *refs),
        "small_end",
        [VMEM] * 3,
        (value, got, vectors),
        [VMEM] * 2,
        [like((rows, width), BF16), like((padded(2 * count), width), F32)],
        (1,),
        [mine],
    )


def fold_kernel(first, second, chunks, value_ref, got_ref, out_ref):
    out_ref[...] = value_ref[...]
    out_ref[0:6] = value_ref[0:6] + got_ref[0:6]
    out_ref[6 : 6 + chunks] = value_ref[6 : 6 + chunks] + got_ref[6 + chunks : 6 + 2 * chunks]
    out_ref[first:second] = value_ref[first:second] + got_ref[first:second]


def fold(value, got, count, chunks):
    return call(
        lambda *refs: fold_kernel(SHARED, SHARED + count, chunks, *refs),
        "fold",
        [VMEM, VMEM],
        (value, got),
        VMEM,
        like(value.shape, F32),
    )


def quarters_kernel(spot_ref, up_ref, down_ref, up_out, down_out, sems):
    count = up_out.shape[0]
    here = pl.ds(pl.multiple_of(spot_ref[0] * count, 16), count)
    copies = [
        pltpu.make_async_copy(up_ref.at[here], up_out, sems.at[0]),
        pltpu.make_async_copy(down_ref.at[here], down_out, sems.at[1]),
    ]
    for copy in copies:
        copy.start()
    for copy in copies:
        copy.wait()


def quarters(up, down, spot):
    shape = (up.shape[0] // 4, up.shape[1])
    return call(
        quarters_kernel,
        "quarters",
        [ANY, ANY],
        (up, down),
        [ANY, ANY],
        [like(shape, BF16)] * 2,
        (1,),
        [spot],
        [pltpu.SemaphoreType.DMA((2,))],
    )


def per_device(
    inputs,
    cotangent,
    src_lengths,
    tgt_mask,
    timesteps,
    importance,
    w_qkv,
    b_qv,
    w_out,
    b_out,
    gain_one,
    shift_one,
    w_up,
    b_up,
    w_down,
    b_down,
    gain_two,
    shift_two,
    w_time1,
    time_bias1,
    w_time2,
    time_bias2,
):
    Order.token, Order.pinned = None, False
    half = lax.axis_index("half")
    tensor = lax.axis_index("tensor")
    seqs, half_rows, width = inputs.shape
    rows = half_rows // lax.axis_size("tensor")
    hidden = w_up.shape[1]
    head_width = w_qkv.shape[2]
    bits = lax.axis_size("dp").bit_length() - 1

    far = swap(inputs, "core")

    spread = [(0, 1), (1, 0)]

    up_quarter, down_quarter = quarters(w_up, w_down, 2 * place(*spread[1]) + place(*spread[0]))
    up_one = swap(up_quarter, "y")
    out_one = swap(w_out, "y")
    down_one = swap(down_quarter, "y")
    bias_one = swap(b_up, "y")
    up_core, down_core = hold(swap(w_up, "core"), swap(w_down, "core"))

    features = sinusoid(timesteps, w_time1.shape[0])
    time_sum = jnp.dot(features, w_time1, precision=HIGHEST) + time_bias1
    time_vec = jnp.dot(jax.nn.silu(time_sum), w_time2, precision=HIGHEST) + time_bias2

    feats = jnp.concatenate([time_sum, features], axis=1)
    feats = jnp.pad(feats, ((0, 0), (0, width - feats.shape[1])))

    def own_first(array):
        return jnp.concatenate(
            [
                lax.dynamic_slice_in_dim(array, tensor * rows, rows, 1),
                lax.dynamic_slice_in_dim(array, (1 - tensor) * rows, rows, 1),
            ],
            axis=1,
        )

    positions = jnp.arange(half_rows, dtype=jnp.int32)
    source_live = positions[None, :] < src_lengths[:, None]
    target_live = tgt_mask == 1
    near_live = own_first(jnp.where(half == 0, source_live, target_live))
    far_live = own_first(jnp.where(half == 0, target_live, source_live))
    allowed = jnp.concatenate([near_live, far_live], axis=1)
    mask = jnp.where(
        (jnp.arange(HEAD) == 0)[None, None, :] & ~allowed[:, :, None], MASKED, 0.0
    ).astype(BF16)

    w_turned = jnp.swapaxes(w_qkv, 1, 2)
    q_near, k_near, v_near, low_near = project(inputs, time_vec, w_turned, b_qv[0], b_qv[1], tensor, (feats, mask))
    far, bias_one = hold(far, bias_one)
    bias_core, bias_two = swap(b_up, "core"), swap(bias_one, "core")
    q_far, k_far, v_far, low_far = project(far, time_vec, w_turned, b_qv[0], b_qv[1], tensor)
    queries, keys, values = (q_near, q_far), (k_near, k_far), (v_near, v_far)

    up_one, bias_core, bias_two = hold(up_one, bias_core, bias_two)
    up_got = swap(up_one, *spread[0])
    att_y, sums_a, powers_a = attend(1, queries, keys, values, mask)
    got_y = swap(att_y, "y")
    (out_one,) = hold(out_one)
    out_core = swap(out_one, "core")
    up_one = join(up_one, up_got, place(*spread[0]))
    up_got = swap(up_one, *spread[1])
    down_one, out_core = hold(down_one, out_core)
    down_got = swap(down_one, *spread[0])
    att_own, sums_b, powers_b = attend(0, queries, keys, values, mask)
    got_h = swap(att_own, "core")
    down_one = join(down_one, down_got, place(*spread[0]))
    down_got = swap(down_one, *spread[1])
    got_y, got_h = hold(got_y, got_h)
    got_far, out_two = swap(got_y, "core"), swap(w_out, "core")
    up_one = join(up_one, up_got, place(*spread[1]))
    up_three = swap(up_one, "core")
    got_far, out_two, up_three = hold(got_far, out_two, up_three)
    down_one = join(down_one, down_got, place(*spread[1]))
    outs_w = [w_out, out_one, out_two, out_core]
    ups_w = [w_up, up_one, up_core, up_three]
    downs_w = [w_down, down_one, down_core, swap(down_one, "core")]
    ups_b = [b_up, bias_one, bias_core, bias_two]
    atts = ((att_own, 0), (got_y, 0), (got_h, 1), (got_far, 1))

    (
        parts,
        outputs,
        grad_pre,
        own,
        core,
        back_own,
        back_h,
        back_y,
    ) = rows_part(
        inputs,
        time_vec,
        cotangent,
        timesteps,
        importance,
        (b_out, gain_one, shift_one, b_down, gain_two, shift_two),
        ups_b,
        atts,
        outs_w,
        ups_w,
        downs_w,
        tensor,
    )
    back_h = swap(back_h, "core")
    back_y = swap(back_y, "y")
    back_h, core = hold(back_h, core)
    far_rows = swap(core, "core")

    down_steps = [(0, "y"), ("y", 0), (1,)]
    up_steps = [(0, 1), ("y",), (1, 0)]
    small_steps = [(0, 1), (1, 0)]
    dqs_b, dk, dv = attend_back(0, ((back_own, 0), (back_h, 0)), sums_b, powers_b, queries, keys, values)
    down_send, down_keep = weight_grad(own, far_rows, (0, True), (4, False), half, place(*down_steps[0]))
    down_got = swap(down_send, *down_steps[0])
    (back_y,) = hold(back_y)
    back_d = swap(back_y, "core")
    up_send, up_keep = weight_grad(own, far_rows, (5, False), (2, True), jnp.int32(0), place(*up_steps[0]))
    up_got = swap(up_send, *up_steps[0])
    out_own, out_other = out_grad(((att_own, 0), (att_own, 1), (got_y, 0), (got_y, 1)), own, far_rows, 6)
    out_got = swap(out_other, "y")
    def step(keep, got, steps, turn):
        send, keep = add_split(keep, got, place(*steps[turn]))
        return keep, swap(send, *steps[turn])

    def collect(value, got, dims, dtype=BF16):
        return join(value, got, place(*dims), dtype)

    down_keep, down_got = step(down_keep, down_got, down_steps, 1)
    dqs_a, dk, dv = attend_back(1, ((back_y, 0), (back_d, 1)), sums_a, powers_a, queries, keys, values, (dk, dv))
    down_keep, down_got = step(down_keep, down_got, down_steps, 2)
    small_send, small_keep, vectors = qkv_grad(
        dqs_b, dqs_a, dk, dv, low_near, low_far, w_turned, out_own, out_got, parts, feats, place(*small_steps[0])
    )
    small_got = swap(small_send, *small_steps[0])
    down = add(down_keep, down_got)
    down_got = swap(down, 2)
    up_keep, up_got = step(up_keep, up_got, up_steps, 1)
    dx_own, dx_y, dx_far = input_grad(dqs_b, dqs_a, dk, dv, w_turned)
    count = seqs
    small_send, small_keep, vectors = small_step(
        small_keep, small_got, vectors, count, place(*small_steps[0]), place(*small_steps[1]), False
    )
    small_got = swap(small_send, *small_steps[1])
    count *= 2
    down = add(down, down_got)
    down_steps, up_next = [(0,), (1,)], small_steps
    if bits == 3:
        down_got = swap(down, *down_steps[1])
    up_keep, up_got = step(up_keep, up_got, up_steps, 2)
    small_send, _, vectors = small_step(
        small_keep, small_got, vectors, count, place(*small_steps[1]), place(2), True
    )
    small_got = swap(small_send, 2)
    count *= 2
    if bits == 3:
        down = collect(down, down_got, down_steps[1])
        down_got = swap(down, *down_steps[0])
    up = add(up_keep, up_got)
    up_got = swap(up, 2)
    (dx_far,) = hold(dx_far)
    dx_got = swap(dx_far, "core")
    small, vectors = small_end(small_send, small_got, vectors, count, place(2))
    count *= 2
    if bits > 3:
        up = add(up, up_got)
        for bit in range(3, bits):
            down, up, small = (add(v, swap(v, bit)) for v in (down, up, small))
            vectors = vector_step(vectors, swap(vectors, bit), bit_of(bit), count)
            count *= 2
        down = collect(down, swap(down, *down_steps[1]), down_steps[1])
        down_got = swap(down, *down_steps[0])
    small_got = swap(small, *small_steps[1])
    vectors_got = swap(vectors, "core")
    dx_cross = swap(input_cross(dx_y, dx_got), "y")
    if bits == 3:
        up = add(up, up_got)
    up_got = swap(up, *up_next[1])
    small = collect(small, small_got, small_steps[1])
    small_got = swap(small, *small_steps[0])
    vectors = fold(vectors, vectors_got, count, 2)
    vectors_got = swap(vectors, "y")
    grad_w_down = collect(down, down_got, down_steps[0], F32)
    up = collect(up, up_got, up_next[1])
    up_got = swap(up, *up_next[0])
    grad_inputs = input_total(grad_pre, dx_own, dx_got, dx_cross)
    vectors = fold(vectors, vectors_got, count, 1)
    grad_w_out, qkv = small_join(small, small_got, place(*small_steps[0]))
    grad_w_qkv = jnp.swapaxes(qkv.reshape(3, head_width, width), 1, 2)
    grad_w_up = collect(up, up_got, up_next[0], F32)

    all_grad = vectors[SHARED : SHARED + count]
    all_sum = vectors[SHARED + count : SHARED + 2 * count, : time_sum.shape[1]]
    all_features = vectors[SHARED + count : SHARED + 2 * count, time_sum.shape[1] : time_sum.shape[1] + features.shape[1]]
    gate_of = jax.nn.sigmoid(all_sum)
    all_hidden = all_sum * gate_of
    grad_w_time2 = lax.dot_general(all_hidden, all_grad, TN, precision=HIGHEST)
    grad_hidden = lax.dot_general(all_grad, w_time2, NT, precision=HIGHEST)
    grad_hidden = grad_hidden * (gate_of * (1.0 + all_sum * (1.0 - gate_of)))
    grad_w_time1 = lax.dot_general(all_features, grad_hidden, TN, precision=HIGHEST)
    return (
        outputs,
        grad_inputs,
        grad_w_qkv,
        vectors[10, : 2 * head_width].reshape(2, head_width),
        grad_w_out,
        vectors[0],
        vectors[1],
        vectors[2],
        grad_w_up,
        vectors[6, :hidden],
        grad_w_down,
        vectors[3],
        vectors[4],
        vectors[5],
        grad_w_time1,
        jnp.sum(grad_hidden, axis=0),
        grad_w_time2,
        jnp.sum(all_grad, axis=0),
    )


def solution(mesh):
    in_specs = (
        P("dp", "half", None),
        P("dp", ("half", "tensor"), None),
        P("dp"),
        P("dp", None),
        P("dp"),
        P(),
        P(None, None, ("tensor", "half")),
        P(None, ("tensor", "half")),
        P(("tensor", "half"), None),
        P(),
        P(),
        P(),
        P(None, ("tensor", "half")),
        P(("tensor", "half")),
        P(("tensor", "half"), None),
        P(),
        P(),
        P(),
        P(),
        P(),
        P(),
        P(),
    )
    out_specs = (
        P("dp", ("half", "tensor"), None),
        P("dp", ("half", "tensor"), None),
        P(None, None, ("tensor", "half")),
        P(None, ("tensor", "half")),
        P(("tensor", "half"), None),
        P(),
        P(),
        P(),
        P(None, ("tensor", "half")),
        P(("tensor", "half")),
        P(("tensor", "half"), None),
        P(),
        P(),
        P(),
        P(),
        P(),
        P(),
        P(),
    )
    return jax.shard_map(
        per_device, mesh=mesh, in_specs=in_specs, out_specs=out_specs, check_vma=False
    )
```

```python
import math

import jax
import jax.numpy as jnp
from jax import lax
from jax.experimental import pallas as pl
from jax.experimental.pallas import tpu as pltpu
from jax.sharding import PartitionSpec as P

HEAD = 64
F32 = jnp.float32
BF16 = jnp.bfloat16
HIGHEST = lax.Precision.HIGHEST
LOG2E = math.log2(math.e)
MASKED = -1e9
MIB = 1024 * 1024
GRANTS = {"rows_part": 38, "attend": 24, "attend_back": 24, "qkv_grad": 14, "weight_grad": 14}
ANY = pl.BlockSpec(memory_space=pl.ANY)
HBM = pl.BlockSpec(memory_space=pltpu.HBM)

NT = (((1,), (1,)), ((), ()))
NN = (((1,), (0,)), ((), ()))
TN = (((0,), (0,)), ((), ()))


def mm(left, right, dims=NN):
    return lax.dot_general(left, right, dims, preferred_element_type=F32)


def bit_of(dim):
    if dim == "y":
        return lax.axis_index("tensor")
    if dim == "core":
        return lax.axis_index("half")
    return (lax.axis_index("dp") >> dim) & 1


def swap(value, *dims):
    axes = ("dp", "half", "tensor")
    sizes = [lax.axis_size(a) for a in axes]
    pairs = []
    for d in range(sizes[0]):
        for h in range(2):
            for t in range(2):
                dim = dims[h % len(dims)]
                if dim == "y":
                    to = (d, h, 1 - t)
                elif dim == "core":
                    to = (d, 1 - h, t)
                else:
                    to = (d ^ (1 << dim), h, t)
                pairs.append(((d * 2 + h) * 2 + t, (to[0] * 2 + to[1]) * 2 + to[2]))
    return lax.ppermute(value, axes, pairs)


def place(*dims):
    if len(dims) == 1:
        return bit_of(dims[0])
    return jnp.where(lax.axis_index("half") == 0, bit_of(dims[0]), bit_of(dims[1]))


class Order:
    token = None
    pinned = False


def call(kernel, name, in_specs, args, out_specs, out_shape, grid=(), scalars=None, scratch_shapes=(), aliases=None, after=(), pins=()):
    tokens = (() if Order.token is None else (Order.token,)) + tuple(after)
    if Order.pinned:
        tokens = (pltpu.with_memory_space_constraint(tokens[0], pltpu.HBM), *tokens[1:])
    first = len(in_specs) + (scalars is not None)

    def body(*refs):
        kernel(*refs[:first], *refs[first + len(tokens) :])

    in_specs = list(in_specs) + [ANY] * len(tokens)
    args = [pltpu.with_memory_space_constraint(a, pltpu.HBM) if i in pins else a for i, a in enumerate(args)]
    if scalars is None:
        rest = dict(grid=grid, in_specs=in_specs, out_specs=out_specs, scratch_shapes=scratch_shapes)
    else:
        rest = dict(
            grid_spec=pltpu.PrefetchScalarGridSpec(
                num_scalar_prefetch=1,
                grid=grid,
                in_specs=in_specs,
                out_specs=out_specs,
                scratch_shapes=scratch_shapes,
            )
        )
        args = (jnp.stack(scalars).astype(jnp.int32), *args)
    out = pl.pallas_call(
        body,
        out_shape=out_shape,
        compiler_params=pltpu.CompilerParams(vmem_limit_bytes=GRANTS.get(name, 12) * MIB),
        cost_estimate=cost(name),
        input_output_aliases=aliases or {},
        name=name,
        **rest,
    )(*args, *tokens)
    several = isinstance(out, (list, tuple))
    Order.token = out[0] if several else out
    Order.pinned = not isinstance(out_shape[0] if several else out_shape, jax.ShapeDtypeStruct)
    return out


def hold(*values):
    return call(
        lambda *refs: None,
        "hold",
        [ANY] * len(values),
        values,
        [ANY] * len(values),
        [like(v.shape, v.dtype) for v in values],
        aliases={i: i for i in range(len(values))},
    )


def like(shape, dtype):
    return jax.ShapeDtypeStruct(shape, dtype)


TIMES = {'project': 1.0, 'rows_part': 24, 'attend': 1.0, 'attend_back': 9, 'weight_grad': 6, 'out_grad': 2.4}


def cost(name):
    return pl.CostEstimate(flops=int(TIMES.get(name, 0) * 1.15e9), bytes_accessed=1024, transcendentals=0)


VMEM = pl.BlockSpec(memory_space=pltpu.VMEM)
SMEM = pl.BlockSpec(memory_space=pltpu.SMEM)


def project_kernel(order_ref, x_ref, tv_ref, w_ref, bq_ref, bv_ref, q_ref, k_ref, v_ref, low_ref):
    low = (x_ref[0].astype(F32) + tv_ref[0]).astype(BF16)
    low_ref[0] = low
    q_ref[0] = ((mm(low, w_ref[0], NT) + bq_ref[...]) * (LOG2E / math.sqrt(HEAD))).astype(BF16)
    k_ref[0] = mm(low, w_ref[1], NT).astype(BF16)
    v_ref[0] = (mm(low, w_ref[2], NT) + bv_ref[...]).astype(BF16)


def project(rows, time_vec, weights, bias_q, bias_v, tensor, after=()):
    seqs, count, width = rows.shape
    head_width = weights.shape[1]
    step = count // 2
    narrow = pl.BlockSpec((1, step, head_width), lambda s, i, t: (s, i, 0))
    bias = pl.BlockSpec((1, head_width), lambda s, i, t: (0, 0))
    return call(
        project_kernel,
        "project",
        [
            pl.BlockSpec((1, step, width), lambda s, i, t: (s, i ^ t[0], 0)),
            pl.BlockSpec((1, 1, width), lambda s, i, t: (s, 0, 0)),
            pl.BlockSpec(weights.shape, lambda s, i, t: (0, 0, 0)),
            bias,
            bias,
        ],
        (rows, time_vec[:, None, :], weights, bias_q[None], bias_v[None]),
        [narrow, narrow, narrow, pl.BlockSpec((1, step, width), lambda s, i, t: (s, i, 0))],
        [like((seqs, count, head_width), BF16)] * 3 + [pltpu.HBM(rows.shape, BF16)],
        (seqs, 2),
        [tensor],
        after=after,
        pins=(0, 2),
    )


def attend_kernel(heads, qn_ref, qf_ref, kn_ref, kf_ref, vn_ref, vf_ref, mask_ref, o_ref, sum_ref, exp_ref, held, sems):
    rows = qn_ref.shape[1]
    seq = pl.program_id(0)

    def store(s, head):
        return pltpu.make_async_copy(held.at[s, head], exp_ref.at[s, head], sems.at[s, head])

    keys = jnp.concatenate([kn_ref[0], kf_ref[0]], axis=0)
    values = jnp.concatenate([vn_ref[0], vf_ref[0]], axis=0)
    queries = jnp.concatenate([qn_ref[0], qf_ref[0]], axis=0)
    ones = jnp.ones((2 * rows, HEAD), BF16)
    many = jnp.ones((keys.shape[0], HEAD), BF16)

    def scores_of(head):
        lanes = slice(head * HEAD, (head + 1) * HEAD)
        return mm(
            jnp.concatenate([queries[:, lanes], ones], axis=1),
            jnp.concatenate([keys[:, lanes], mask_ref[0]], axis=1),
            NT,
        )

    outs = []
    scores = scores_of(0)
    for head in range(heads):
        later = scores_of(head + 1) if head + 1 < heads else None
        power = jnp.exp2(scores - jnp.max(scores, axis=1, keepdims=True)).astype(BF16)
        lanes = slice(head * HEAD, (head + 1) * HEAD)
        total = mm(power, jnp.concatenate([values[:, lanes], many], axis=1))
        held[seq, head] = power
        store(seq, head).start()
        inverse = 1.0 / total[:, HEAD:]
        out = (total[:, :HEAD] * inverse).astype(BF16)
        high = inverse.astype(BF16)
        rest = (inverse - high.astype(F32)).astype(BF16)
        sum_ref[0, head] = jnp.concatenate([out, high[:, : HEAD // 2], rest[:, HEAD // 2 :]], axis=1)
        outs.append(out)
        scores = later
    out = jnp.concatenate(outs, axis=1)
    o_ref[0, 0] = out[:rows]
    o_ref[1, 0] = out[rows:]

    @pl.when(seq == pl.num_programs(0) - 1)
    def _():
        for s in range(exp_ref.shape[0]):
            for head in range(heads):
                store(s, head).wait()


def attend(part, queries, keys, values, mask):
    seqs, half_rows, head_width = queries[0].shape
    rows = half_rows // 2
    heads = head_width // HEAD
    q_spec = pl.BlockSpec((1, rows, head_width), lambda s: (s, part, 0))
    k_spec = pl.BlockSpec((1, half_rows, head_width), lambda s: (s, 0, 0))
    return call(
        lambda *refs: attend_kernel(heads, *refs),
        "attend",
        [q_spec, q_spec, k_spec, k_spec, k_spec, k_spec]
        + [pl.BlockSpec((1, 2 * half_rows, HEAD), lambda s: (s, 0, 0))],
        (*queries, *keys, *values, mask),
        [
            pl.BlockSpec((2, 1, rows, head_width), lambda s: (0, s, 0, 0)),
            pl.BlockSpec((1, heads, 2 * rows, 2 * HEAD), lambda s: (s, 0, 0, 0)),
            HBM,
        ],
        [
            like((2, seqs, rows, head_width), BF16),
            pltpu.HBM((seqs, heads, 2 * rows, 2 * HEAD), BF16),
            pltpu.HBM((seqs, heads, 2 * rows, 2 * half_rows), BF16),
        ],
        (seqs,),
        None,
        [
            pltpu.VMEM((seqs, heads, 2 * rows, 2 * half_rows), BF16),
            pltpu.SemaphoreType.DMA((seqs, heads)),
        ],
    )


def attend_back_kernel(part, blocks, first, gn_hbm, gf_hbm, sum_hbm, exp_hbm, qn_hbm, qf_hbm, kn_hbm, kf_hbm, vn_hbm, vf_hbm, *refs):
    before, (dq_ref, dk_ref, dv_ref) = refs[: 0 if first else 2], refs[-10:-7]
    grads, sums, held, queries, keys, values, sems = refs[-7:]
    seqs, heads, rows = sums.shape[0], sums.shape[1], sums.shape[2] // 2
    half_rows = keys.shape[1] // 2
    near, far = pl.ds(0, rows), pl.ds(rows, rows)
    near_keys, far_keys = pl.ds(0, half_rows), pl.ds(half_rows, half_rows)

    def copies(s):
        pairs = [
            (gn_hbm.at[blocks[0], s], grads.at[s, near]),
            (gf_hbm.at[blocks[1], s], grads.at[s, far]),
            (sum_hbm.at[s], sums.at[s]),
            (vn_hbm.at[s], values.at[s, near_keys]),
            (vf_hbm.at[s], values.at[s, far_keys]),
            (exp_hbm.at[s, 0], held.at[s, 0]),
            (kn_hbm.at[s], keys.at[s, near_keys]),
            (kf_hbm.at[s], keys.at[s, far_keys]),
            (qn_hbm.at[s, pl.ds(part * rows, rows)], queries.at[s, near]),
            (qf_hbm.at[s, pl.ds(part * rows, rows)], queries.at[s, far]),
        ] + [(exp_hbm.at[s, head], held.at[s, head]) for head in range(1, heads)]
        return [pltpu.make_async_copy(a, b, sems.at[s, i]) for i, (a, b) in enumerate(pairs)]

    loads = [copies(s) for s in range(seqs)]
    for s in range(seqs):
        for copy in loads[s]:
            copy.start()

    def prepare(unit):
        s, head = divmod(unit, heads)
        if head == 0:
            for copy in loads[s][:5]:
                copy.wait()
        lanes = slice(head * HEAD, (head + 1) * HEAD)
        kept = sums[s, head].astype(F32)
        inverse = kept[:, HEAD : HEAD + 1] + kept[:, 3 * HEAD // 2 : 3 * HEAD // 2 + 1]
        grad = (grads[s, :, lanes].astype(F32) * inverse).astype(BF16)
        inner = jnp.sum(grad.astype(F32) * kept[:, :HEAD], axis=1, keepdims=True)
        return grad, inner, mm(grad, values[s, :, lanes], NT)

    grad_q = []
    ready = prepare(0)
    for unit in range(seqs * heads):
        s, head = divmod(unit, heads)
        later = prepare(unit + 1) if unit + 1 < seqs * heads else None
        for copy in loads[s][5:10] if head == 0 else loads[s][9 + head : 10 + head]:
            copy.wait()
        lanes = slice(head * HEAD, (head + 1) * HEAD)
        grad, inner, grad_power = ready
        power = held[s, head]
        grad_scores = power * (grad_power - inner).astype(BF16)
        grad_q.append(mm(grad_scores, keys[s, :, lanes]) * (1.0 / math.sqrt(HEAD)))
        grad_k = mm(queries[s, :, lanes], grad_scores, TN) * (1.0 / LOG2E)
        grad_v = mm(grad, power, TN)
        if not first:
            grad_k = grad_k + before[0][s, lanes].astype(F32)
            grad_v = grad_v + before[1][s, lanes].astype(F32)
        dk_ref[s, lanes] = grad_k.astype(BF16)
        dv_ref[s, lanes] = grad_v.astype(BF16)
        if head == heads - 1:
            whole = jnp.concatenate(grad_q, axis=1).astype(BF16)
            dq_ref[0, s] = whole[:rows]
            dq_ref[1, s] = whole[rows:]
            grad_q = []
        ready = later


def attend_back(part, grads, sums, powers, queries, keys, values, before=()):
    seqs, half_rows, head_width = queries[0].shape
    rows = half_rows // 2
    heads = head_width // HEAD
    (near_grad, near_block), (far_grad, far_block) = grads
    return call(
        lambda *refs: attend_back_kernel(part, (near_block, far_block), not before, *refs),
        "attend_back",
        [ANY] * 10 + [VMEM] * len(before),
        (near_grad, far_grad, sums, powers, *queries, *keys, *values, *before),
        [VMEM] * 3,
        [like((2, seqs, rows, head_width), BF16)] + [like((seqs, head_width, 2 * half_rows), BF16)] * 2,
        (1,),
        None,
        [
            pltpu.VMEM((seqs, 2 * rows, head_width), BF16),
            pltpu.VMEM((seqs, heads, 2 * rows, 2 * HEAD), BF16),
            pltpu.VMEM((seqs, heads, 2 * rows, 2 * half_rows), BF16),
            pltpu.VMEM((seqs, 2 * rows, head_width), BF16),
            pltpu.VMEM((seqs, 2 * half_rows, head_width), BF16),
            pltpu.VMEM((seqs, 2 * half_rows, head_width), BF16),
            pltpu.SemaphoreType.DMA((seqs, 16)),
        ],
        pins=tuple(range(2, 10)),
    )


def normalize(values):
    centre = values - jnp.mean(values, axis=-1, keepdims=True)
    scale = lax.rsqrt(jnp.mean(centre * centre, axis=-1, keepdims=True) + 1e-05)
    return centre * scale, scale


def normalize_back(grad, unit, scale):
    return scale * (
        grad
        - jnp.mean(grad, axis=-1, keepdims=True)
        - unit * jnp.mean(grad * unit, axis=-1, keepdims=True)
    )


def gelu_parts(values):
    size = jnp.abs(values)
    bell = jnp.exp2(values * values * (-0.5 * LOG2E))
    t = 1.0 / (1.0 + (0.3275911 * math.sqrt(0.5)) * size)
    tail = 0.5 * 1.061405429
    for factor in (-1.453152027, 1.421413741, -0.284496736, 0.254829592):
        tail = tail * t + 0.5 * factor
    tail = tail * t * bell
    below = jnp.where(values < 0.0, tail, 1.0 - tail)
    return values * below, below + values * (bell * (1.0 / math.sqrt(2.0 * math.pi)))


def staged(count, stages):
    depth = len(stages)

    def turn(now, parity, first, last):
        for k in range(first, last):
            stages[k](now - k, (parity - k) % 2)

    for now in range(depth - 1):
        turn(now, now % 2, 0, now + 1)

    def body(step, carry):
        for p in range(2):
            turn(2 * step + p + depth - 1, (p + depth - 1) % 2, 0, depth)
        return carry

    full = count - depth + 1
    lax.fori_loop(0, full // 2, body, 0)
    for now in range(count - full % 2, count):
        turn(now, now % 2, 0, depth)
    for now in range(count, count + depth - 1):
        turn(now, now % 2, now - count + 1, depth)


def rows_kernel(order_ref, near_ref, tv_ref, cot_ref, steps_ref, table_ref, bo_ref, g1_ref, s1_ref, bd_ref, g2_ref, s2_ref, bu0, bu1, bu2, bu3, *refs):
    atts, wos, wus, wds = refs[:4], refs[4:8], refs[8:12], refs[12:16]
    part_ref = refs[16]
    out_o, gpre_o, own_o, core_o, back_own_o, back_h_o, back_y_o = refs[17:24]
    wo, wu, wd, slopes, held_a, held_b, now_a, now_b, unit_one, scale_one, total = refs[24:35]
    out_v, gpre_v, low_v, act_v, mix_v, grad_v, branch_v, back_v = refs[35:43]
    bias_up = refs[43]
    sems, out_sems = refs[44:46]
    held, now = (held_a, held_b), (now_a, now_b)
    seqs, rows, width = cot_ref.shape
    loads = [
        [pltpu.make_async_copy(s, target.at[j], sems.at[group, j]) for j, s in enumerate(sources)]
        for group, (sources, target) in enumerate(((wos, wo), (wus, wu), (wds, wd)))
    ]
    for j in range(4):
        loads[0][j].start()
    for j in range(4):
        loads[1][j].start()
        loads[2][j].start()
    for j, ref in enumerate((bu0, bu1, bu2, bu3)):
        bias_up[j : j + 1] = ref[...]
    stores = []

    def store(source, target):
        copy = pltpu.make_async_copy(source, target, out_sems.at[len(stores)])
        copy.start()
        stores.append(copy)

    for copy in loads[0]:
        copy.wait()
    for s in range(seqs):
        here = pl.ds(s * rows, rows)
        pre = near_ref[s].astype(F32) + tv_ref[s : s + 1] + bo_ref[...]
        for j in range(4):
            pre = pre + mm(atts[j][0, s], wo[j])
        unit, scale = normalize(pre)
        unit_one[here] = unit
        scale_one[here] = scale
        normed = unit * g1_ref[...] + s1_ref[...]
        low_v[here] = normed.astype(BF16)
        total[here] = normed + bd_ref[...]
    store(low_v, own_o.at[5])
    store(low_v, core_o.at[5])
    for copy in loads[1] + loads[2]:
        copy.wait()

    def where(i):
        return i // seqs, pl.ds(lax.rem(i, seqs) * rows, rows)

    def upward(i, p):
        j, here = where(i)
        held[p][...] = mm(low_v[here], wu[j]) + bias_up[pl.ds(j, 1)]

    def gelu(i, p):
        j, here = where(i)
        act, slope = gelu_parts(held[p][...])
        act = act.astype(BF16)
        now[p][...] = act
        act_v[j, here] = act
        slopes[j, here] = slope.astype(BF16)

    def downward(i, p):
        j, here = where(i)
        total[here] += mm(now[p][...], wd[j])

    staged(4 * seqs, (upward, gelu, downward))
    store(act_v.at[2:4], core_o.at[0:2])
    store(act_v.at[0:2], own_o.at[0:2])

    sums = [0.0] * 3
    for s in range(seqs):
        here = pl.ds(s * rows, rows)
        unit, scale = normalize(total[here])
        out_v[s] = (unit * g2_ref[...] + s2_ref[...]).astype(BF16)
        grad = cot_ref[s].astype(F32) * table_ref[steps_ref[s]]
        sums[1] += jnp.sum(grad * unit, axis=0, keepdims=True)
        sums[2] += jnp.sum(grad, axis=0, keepdims=True)
        grad = normalize_back(grad * g2_ref[...], unit, scale)
        mixed = grad.astype(BF16)
        mix_v[here] = mixed
        total[here] = grad
        sums[0] += jnp.sum(mixed.astype(F32), axis=0, keepdims=True)
    store(out_v, out_o)
    store(mix_v, core_o.at[4])
    store(mix_v, own_o.at[4])
    part_ref[3:6] = jnp.concatenate(sums)
    part_ref[8:16] = jnp.zeros((8, width), F32)

    def back_down(i, p):
        j, here = where(i)
        held[p][...] = mm(mix_v[here], wd[j], NT)

    def back_gelu(i, p):
        j, here = where(i)
        grad = (held[p][...] * slopes[j, here].astype(F32)).astype(BF16)
        now[p][...] = grad
        grad_v[j, here] = grad
        part_ref[pl.ds(8 + j, 1)] += jnp.sum(grad.astype(F32), axis=0, keepdims=True)

    def back_up(i, p):
        j, here = where(i)
        total[here] += mm(now[p][...], wu[j], NT)

    staged(4 * seqs, (back_down, back_gelu, back_up))
    store(grad_v.at[2:4], core_o.at[2:4])
    store(grad_v.at[0:2], own_o.at[2:4])
    sums = [0.0] * 3
    for s in range(seqs):
        here = pl.ds(s * rows, rows)
        unit, grad = unit_one[here], total[here]
        sums[1] += jnp.sum(grad * unit, axis=0, keepdims=True)
        sums[2] += jnp.sum(grad, axis=0, keepdims=True)
        grad_pre = normalize_back(grad * g1_ref[...], unit, scale_one[here])
        gpre_v[here] = grad_pre
        branch = grad_pre.astype(BF16)
        branch_v[here] = branch
        sums[0] += jnp.sum(branch.astype(F32), axis=0, keepdims=True)
        part_ref[6 + s : 7 + s] = jnp.sum(grad_pre, axis=0, keepdims=True)
        for j in range(4):
            back_v[j, s] = mm(branch, wo[j], NT).astype(BF16)
    store(back_v.at[1], back_y_o.at[0])
    store(back_v.at[3], back_y_o.at[1])
    store(back_v.at[2], back_h_o.at[0])
    store(back_v.at[0], back_own_o.at[0])
    store(branch_v, core_o.at[6])
    store(branch_v, own_o.at[6])
    store(gpre_v, gpre_o)
    part_ref[0:3] = jnp.concatenate(sums)
    for copy in stores:
        copy.wait()


def rows_part(inputs, time_vec, cotangent, timesteps, importance, vectors, bias_up, atts, wos, wus, wds, tensor):
    seqs, rows, width = cotangent.shape
    flat, hidden, head_width = seqs * rows, wus[0].shape[1], wos[0].shape[0]
    kept = [
        like((seqs, rows, width), BF16),
        like((flat, width), F32),
        pltpu.HBM((7, flat, hidden), BF16),
        pltpu.HBM((7, flat, hidden), BF16),
        pltpu.HBM((1, seqs, rows, head_width), BF16),
        pltpu.HBM((1, seqs, rows, head_width), BF16),
        pltpu.HBM((2, seqs, rows, head_width), BF16),
    ]
    return call(
        rows_kernel,
        "rows_part",
        [pl.BlockSpec((seqs, rows, width), lambda i, t: (0, t[0], 0)), VMEM, VMEM, SMEM, SMEM]
        + [VMEM] * 6
        + [VMEM] * 4
        + [pl.BlockSpec((1, seqs, rows, head_width), lambda i, t, b=b: (b, 0, 0, 0)) for _, b in atts]
        + [HBM] * 12,
        (
            inputs,
            time_vec,
            cotangent,
            timesteps,
            importance,
            *[v[None] for v in vectors],
            *[v[None] for v in bias_up],
            *[a for a, _ in atts],
            *wos,
            *wus,
            *wds,
        ),
        [VMEM] + [HBM] * len(kept),
        [like((16, width), F32)] + kept,
        (1,),
        [tensor],
        [
            pltpu.VMEM((4,) + wos[0].shape, BF16),
            pltpu.VMEM((4,) + wus[0].shape, BF16),
            pltpu.VMEM((4,) + wds[0].shape, BF16),
            pltpu.VMEM((4, flat, hidden), BF16),
            pltpu.VMEM((rows, hidden), F32),
            pltpu.VMEM((rows, hidden), F32),
            pltpu.VMEM((rows, hidden), BF16),
            pltpu.VMEM((rows, hidden), BF16),
            pltpu.VMEM((flat, width), F32),
            pltpu.VMEM((flat, 1), F32),
            pltpu.VMEM((flat, width), F32),
            pltpu.VMEM((seqs, rows, width), BF16),
            pltpu.VMEM((flat, width), F32),
            pltpu.VMEM((flat, width), BF16),
            pltpu.VMEM((4, flat, hidden), BF16),
            pltpu.VMEM((flat, width), BF16),
            pltpu.VMEM((4, flat, hidden), BF16),
            pltpu.VMEM((flat, width), BF16),
            pltpu.VMEM((4, seqs, rows, head_width), BF16),
            pltpu.VMEM((4, hidden), F32),
            pltpu.SemaphoreType.DMA((3, 4)),
            pltpu.SemaphoreType.DMA((20,)),
        ],
        pins=tuple(range(19, 30)),
    )


def weight_grad_kernel(sides, place_ref, own_ref, far_ref, send_ref, keep_ref, left, right, out, sems, out_sems):
    _, rows, width = own_ref.shape
    step = width // 2
    y_first, mine, tensor = place_ref[0], place_ref[1], place_ref[2]
    loads = {}
    for chunk in range(2):
        for number, (target, (first, chunks)) in enumerate(zip((right, left), reversed(sides))):
            if chunk < target.shape[0]:
                loads[number, chunk] = [
                    pltpu.make_async_copy(
                        ref.at[first + chunk], target.at[chunk, pl.ds(source * rows, rows)], sems.at[number, chunk, source]
                    )
                    for source, ref in enumerate((own_ref, far_ref))
                ]
                for copy in loads[number, chunk]:
                    copy.start()
    for chunk in range(2):
        for number in range(2):
            for copy in loads.get((number, chunk), ()):
                copy.wait()
        for half in range(2):
            lanes = slice(half * step, (half + 1) * step)
            spot = 2 * chunk + half
            out[spot] = mm(left[min(chunk, left.shape[0] - 1), :, lanes], right[min(chunk, right.shape[0] - 1)], TN).astype(BF16)
            tens = tensor ^ chunk
            outer = jnp.where(y_first == 1, tens, half)
            inside = jnp.where(y_first == 1, half, tens)

            @pl.when(outer != mine)
            def _():
                pltpu.make_async_copy(out.at[spot], send_ref.at[pl.ds(inside * step, step)], out_sems.at[spot]).start()

            @pl.when(outer == mine)
            def _():
                pltpu.make_async_copy(out.at[spot], keep_ref.at[pl.ds(inside * step, step)], out_sems.at[spot]).start()

    for spot in range(4):
        pltpu.make_async_copy(out.at[spot], send_ref.at[pl.ds(0, step)], out_sems.at[spot]).wait()


def weight_grad(own, far, left, right, y_first, first):
    _, rows, width = own.shape
    step = width // 2
    return call(
        lambda *refs: weight_grad_kernel((left, right), *refs),
        "weight_grad",
        [ANY, ANY],
        (own, far),
        [ANY, ANY],
        [pltpu.HBM((2 * step, width), BF16)] * 2,
        (1,),
        [y_first, first, lax.axis_index("tensor")],
        [
            pltpu.VMEM((1 + left[1], 2 * rows, width), BF16),
            pltpu.VMEM((1 + right[1], 2 * rows, width), BF16),
            pltpu.VMEM((4, step, width), BF16),
            pltpu.SemaphoreType.DMA((2, 2, 2)),
            pltpu.SemaphoreType.DMA((4,)),
        ],
        pins=(0, 1),
    )


def out_grad_kernel(own_ref, far_ref, other_ref, other_far_ref, right_ref, right_far_ref, own_out, other_out):
    count = right_ref.shape[1]

    def product(near, far):
        return (
            mm(near[...].reshape(count, -1), right_ref[0], TN)
            + mm(far[...].reshape(count, -1), right_far_ref[0], TN)
        ).astype(BF16)

    other_out[...] = product(other_ref, other_far_ref)
    own_out[...] = product(own_ref, far_ref)


def out_grad(sides, own, far, place_of):
    _, rows, width = own.shape
    head_width = sides[0][0].shape[3]
    shape = (head_width, width)
    right = pl.BlockSpec((1, rows, width), lambda i: (place_of, 0, 0))
    return call(
        out_grad_kernel,
        "out_grad",
        [pl.BlockSpec((1,) + a.shape[1:], lambda i, b=b: (b, 0, 0, 0)) for a, b in sides] + [right, right],
        (*[a for a, _ in sides], own, far),
        [VMEM, VMEM],
        [like(shape, BF16)] * 2,
        (1,),
        pins=tuple(range(6)),
    )


SHARED = 16


def padded(count):
    return -(-(SHARED + 2 * count) // 16) * 16


def put_vectors(ref, first, value):
    rows = value.shape[0]
    high = value.astype(BF16)
    low = (value - high.astype(F32)).astype(BF16)
    ref[first : first + rows] = high
    ref[first + rows : first + 2 * rows] = low
    return high.astype(F32) + low.astype(F32)


def get_vectors(ref, first, rows):
    return ref[first : first + rows].astype(F32) + ref[first + rows : first + 2 * rows].astype(F32)


def qkv_grad_kernel(place_ref, dqs_b, dqs_a, dk_ref, dv_ref, near_ref, far_ref, w_ref, out_ref, got_ref, parts_ref, feat_ref, send_ref, keep_ref, vec_ref):
    seqs, half_rows, _ = near_ref.shape
    rows = half_rows // 2
    width = dk_ref.shape[1]
    blocks = ((dqs_b, 0, near_ref, 0), (dqs_a, 0, near_ref, rows), (dqs_b, 1, far_ref, 0), (dqs_a, 1, far_ref, rows))

    def put(half, first, value):
        @pl.when(place_ref[0] == half)
        def _():
            keep_ref[first : first + width] = value

        @pl.when(place_ref[0] != half)
        def _():
            send_ref[first : first + width] = value

    for c, ref in ((1, dk_ref), (2, dv_ref)):
        grad = sum(
            mm(ref[s, :, :half_rows], near_ref[s]) + mm(ref[s, :, half_rows:], far_ref[s])
            for s in range(seqs)
        )
        put(1, (c - 1) * width, grad.astype(BF16))
    grad_q = sum(
        mm(dq[b, s], low[s, first : first + rows], TN)
        for dq, b, low, first in blocks
        for s in range(seqs)
    )
    put(0, 0, (out_ref[...].astype(F32) + got_ref[...].astype(F32)).astype(BF16))
    put(0, width, grad_q.astype(BF16))
    vec_ref[...] = jnp.zeros_like(vec_ref)
    vec_ref[0:6] = parts_ref[0:6]
    vec_ref[6:10] = parts_ref[8:12]
    ones = jnp.ones((8, rows), BF16)
    many = jnp.ones((8, 2 * half_rows), BF16)
    bias = [0.0] * 3
    for s in range(seqs):
        sums = [
            sum(mm(ones, dq[b, s]) for dq, b, _, _ in blocks),
            mm(many, dk_ref[s], NT),
            mm(many, dv_ref[s], NT),
        ]
        back = 0.0
        for c in range(3):
            bias[c] = bias[c] + sums[c][0:1]
            high = sums[c].astype(BF16)
            rest = (sums[c] - high.astype(F32)).astype(BF16)
            back = back + mm(high, w_ref[c]) + mm(rest, w_ref[c])
        vec_ref[SHARED + s : SHARED + s + 1] = parts_ref[6 + s : 7 + s] + back[0:1]
    empty = jnp.zeros((1, vec_ref.shape[1] - 2 * width), F32)
    vec_ref[10:11] = jnp.concatenate([bias[0], bias[2], empty], axis=1)
    vec_ref[SHARED + seqs : SHARED + 2 * seqs] = feat_ref[...]
    vec_ref[...] = put_vectors(send_ref, 2 * width, vec_ref[...])


def qkv_grad(dqs_b, dqs_a, dk, dv, near, far, weights, out_own, out_got, parts, feats, mine):
    seqs, _, width = near.shape
    head_width = weights.shape[1]
    return call(
        qkv_grad_kernel,
        "qkv_grad",
        [VMEM] * 11,
        (dqs_b, dqs_a, dk, dv, near, far, weights, out_own, out_got, parts, feats),
        [VMEM] * 3,
        [
            like((2 * head_width + 2 * padded(seqs), width), BF16),
            pltpu.HBM((2 * head_width, width), BF16),
            like((padded(seqs), width), F32),
        ],
        (1,),
        [mine],
    )


def input_grad_kernel(dqs_b, dqs_a, dk_ref, dv_ref, w_ref, own_ref, y_ref, far_ref):
    seqs, width, columns = dk_ref.shape
    half_rows = columns // 2
    rows = half_rows // 2
    for half in (1, 0):
        for s in range(seqs):
            lanes = slice(half * half_rows, (half + 1) * half_rows)
            part = mm(dk_ref[s, :, lanes], w_ref[1], TN) + mm(dv_ref[s, :, lanes], w_ref[2], TN)
            own = part[:rows] + mm(dqs_b[half, s], w_ref[0])
            other = part[rows:] + mm(dqs_a[half, s], w_ref[0])
            if half == 0:
                own_ref[s] = own
                y_ref[s] = other.astype(BF16)
            else:
                far_ref[0, s] = own.astype(BF16)
                far_ref[1, s] = other.astype(BF16)


def input_grad(dqs_b, dqs_a, dk, dv, weights):
    seqs, head_width, columns = dk.shape
    width, rows = weights.shape[2], columns // 4
    return call(
        input_grad_kernel,
        "input_grad",
        [VMEM] * 5,
        (dqs_b, dqs_a, dk, dv, weights),
        [VMEM] * 3,
        [
            like((seqs, rows, width), F32),
            like((seqs, rows, width), BF16),
            like((2, seqs, rows, width), BF16),
        ],
    )


def input_cross_kernel(y_ref, got_ref, out_ref):
    out_ref[...] = (y_ref[...].astype(F32) + got_ref[0].astype(F32)).astype(BF16)


def input_cross(part, got):
    seqs, rows, width = part.shape
    block = pl.BlockSpec((1, rows, width), lambda s: (s, 0, 0))
    return call(
        input_cross_kernel,
        "input_cross",
        [block, pl.BlockSpec((1, 1, rows, width), lambda s: (1, s, 0, 0))],
        (part, got),
        block,
        like(part.shape, BF16),
        (seqs,),
    )


def input_total_kernel(pre_ref, own_ref, got_ref, cross_ref, out_ref):
    out_ref[0] = pre_ref[...] + (own_ref[0] + got_ref[0, 0].astype(F32)) + cross_ref[0].astype(F32)


def input_total(pre, own, got, cross):
    seqs, rows, width = own.shape
    block = pl.BlockSpec((1, rows, width), lambda s: (s, 0, 0))
    return call(
        input_total_kernel,
        "input_total",
        [pl.BlockSpec((rows, width), lambda s: (s, 0)), block, pl.BlockSpec((1, 1, rows, width), lambda s: (0, s, 0, 0)), block],
        (pre, own, got, cross),
        block,
        pltpu.HBM(own.shape, F32),
        (seqs,),
    )


def sinusoid(step_ids, feature_count):
    halfway = feature_count // 2
    frequency = jnp.exp(-math.log(10000.0) * jnp.arange(halfway, dtype=F32) / halfway)
    angles = step_ids.astype(F32)[:, None] * frequency[None, :]
    return jnp.concatenate([jnp.cos(angles), jnp.sin(angles)], axis=1)


def halved(value, mine):
    rows = value.shape[0] // 2
    return (
        lax.dynamic_slice_in_dim(value, (1 - mine) * rows, rows, 0),
        lax.dynamic_slice_in_dim(value, mine * rows, rows, 0),
    )


def split_kernel(mine_ref, keep_send, got_send, keep_keep, got_keep, send_ref, keep_ref):
    send_ref[...] = (keep_send[...].astype(F32) + got_send[...].astype(F32)).astype(BF16)
    keep_ref[...] = (keep_keep[...].astype(F32) + got_keep[...].astype(F32)).astype(BF16)


def add_split(keep, got, mine):
    rows, width = keep.shape
    blocks = 2 if rows % 64 == 0 else 1
    step = rows // 2 // blocks
    send = pl.BlockSpec((step, width), lambda i, m: ((1 - m[0]) * blocks + i, 0))
    stay = pl.BlockSpec((step, width), lambda i, m: (m[0] * blocks + i, 0))
    out = pl.BlockSpec((step, width), lambda i, m: (i, 0))
    if step % 8:
        total = (keep.astype(F32) + got.astype(F32)).astype(BF16)
        return halved(total, mine)
    return call(
        split_kernel,
        "add_split",
        [send, send, stay, stay],
        (keep, got, keep, got),
        [out, out],
        [like((rows // 2, width), BF16)] * 2,
        (blocks,),
        [mine],
    )


def add_kernel(left, right, out_ref):
    out_ref[...] = (left[...].astype(F32) + right[...].astype(F32)).astype(BF16)


def add(left, right):
    return call(add_kernel, "add", [VMEM, VMEM], (left, right), VMEM, like(left.shape, BF16))


def join_kernel(mine_ref, value_ref, got_ref, out_ref):
    @pl.when(pl.program_id(0) == mine_ref[0])
    def _():
        out_ref[...] = value_ref[...].astype(out_ref.dtype)

    @pl.when(pl.program_id(0) != mine_ref[0])
    def _():
        out_ref[...] = got_ref[...].astype(out_ref.dtype)


def join(value, got, mine, dtype=BF16):
    rows, width = value.shape
    if rows % 8:
        out = jnp.where(mine == 0, jnp.concatenate([value, got]), jnp.concatenate([got, value]))
        return out.astype(dtype)
    whole = pl.BlockSpec((rows, width), lambda i, m: (0, 0))
    return call(
        join_kernel,
        "join",
        [whole, whole],
        (value, got),
        pl.BlockSpec((rows, width), lambda i, m: (i, 0)),
        (pltpu.HBM if dtype == F32 else like)((2 * rows, width), dtype),
        (2,),
        [mine],
    )


def joined_vectors(count, mine, value, got, inner=None):
    pieces = [value[:SHARED] + got[:SHARED]]
    for first in (SHARED, SHARED + count):
        own, other = value[first : first + count], got[first : first + count]
        low, high = jnp.where(mine == 0, own, other), jnp.where(mine == 0, other, own)
        if inner is not None:
            middle = count // 2
            a, b = low[middle:], high[:middle]
            low = jnp.concatenate([low[:middle], jnp.where(inner == 1, b, a)])
            high = jnp.concatenate([jnp.where(inner == 1, a, b), high[middle:]])
        pieces += [low, high]
    rest = padded(2 * count) - SHARED - 4 * count
    return jnp.concatenate(pieces + [jnp.zeros((rest, value.shape[1]), F32)] * (rest > 0))


def small_join_kernel(mine_ref, value_ref, got_ref, out_ref, qkv_ref):
    first = mine_ref[0] == 0
    low = jnp.where(first, value_ref[...], got_ref[...]).astype(F32)
    high = jnp.where(first, got_ref[...], value_ref[...]).astype(F32)
    count = out_ref.shape[0]
    out_ref[...] = low[:count]
    qkv_ref[:count] = low[count:]
    qkv_ref[count:] = high


def joined_vectors(count, mine, value, got, inner=None):
    pieces = [value[:SHARED] + got[:SHARED]]
    for first in (SHARED, SHARED + count):
        own, other = value[first : first + count], got[first : first + count]
        low, high = jnp.where(mine == 0, own, other), jnp.where(mine == 0, other, own)
        if inner is not None:
            middle = count // 2
            a, b = low[middle:], high[:middle]
            low = jnp.concatenate([low[:middle], jnp.where(inner == 1, b, a)])
            high = jnp.concatenate([jnp.where(inner == 1, a, b), high[middle:]])
        pieces += [low, high]
    rest = padded(2 * count) - SHARED - 4 * count
    return jnp.concatenate(pieces + [jnp.zeros((rest, value.shape[1]), F32)] * (rest > 0))


def small_join_kernel(mine_ref, value_ref, got_ref, out_ref, qkv_ref):
    first = mine_ref[0] == 0
    low = jnp.where(first, value_ref[...], got_ref[...]).astype(F32)
    high = jnp.where(first, got_ref[...], value_ref[...]).astype(F32)
    count = out_ref.shape[0]
    out_ref[...] = low[:count]
    qkv_ref[:count] = low[count:]
    qkv_ref[count:] = high


def small_join(value, got, mine):
    rows, width = value.shape
    return call(
        small_join_kernel,
        "small_join",
        [VMEM, VMEM],
        (value, got),
        [VMEM, VMEM],
        [like((rows // 2, width), F32), like((rows // 2 * 3, width), F32)],
        (1,),
        [mine],
    )


def vector_kernel(count, mine_ref, value_ref, got_ref, out_ref):
    out_ref[...] = joined_vectors(count, mine_ref[0], value_ref[...], got_ref[...])


def vector_step(value, got, mine, count):
    return call(
        lambda *refs: vector_kernel(count, *refs),
        "vector_step",
        [VMEM, VMEM],
        (value, got),
        VMEM,
        like((padded(2 * count), value.shape[1]), F32),
        (1,),
        [mine],
    )


def small_kernel(count, last, mine_ref, keep_ref, got_ref, vec_ref, *outs):
    rows = keep_ref.shape[0]
    place_before, mine = mine_ref[0], mine_ref[1]
    vectors = joined_vectors(
        count, place_before, vec_ref[...], get_vectors(got_ref, rows, vec_ref.shape[0]), mine_ref[2] if last else None
    )

    def total(first, size):
        here = pl.ds(pl.multiple_of(first, 16), size)
        return (keep_ref[here].astype(F32) + got_ref[here].astype(F32)).astype(BF16)

    if last:
        outs[0][0:rows] = total(0, rows)
        outs[-1][...] = put_vectors(outs[0], rows, vectors)
    else:
        size = rows // 2
        outs[0][0:size] = total((1 - mine) * size, size)
        outs[-1][...] = put_vectors(outs[0], size, vectors)
        outs[1][...] = total(mine * size, size)


def small_step(keep, got, vectors, count, place_before, mine, last):
    rows, width = keep.shape
    after = padded(2 * count)
    size = rows if last else rows // 2
    out = call(
        lambda *refs: small_kernel(count, last, *refs),
        "small_step",
        [VMEM] * 3,
        (keep, got, vectors),
        [VMEM] * (2 if last else 3),
        [like((size + 2 * after, width), BF16)]
        + ([] if last else [like((size, width), BF16)])
        + [like((after, width), F32)],
        (1,),
        [place_before, mine, lax.axis_index("half")],
    )
    return (out[0], None, out[1]) if last else out


def small_end_kernel(count, mine_ref, value_ref, got_ref, vec_ref, out_ref, vec_out):
    rows = out_ref.shape[0]
    vec_out[...] = joined_vectors(count, mine_ref[0], vec_ref[...], get_vectors(got_ref, rows, vec_ref.shape[0]))
    out_ref[...] = (value_ref[0:rows].astype(F32) + got_ref[0:rows].astype(F32)).astype(BF16)


def small_end(value, got, vectors, count, mine):
    rows = value.shape[0] - 2 * vectors.shape[0]
    width = value.shape[1]
    return call(
        lambda *refs: small_end_kernel(count, *refs),
        "small_end",
        [VMEM] * 3,
        (value, got, vectors),
        [VMEM] * 2,
        [like((rows, width), BF16), like((padded(2 * count), width), F32)],
        (1,),
        [mine],
    )


def fold_kernel(first, second, chunks, value_ref, got_ref, out_ref):
    out_ref[...] = value_ref[...]
    out_ref[0:6] = value_ref[0:6] + got_ref[0:6]
    out_ref[6 : 6 + chunks] = value_ref[6 : 6 + chunks] + got_ref[6 + chunks : 6 + 2 * chunks]
    out_ref[first:second] = value_ref[first:second] + got_ref[first:second]


def fold(value, got, count, chunks):
    return call(
        lambda *refs: fold_kernel(SHARED, SHARED + count, chunks, *refs),
        "fold",
        [VMEM, VMEM],
        (value, got),
        VMEM,
        like(value.shape, F32),
    )


def quarters_kernel(spot_ref, up_ref, down_ref, up_out, down_out, sems):
    count = up_out.shape[0]
    here = pl.ds(pl.multiple_of(spot_ref[0] * count, 16), count)
    copies = [
        pltpu.make_async_copy(up_ref.at[here], up_out, sems.at[0]),
        pltpu.make_async_copy(down_ref.at[here], down_out, sems.at[1]),
    ]
    for copy in copies:
        copy.start()
    for copy in copies:
        copy.wait()


def quarters(up, down, spot):
    shape = (up.shape[0] // 4, up.shape[1])
    return call(
        quarters_kernel,
        "quarters",
        [ANY, ANY],
        (up, down),
        [ANY, ANY],
        [like(shape, BF16)] * 2,
        (1,),
        [spot],
        [pltpu.SemaphoreType.DMA((2,))],
    )


def per_device(
    inputs,
    cotangent,
    src_lengths,
    tgt_mask,
    timesteps,
    importance,
    w_qkv,
    b_qv,
    w_out,
    b_out,
    gain_one,
    shift_one,
    w_up,
    b_up,
    w_down,
    b_down,
    gain_two,
    shift_two,
    w_time1,
    time_bias1,
    w_time2,
    time_bias2,
):
    Order.token, Order.pinned = None, False
    half = lax.axis_index("half")
    tensor = lax.axis_index("tensor")
    seqs, half_rows, width = inputs.shape
    rows = half_rows // lax.axis_size("tensor")
    hidden = w_up.shape[1]
    head_width = w_qkv.shape[2]
    bits = lax.axis_size("dp").bit_length() - 1

    far = swap(inputs, "core")

    spread = [(0, 1), (1, 0)]

    up_quarter, down_quarter = quarters(w_up, w_down, 2 * place(*spread[1]) + place(*spread[0]))
    up_one = swap(up_quarter, "y")
    out_one = swap(w_out, "y")
    down_one = swap(down_quarter, "y")
    bias_one = swap(b_up, "y")
    up_core, down_core = hold(swap(w_up, "core"), swap(w_down, "core"))

    features = sinusoid(timesteps, w_time1.shape[0])
    time_sum = jnp.dot(features, w_time1, precision=HIGHEST) + time_bias1
    time_vec = jnp.dot(jax.nn.silu(time_sum), w_time2, precision=HIGHEST) + time_bias2

    feats = jnp.concatenate([time_sum, features], axis=1)
    feats = jnp.pad(feats, ((0, 0), (0, width - feats.shape[1])))

    def own_first(array):
        return jnp.concatenate(
            [
                lax.dynamic_slice_in_dim(array, tensor * rows, rows, 1),
                lax.dynamic_slice_in_dim(array, (1 - tensor) * rows, rows, 1),
            ],
            axis=1,
        )

    positions = jnp.arange(half_rows, dtype=jnp.int32)
    source_live = positions[None, :] < src_lengths[:, None]
    target_live = tgt_mask == 1
    near_live = own_first(jnp.where(half == 0, source_live, target_live))
    far_live = own_first(jnp.where(half == 0, target_live, source_live))
    allowed = jnp.concatenate([near_live, far_live], axis=1)
    mask = jnp.where(
        (jnp.arange(HEAD) == 0)[None, None, :] & ~allowed[:, :, None], MASKED, 0.0
    ).astype(BF16)

    w_turned = jnp.swapaxes(w_qkv, 1, 2)
    q_near, k_near, v_near, low_near = project(inputs, time_vec, w_turned, b_qv[0], b_qv[1], tensor, (feats, mask))
    far, bias_one = hold(far, bias_one)
    bias_core, bias_two = swap(b_up, "core"), swap(bias_one, "core")
    q_far, k_far, v_far, low_far = project(far, time_vec, w_turned, b_qv[0], b_qv[1], tensor)
    queries, keys, values = (q_near, q_far), (k_near, k_far), (v_near, v_far)

    up_one, bias_core, bias_two = hold(up_one, bias_core, bias_two)
    up_got = swap(up_one, *spread[0])
    att_y, sums_a, powers_a = attend(1, queries, keys, values, mask)
    got_y = swap(att_y, "y")
    (out_one,) = hold(out_one)
    out_core = swap(out_one, "core")
    up_one = join(up_one, up_got, place(*spread[0]))
    up_got = swap(up_one, *spread[1])
    down_one, out_core = hold(down_one, out_core)
    down_got = swap(down_one, *spread[0])
    att_own, sums_b, powers_b = attend(0, queries, keys, values, mask)
    got_h = swap(att_own, "core")
    down_one = join(down_one, down_got, place(*spread[0]))
    down_got = swap(down_one, *spread[1])
    got_y, got_h = hold(got_y, got_h)
    got_far, out_two = swap(got_y, "core"), swap(w_out, "core")
    up_one = join(up_one, up_got, place(*spread[1]))
    up_three = swap(up_one, "core")
    got_far, out_two, up_three = hold(got_far, out_two, up_three)
    down_one = join(down_one, down_got, place(*spread[1]))
    outs_w = [w_out, out_one, out_two, out_core]
    ups_w = [w_up, up_one, up_core, up_three]
    downs_w = [w_down, down_one, down_core, swap(down_one, "core")]
    ups_b = [b_up, bias_one, bias_core, bias_two]
    atts = ((att_own, 0), (got_y, 0), (got_h, 1), (got_far, 1))

    (
        parts,
        outputs,
        grad_pre,
        own,
        core,
        back_own,
        back_h,
        back_y,
    ) = rows_part(
        inputs,
        time_vec,
        cotangent,
        timesteps,
        importance,
        (b_out, gain_one, shift_one, b_down, gain_two, shift_two),
        ups_b,
        atts,
        outs_w,
        ups_w,
        downs_w,
        tensor,
    )
    back_h = swap(back_h, "core")
    back_y = swap(back_y, "y")
    back_h, core = hold(back_h, core)
    far_rows = swap(core, "core")

    down_steps = [(0, "y"), ("y", 0), (1,)]
    up_steps = [(0, 1), ("y",), (1, 0)]
    small_steps = [(0, 1), (1, 0)]
    dqs_b, dk, dv = attend_back(0, ((back_own, 0), (back_h, 0)), sums_b, powers_b, queries, keys, values)
    down_send, down_keep = weight_grad(own, far_rows, (0, True), (4, False), half, place(*down_steps[0]))
    down_got = swap(down_send, *down_steps[0])
    (back_y,) = hold(back_y)
    back_d = swap(back_y, "core")
    up_send, up_keep = weight_grad(own, far_rows, (5, False), (2, True), jnp.int32(0), place(*up_steps[0]))
    up_got = swap(up_send, *up_steps[0])
    out_own, out_other = out_grad(((att_own, 0), (att_own, 1), (got_y, 0), (got_y, 1)), own, far_rows, 6)
    out_got = swap(out_other, "y")
    def step(keep, got, steps, turn):
        send, keep = add_split(keep, got, place(*steps[turn]))
        return keep, swap(send, *steps[turn])

    def collect(value, got, dims, dtype=BF16):
        return join(value, got, place(*dims), dtype)

    down_keep, down_got = step(down_keep, down_got, down_steps, 1)
    dqs_a, dk, dv = attend_back(1, ((back_y, 0), (back_d, 1)), sums_a, powers_a, queries, keys, values, (dk, dv))
    down_keep, down_got = step(down_keep, down_got, down_steps, 2)
    small_send, small_keep, vectors = qkv_grad(
        dqs_b, dqs_a, dk, dv, low_near, low_far, w_turned, out_own, out_got, parts, feats, place(*small_steps[0])
    )
    small_got = swap(small_send, *small_steps[0])
    down = add(down_keep, down_got)
    down_got = swap(down, 2)
    up_keep, up_got = step(up_keep, up_got, up_steps, 1)
    dx_own, dx_y, dx_far = input_grad(dqs_b, dqs_a, dk, dv, w_turned)
    (dx_far,) = hold(dx_far)
    dx_got = swap(dx_far, "core")
    count = seqs
    small_send, small_keep, vectors = small_step(
        small_keep, small_got, vectors, count, place(*small_steps[0]), place(*small_steps[1]), False
    )
    small_got = swap(small_send, *small_steps[1])
    count *= 2
    down = add(down, down_got)
    down_steps, up_next = [(0,), (1,)], small_steps
    if bits == 3:
        down_got = swap(down, *down_steps[1])
    dx_cross = swap(input_cross(dx_y, dx_got), "y")
    up_keep, up_got = step(up_keep, up_got, up_steps, 2)
    small_send, _, vectors = small_step(
        small_keep, small_got, vectors, count, place(*small_steps[1]), place(2), True
    )
    small_got = swap(small_send, 2)
    count *= 2
    if bits == 3:
        down = collect(down, down_got, down_steps[1])
        down_got = swap(down, *down_steps[0])
    up = add(up_keep, up_got)
    up_got = swap(up, 2)
    if bits == 3:
        grad_w_down = collect(down, down_got, down_steps[0], F32)
    grad_inputs = input_total(grad_pre, dx_own, dx_got, dx_cross)
    small, vectors = small_end(small_send, small_got, vectors, count, place(2))
    count *= 2
    if bits > 3:
        up = add(up, up_got)
        for bit in range(3, bits):
            down, up, small = (add(v, swap(v, bit)) for v in (down, up, small))
            vectors = vector_step(vectors, swap(vectors, bit), bit_of(bit), count)
            count *= 2
        down = collect(down, swap(down, *down_steps[1]), down_steps[1])
        grad_w_down = collect(down, swap(down, *down_steps[0]), down_steps[0], F32)
    small_got = swap(small, *small_steps[1])
    vectors_got = swap(vectors, "core")
    if bits == 3:
        up = add(up, up_got)
    up_got = swap(up, *up_next[1])
    small = collect(small, small_got, small_steps[1])
    small_got = swap(small, *small_steps[0])
    vectors = fold(vectors, vectors_got, count, 2)
    vectors_got = swap(vectors, "y")
    up = collect(up, up_got, up_next[1])
    up_got = swap(up, *up_next[0])
    vectors = fold(vectors, vectors_got, count, 1)
    grad_w_out, qkv = small_join(small, small_got, place(*small_steps[0]))
    grad_w_qkv = jnp.swapaxes(qkv.reshape(3, head_width, width), 1, 2)
    grad_w_up = collect(up, up_got, up_next[0], F32)

    all_grad = vectors[SHARED : SHARED + count]
    all_sum = vectors[SHARED + count : SHARED + 2 * count, : time_sum.shape[1]]
    all_features = vectors[SHARED + count : SHARED + 2 * count, time_sum.shape[1] : time_sum.shape[1] + features.shape[1]]
    gate_of = jax.nn.sigmoid(all_sum)
    all_hidden = all_sum * gate_of
    grad_w_time2 = lax.dot_general(all_hidden, all_grad, TN, precision=HIGHEST)
    grad_hidden = lax.dot_general(all_grad, w_time2, NT, precision=HIGHEST)
    grad_hidden = grad_hidden * (gate_of * (1.0 + all_sum * (1.0 - gate_of)))
    grad_w_time1 = lax.dot_general(all_features, grad_hidden, TN, precision=HIGHEST)
    return (
        outputs,
        grad_inputs,
        grad_w_qkv,
        vectors[10, : 2 * head_width].reshape(2, head_width),
        grad_w_out,
        vectors[0],
        vectors[1],
        vectors[2],
        grad_w_up,
        vectors[6, :hidden],
        grad_w_down,
        vectors[3],
        vectors[4],
        vectors[5],
        grad_w_time1,
        jnp.sum(grad_hidden, axis=0),
        grad_w_time2,
        jnp.sum(all_grad, axis=0),
    )


def solution(mesh):
    in_specs = (
        P("dp", "half", None),
        P("dp", ("half", "tensor"), None),
        P("dp"),
        P("dp", None),
        P("dp"),
        P(),
        P(None, None, ("tensor", "half")),
        P(None, ("tensor", "half")),
        P(("tensor", "half"), None),
        P(),
        P(),
        P(),
        P(None, ("tensor", "half")),
        P(("tensor", "half")),
        P(("tensor", "half"), None),
        P(),
        P(),
        P(),
        P(),
        P(),
        P(),
        P(),
    )
    out_specs = (
        P("dp", ("half", "tensor"), None),
        P("dp", ("half", "tensor"), None),
        P(None, None, ("tensor", "half")),
        P(None, ("tensor", "half")),
        P(("tensor", "half"), None),
        P(),
        P(),
        P(),
        P(None, ("tensor", "half")),
        P(("tensor", "half")),
        P(("tensor", "half"), None),
        P(),
        P(),
        P(),
        P(),
        P(),
        P(),
        P(),
    )
    return jax.shard_map(
        per_device, mesh=mesh, in_specs=in_specs, out_specs=out_specs, check_vma=False
    )
```

```python
import math

import jax
import jax.numpy as jnp
from jax import lax
from jax.experimental import pallas as pl
from jax.experimental.pallas import tpu as pltpu
from jax.sharding import PartitionSpec as P

HEAD = 64
F32 = jnp.float32
BF16 = jnp.bfloat16
HIGHEST = lax.Precision.HIGHEST
LOG2E = math.log2(math.e)
MASKED = -1e9
MIB = 1024 * 1024
GRANTS = {"rows_part": 38, "attend": 24, "attend_back": 24, "qkv_grad": 14, "weight_grad": 14}
ANY = pl.BlockSpec(memory_space=pl.ANY)
HBM = pl.BlockSpec(memory_space=pltpu.HBM)

NT = (((1,), (1,)), ((), ()))
NN = (((1,), (0,)), ((), ()))
TN = (((0,), (0,)), ((), ()))


def mm(left, right, dims=NN):
    return lax.dot_general(left, right, dims, preferred_element_type=F32)


def bit_of(dim):
    if dim == "y":
        return lax.axis_index("tensor")
    if dim == "core":
        return lax.axis_index("half")
    return (lax.axis_index("dp") >> dim) & 1


def swap(value, *dims):
    axes = ("dp", "half", "tensor")
    sizes = [lax.axis_size(a) for a in axes]
    pairs = []
    for d in range(sizes[0]):
        for h in range(2):
            for t in range(2):
                dim = dims[h % len(dims)]
                if dim == "y":
                    to = (d, h, 1 - t)
                elif dim == "core":
                    to = (d, 1 - h, t)
                else:
                    to = (d ^ (1 << dim), h, t)
                pairs.append(((d * 2 + h) * 2 + t, (to[0] * 2 + to[1]) * 2 + to[2]))
    return lax.ppermute(value, axes, pairs)


def place(*dims):
    if len(dims) == 1:
        return bit_of(dims[0])
    return jnp.where(lax.axis_index("half") == 0, bit_of(dims[0]), bit_of(dims[1]))


class Order:
    token = None
    pinned = False


def call(kernel, name, in_specs, args, out_specs, out_shape, grid=(), scalars=None, scratch_shapes=(), aliases=None, after=(), pins=()):
    tokens = (() if Order.token is None else (Order.token,)) + tuple(after)
    if Order.pinned:
        tokens = (pltpu.with_memory_space_constraint(tokens[0], pltpu.HBM), *tokens[1:])
    first = len(in_specs) + (scalars is not None)

    def body(*refs):
        kernel(*refs[:first], *refs[first + len(tokens) :])

    in_specs = list(in_specs) + [ANY] * len(tokens)
    args = [pltpu.with_memory_space_constraint(a, pltpu.HBM) if i in pins else a for i, a in enumerate(args)]
    if scalars is None:
        rest = dict(grid=grid, in_specs=in_specs, out_specs=out_specs, scratch_shapes=scratch_shapes)
    else:
        rest = dict(
            grid_spec=pltpu.PrefetchScalarGridSpec(
                num_scalar_prefetch=1,
                grid=grid,
                in_specs=in_specs,
                out_specs=out_specs,
                scratch_shapes=scratch_shapes,
            )
        )
        args = (jnp.stack(scalars).astype(jnp.int32), *args)
    out = pl.pallas_call(
        body,
        out_shape=out_shape,
        compiler_params=pltpu.CompilerParams(vmem_limit_bytes=GRANTS.get(name, 12) * MIB),
        cost_estimate=cost(name),
        input_output_aliases=aliases or {},
        name=name,
        **rest,
    )(*args, *tokens)
    several = isinstance(out, (list, tuple))
    Order.token = out[0] if several else out
    Order.pinned = not isinstance(out_shape[0] if several else out_shape, jax.ShapeDtypeStruct)
    return out


def hold(*values):
    return call(
        lambda *refs: None,
        "hold",
        [ANY] * len(values),
        values,
        [ANY] * len(values),
        [like(v.shape, v.dtype) for v in values],
        aliases={i: i for i in range(len(values))},
    )


def like(shape, dtype):
    return jax.ShapeDtypeStruct(shape, dtype)


TIMES = {'project': 1.0, 'rows_part': 24, 'attend': 1.0, 'attend_back': 9, 'weight_grad': 6, 'out_grad': 2.4}


def cost(name):
    return pl.CostEstimate(flops=int(TIMES.get(name, 0) * 1.15e9), bytes_accessed=1024, transcendentals=0)


VMEM = pl.BlockSpec(memory_space=pltpu.VMEM)
SMEM = pl.BlockSpec(memory_space=pltpu.SMEM)


def project_kernel(order_ref, x_ref, tv_ref, w_ref, bq_ref, bv_ref, q_ref, k_ref, v_ref, low_ref):
    low = (x_ref[0].astype(F32) + tv_ref[0]).astype(BF16)
    low_ref[0] = low
    q_ref[0] = ((mm(low, w_ref[0], NT) + bq_ref[...]) * (LOG2E / math.sqrt(HEAD))).astype(BF16)
    k_ref[0] = mm(low, w_ref[1], NT).astype(BF16)
    v_ref[0] = (mm(low, w_ref[2], NT) + bv_ref[...]).astype(BF16)


def project(rows, time_vec, weights, bias_q, bias_v, tensor, after=()):
    seqs, count, width = rows.shape
    head_width = weights.shape[1]
    step = count // 2
    narrow = pl.BlockSpec((1, step, head_width), lambda s, i, t: (s, i, 0))
    bias = pl.BlockSpec((1, head_width), lambda s, i, t: (0, 0))
    return call(
        project_kernel,
        "project",
        [
            pl.BlockSpec((1, step, width), lambda s, i, t: (s, i ^ t[0], 0)),
            pl.BlockSpec((1, 1, width), lambda s, i, t: (s, 0, 0)),
            pl.BlockSpec(weights.shape, lambda s, i, t: (0, 0, 0)),
            bias,
            bias,
        ],
        (rows, time_vec[:, None, :], weights, bias_q[None], bias_v[None]),
        [narrow, narrow, narrow, pl.BlockSpec((1, step, width), lambda s, i, t: (s, i, 0))],
        [like((seqs, count, head_width), BF16)] * 3 + [pltpu.HBM(rows.shape, BF16)],
        (seqs, 2),
        [tensor],
        after=after,
        pins=(0, 2),
    )


def attend_kernel(heads, qn_ref, qf_ref, kn_ref, kf_ref, vn_ref, vf_ref, mask_ref, o_ref, sum_ref, exp_ref, held, sems):
    rows = qn_ref.shape[1]
    seq = pl.program_id(0)

    def store(s, head):
        return pltpu.make_async_copy(held.at[s, head], exp_ref.at[s, head], sems.at[s, head])

    keys = jnp.concatenate([kn_ref[0], kf_ref[0]], axis=0)
    values = jnp.concatenate([vn_ref[0], vf_ref[0]], axis=0)
    queries = jnp.concatenate([qn_ref[0], qf_ref[0]], axis=0)
    ones = jnp.ones((2 * rows, HEAD), BF16)
    many = jnp.ones((keys.shape[0], HEAD), BF16)

    def scores_of(head):
        lanes = slice(head * HEAD, (head + 1) * HEAD)
        return mm(
            jnp.concatenate([queries[:, lanes], ones], axis=1),
            jnp.concatenate([keys[:, lanes], mask_ref[0]], axis=1),
            NT,
        )

    outs = []
    scores = scores_of(0)
    for head in range(heads):
        later = scores_of(head + 1) if head + 1 < heads else None
        power = jnp.exp2(scores - jnp.max(scores, axis=1, keepdims=True)).astype(BF16)
        lanes = slice(head * HEAD, (head + 1) * HEAD)
        total = mm(power, jnp.concatenate([values[:, lanes], many], axis=1))
        held[seq, head] = power
        store(seq, head).start()
        inverse = 1.0 / total[:, HEAD:]
        out = (total[:, :HEAD] * inverse).astype(BF16)
        high = inverse.astype(BF16)
        rest = (inverse - high.astype(F32)).astype(BF16)
        sum_ref[0, head] = jnp.concatenate([out, high[:, : HEAD // 2], rest[:, HEAD // 2 :]], axis=1)
        outs.append(out)
        scores = later
    out = jnp.concatenate(outs, axis=1)
    o_ref[0, 0] = out[:rows]
    o_ref[1, 0] = out[rows:]

    @pl.when(seq == pl.num_programs(0) - 1)
    def _():
        for s in range(exp_ref.shape[0]):
            for head in range(heads):
                store(s, head).wait()


def attend(part, queries, keys, values, mask):
    seqs, half_rows, head_width = queries[0].shape
    rows = half_rows // 2
    heads = head_width // HEAD
    q_spec = pl.BlockSpec((1, rows, head_width), lambda s: (s, part, 0))
    k_spec = pl.BlockSpec((1, half_rows, head_width), lambda s: (s, 0, 0))
    return call(
        lambda *refs: attend_kernel(heads, *refs),
        "attend",
        [q_spec, q_spec, k_spec, k_spec, k_spec, k_spec]
        + [pl.BlockSpec((1, 2 * half_rows, HEAD), lambda s: (s, 0, 0))],
        (*queries, *keys, *values, mask),
        [
            pl.BlockSpec((2, 1, rows, head_width), lambda s: (0, s, 0, 0)),
            pl.BlockSpec((1, heads, 2 * rows, 2 * HEAD), lambda s: (s, 0, 0, 0)),
            HBM,
        ],
        [
            like((2, seqs, rows, head_width), BF16),
            pltpu.HBM((seqs, heads, 2 * rows, 2 * HEAD), BF16),
            pltpu.HBM((seqs, heads, 2 * rows, 2 * half_rows), BF16),
        ],
        (seqs,),
        None,
        [
            pltpu.VMEM((seqs, heads, 2 * rows, 2 * half_rows), BF16),
            pltpu.SemaphoreType.DMA((seqs, heads)),
        ],
    )


def attend_back_kernel(part, blocks, first, gn_hbm, gf_hbm, sum_hbm, exp_hbm, qn_hbm, qf_hbm, kn_hbm, kf_hbm, vn_hbm, vf_hbm, *refs):
    before, (dq_ref, dk_ref, dv_ref) = refs[: 0 if first else 2], refs[-10:-7]
    grads, sums, held, queries, keys, values, sems = refs[-7:]
    seqs, heads, rows = sums.shape[0], sums.shape[1], sums.shape[2] // 2
    half_rows = keys.shape[1] // 2
    near, far = pl.ds(0, rows), pl.ds(rows, rows)
    near_keys, far_keys = pl.ds(0, half_rows), pl.ds(half_rows, half_rows)

    def copies(s):
        pairs = [
            (gn_hbm.at[blocks[0], s], grads.at[s, near]),
            (gf_hbm.at[blocks[1], s], grads.at[s, far]),
            (sum_hbm.at[s], sums.at[s]),
            (vn_hbm.at[s], values.at[s, near_keys]),
            (vf_hbm.at[s], values.at[s, far_keys]),
            (exp_hbm.at[s, 0], held.at[s, 0]),
            (kn_hbm.at[s], keys.at[s, near_keys]),
            (kf_hbm.at[s], keys.at[s, far_keys]),
            (qn_hbm.at[s, pl.ds(part * rows, rows)], queries.at[s, near]),
            (qf_hbm.at[s, pl.ds(part * rows, rows)], queries.at[s, far]),
        ] + [(exp_hbm.at[s, head], held.at[s, head]) for head in range(1, heads)]
        return [pltpu.make_async_copy(a, b, sems.at[s, i]) for i, (a, b) in enumerate(pairs)]

    loads = [copies(s) for s in range(seqs)]
    for s in range(seqs):
        for copy in loads[s]:
            copy.start()

    def prepare(unit):
        s, head = divmod(unit, heads)
        if head == 0:
            for copy in loads[s][:5]:
                copy.wait()
        lanes = slice(head * HEAD, (head + 1) * HEAD)
        kept = sums[s, head].astype(F32)
        inverse = kept[:, HEAD : HEAD + 1] + kept[:, 3 * HEAD // 2 : 3 * HEAD // 2 + 1]
        grad = (grads[s, :, lanes].astype(F32) * inverse).astype(BF16)
        inner = jnp.sum(grad.astype(F32) * kept[:, :HEAD], axis=1, keepdims=True)
        return grad, inner, mm(grad, values[s, :, lanes], NT)

    grad_q = []
    ready = prepare(0)
    for unit in range(seqs * heads):
        s, head = divmod(unit, heads)
        later = prepare(unit + 1) if unit + 1 < seqs * heads else None
        for copy in loads[s][5:10] if head == 0 else loads[s][9 + head : 10 + head]:
            copy.wait()
        lanes = slice(head * HEAD, (head + 1) * HEAD)
        grad, inner, grad_power = ready
        power = held[s, head]
        grad_scores = power * (grad_power - inner).astype(BF16)
        grad_q.append(mm(grad_scores, keys[s, :, lanes]) * (1.0 / math.sqrt(HEAD)))
        grad_k = mm(queries[s, :, lanes], grad_scores, TN) * (1.0 / LOG2E)
        grad_v = mm(grad, power, TN)
        if not first:
            grad_k = grad_k + before[0][s, lanes].astype(F32)
            grad_v = grad_v + before[1][s, lanes].astype(F32)
        dk_ref[s, lanes] = grad_k.astype(BF16)
        dv_ref[s, lanes] = grad_v.astype(BF16)
        if head == heads - 1:
            whole = jnp.concatenate(grad_q, axis=1).astype(BF16)
            dq_ref[0, s] = whole[:rows]
            dq_ref[1, s] = whole[rows:]
            grad_q = []
        ready = later


def attend_back(part, grads, sums, powers, queries, keys, values, before=()):
    seqs, half_rows, head_width = queries[0].shape
    rows = half_rows // 2
    heads = head_width // HEAD
    (near_grad, near_block), (far_grad, far_block) = grads
    return call(
        lambda *refs: attend_back_kernel(part, (near_block, far_block), not before, *refs),
        "attend_back",
        [ANY] * 10 + [VMEM] * len(before),
        (near_grad, far_grad, sums, powers, *queries, *keys, *values, *before),
        [VMEM] * 3,
        [like((2, seqs, rows, head_width), BF16)] + [like((seqs, head_width, 2 * half_rows), BF16)] * 2,
        (1,),
        None,
        [
            pltpu.VMEM((seqs, 2 * rows, head_width), BF16),
            pltpu.VMEM((seqs, heads, 2 * rows, 2 * HEAD), BF16),
            pltpu.VMEM((seqs, heads, 2 * rows, 2 * half_rows), BF16),
            pltpu.VMEM((seqs, 2 * rows, head_width), BF16),
            pltpu.VMEM((seqs, 2 * half_rows, head_width), BF16),
            pltpu.VMEM((seqs, 2 * half_rows, head_width), BF16),
            pltpu.SemaphoreType.DMA((seqs, 16)),
        ],
        pins=tuple(range(2, 10)),
    )


def normalize(values):
    centre = values - jnp.mean(values, axis=-1, keepdims=True)
    scale = lax.rsqrt(jnp.mean(centre * centre, axis=-1, keepdims=True) + 1e-05)
    return centre * scale, scale


def normalize_back(grad, unit, scale):
    return scale * (
        grad
        - jnp.mean(grad, axis=-1, keepdims=True)
        - unit * jnp.mean(grad * unit, axis=-1, keepdims=True)
    )


def gelu_parts(values):
    size = jnp.abs(values)
    bell = jnp.exp2(values * values * (-0.5 * LOG2E))
    t = 1.0 / (1.0 + (0.3275911 * math.sqrt(0.5)) * size)
    tail = 0.5 * 1.061405429
    for factor in (-1.453152027, 1.421413741, -0.284496736, 0.254829592):
        tail = tail * t + 0.5 * factor
    tail = tail * t * bell
    below = jnp.where(values < 0.0, tail, 1.0 - tail)
    return values * below, below + values * (bell * (1.0 / math.sqrt(2.0 * math.pi)))


def staged(count, stages):
    depth = len(stages)

    def turn(now, parity, first, last):
        for k in range(first, last):
            stages[k](now - k, (parity - k) % 2)

    for now in range(depth - 1):
        turn(now, now % 2, 0, now + 1)

    def body(step, carry):
        for p in range(2):
            turn(2 * step + p + depth - 1, (p + depth - 1) % 2, 0, depth)
        return carry

    full = count - depth + 1
    lax.fori_loop(0, full // 2, body, 0)
    for now in range(count - full % 2, count):
        turn(now, now % 2, 0, depth)
    for now in range(count, count + depth - 1):
        turn(now, now % 2, now - count + 1, depth)


def rows_kernel(order_ref, near_ref, tv_ref, cot_ref, steps_ref, table_ref, bo_ref, g1_ref, s1_ref, bd_ref, g2_ref, s2_ref, bu0, bu1, bu2, bu3, *refs):
    atts, wos, wus, wds = refs[:4], refs[4:8], refs[8:12], refs[12:16]
    part_ref = refs[16]
    out_o, gpre_o, own_o, core_o, back_own_o, back_h_o, back_y_o = refs[17:24]
    wo, wu, wd, slopes, held_a, held_b, now_a, now_b, unit_one, scale_one, total = refs[24:35]
    out_v, gpre_v, low_v, act_v, mix_v, grad_v, branch_v, back_v = refs[35:43]
    bias_up = refs[43]
    sems, out_sems = refs[44:46]
    held, now = (held_a, held_b), (now_a, now_b)
    seqs, rows, width = cot_ref.shape
    loads = [
        [pltpu.make_async_copy(s, target.at[j], sems.at[group, j]) for j, s in enumerate(sources)]
        for group, (sources, target) in enumerate(((wos, wo), (wus, wu), (wds, wd)))
    ]
    for j in range(4):
        loads[0][j].start()
    for j in range(4):
        loads[1][j].start()
        loads[2][j].start()
    for j, ref in enumerate((bu0, bu1, bu2, bu3)):
        bias_up[j : j + 1] = ref[...]
    stores = []

    def store(source, target):
        copy = pltpu.make_async_copy(source, target, out_sems.at[len(stores)])
        copy.start()
        stores.append(copy)

    for copy in loads[0]:
        copy.wait()
    for s in range(seqs):
        here = pl.ds(s * rows, rows)
        pre = near_ref[s].astype(F32) + tv_ref[s : s + 1] + bo_ref[...]
        for j in range(4):
            pre = pre + mm(atts[j][0, s], wo[j])
        unit, scale = normalize(pre)
        unit_one[here] = unit
        scale_one[here] = scale
        normed = unit * g1_ref[...] + s1_ref[...]
        low_v[here] = normed.astype(BF16)
        total[here] = normed + bd_ref[...]
    store(low_v, own_o.at[5])
    store(low_v, core_o.at[5])
    for copy in loads[1] + loads[2]:
        copy.wait()

    def where(i):
        return i // seqs, pl.ds(lax.rem(i, seqs) * rows, rows)

    def upward(i, p):
        j, here = where(i)
        held[p][...] = mm(low_v[here], wu[j]) + bias_up[pl.ds(j, 1)]

    def gelu(i, p):
        j, here = where(i)
        act, slope = gelu_parts(held[p][...])
        act = act.astype(BF16)
        now[p][...] = act
        act_v[j, here] = act
        slopes[j, here] = slope.astype(BF16)

    def downward(i, p):
        j, here = where(i)
        total[here] += mm(now[p][...], wd[j])

    staged(4 * seqs, (upward, gelu, downward))
    store(act_v.at[2:4], core_o.at[0:2])
    store(act_v.at[0:2], own_o.at[0:2])

    sums = [0.0] * 3
    for s in range(seqs):
        here = pl.ds(s * rows, rows)
        unit, scale = normalize(total[here])
        out_v[s] = (unit * g2_ref[...] + s2_ref[...]).astype(BF16)
        grad = cot_ref[s].astype(F32) * table_ref[steps_ref[s]]
        sums[1] += jnp.sum(grad * unit, axis=0, keepdims=True)
        sums[2] += jnp.sum(grad, axis=0, keepdims=True)
        grad = normalize_back(grad * g2_ref[...], unit, scale)
        mixed = grad.astype(BF16)
        mix_v[here] = mixed
        total[here] = grad
        sums[0] += jnp.sum(mixed.astype(F32), axis=0, keepdims=True)
    store(out_v, out_o)
    store(mix_v, core_o.at[4])
    store(mix_v, own_o.at[4])
    part_ref[3:6] = jnp.concatenate(sums)
    part_ref[8:16] = jnp.zeros((8, width), F32)

    def back_down(i, p):
        j, here = where(i)
        held[p][...] = mm(mix_v[here], wd[j], NT)

    def back_gelu(i, p):
        j, here = where(i)
        grad = (held[p][...] * slopes[j, here].astype(F32)).astype(BF16)
        now[p][...] = grad
        grad_v[j, here] = grad
        part_ref[pl.ds(8 + j, 1)] += jnp.sum(grad.astype(F32), axis=0, keepdims=True)

    def back_up(i, p):
        j, here = where(i)
        total[here] += mm(now[p][...], wu[j], NT)

    staged(4 * seqs, (back_down, back_gelu, back_up))
    store(grad_v.at[2:4], core_o.at[2:4])
    store(grad_v.at[0:2], own_o.at[2:4])
    sums = [0.0] * 3
    for s in range(seqs):
        here = pl.ds(s * rows, rows)
        unit, grad = unit_one[here], total[here]
        sums[1] += jnp.sum(grad * unit, axis=0, keepdims=True)
        sums[2] += jnp.sum(grad, axis=0, keepdims=True)
        grad_pre = normalize_back(grad * g1_ref[...], unit, scale_one[here])
        gpre_v[here] = grad_pre
        branch = grad_pre.astype(BF16)
        branch_v[here] = branch
        sums[0] += jnp.sum(branch.astype(F32), axis=0, keepdims=True)
        part_ref[6 + s : 7 + s] = jnp.sum(grad_pre, axis=0, keepdims=True)
        for j in range(4):
            back_v[j, s] = mm(branch, wo[j], NT).astype(BF16)
    store(back_v.at[1], back_y_o.at[0])
    store(back_v.at[3], back_y_o.at[1])
    store(back_v.at[2], back_h_o.at[0])
    store(back_v.at[0], back_own_o.at[0])
    store(branch_v, core_o.at[6])
    store(branch_v, own_o.at[6])
    store(gpre_v, gpre_o)
    part_ref[0:3] = jnp.concatenate(sums)
    for copy in stores:
        copy.wait()


def rows_part(inputs, time_vec, cotangent, timesteps, importance, vectors, bias_up, atts, wos, wus, wds, tensor):
    seqs, rows, width = cotangent.shape
    flat, hidden, head_width = seqs * rows, wus[0].shape[1], wos[0].shape[0]
    kept = [
        like((seqs, rows, width), BF16),
        like((flat, width), F32),
        pltpu.HBM((7, flat, hidden), BF16),
        pltpu.HBM((7, flat, hidden), BF16),
        pltpu.HBM((1, seqs, rows, head_width), BF16),
        pltpu.HBM((1, seqs, rows, head_width), BF16),
        pltpu.HBM((2, seqs, rows, head_width), BF16),
    ]
    return call(
        rows_kernel,
        "rows_part",
        [pl.BlockSpec((seqs, rows, width), lambda i, t: (0, t[0], 0)), VMEM, VMEM, SMEM, SMEM]
        + [VMEM] * 6
        + [VMEM] * 4
        + [pl.BlockSpec((1, seqs, rows, head_width), lambda i, t, b=b: (b, 0, 0, 0)) for _, b in atts]
        + [HBM] * 12,
        (
            inputs,
            time_vec,
            cotangent,
            timesteps,
            importance,
            *[v[None] for v in vectors],
            *[v[None] for v in bias_up],
            *[a for a, _ in atts],
            *wos,
            *wus,
            *wds,
        ),
        [VMEM] + [HBM] * len(kept),
        [like((16, width), F32)] + kept,
        (1,),
        [tensor],
        [
            pltpu.VMEM((4,) + wos[0].shape, BF16),
            pltpu.VMEM((4,) + wus[0].shape, BF16),
            pltpu.VMEM((4,) + wds[0].shape, BF16),
            pltpu.VMEM((4, flat, hidden), BF16),
            pltpu.VMEM((rows, hidden), F32),
            pltpu.VMEM((rows, hidden), F32),
            pltpu.VMEM((rows, hidden), BF16),
            pltpu.VMEM((rows, hidden), BF16),
            pltpu.VMEM((flat, width), F32),
            pltpu.VMEM((flat, 1), F32),
            pltpu.VMEM((flat, width), F32),
            pltpu.VMEM((seqs, rows, width), BF16),
            pltpu.VMEM((flat, width), F32),
            pltpu.VMEM((flat, width), BF16),
            pltpu.VMEM((4, flat, hidden), BF16),
            pltpu.VMEM((flat, width), BF16),
            pltpu.VMEM((4, flat, hidden), BF16),
            pltpu.VMEM((flat, width), BF16),
            pltpu.VMEM((4, seqs, rows, head_width), BF16),
            pltpu.VMEM((4, hidden), F32),
            pltpu.SemaphoreType.DMA((3, 4)),
            pltpu.SemaphoreType.DMA((20,)),
        ],
        pins=tuple(range(19, 30)),
    )


def weight_grad_kernel(sides, place_ref, own_ref, far_ref, send_ref, keep_ref, left, right, out, sems, out_sems):
    _, rows, width = own_ref.shape
    step = width // 2
    y_first, mine, tensor = place_ref[0], place_ref[1], place_ref[2]
    loads = {}
    for chunk in range(2):
        for number, (target, (first, chunks)) in enumerate(zip((right, left), reversed(sides))):
            if chunk < target.shape[0]:
                loads[number, chunk] = [
                    pltpu.make_async_copy(
                        ref.at[first + chunk], target.at[chunk, pl.ds(source * rows, rows)], sems.at[number, chunk, source]
                    )
                    for source, ref in enumerate((own_ref, far_ref))
                ]
                for copy in loads[number, chunk]:
                    copy.start()
    for chunk in range(2):
        for number in range(2):
            for copy in loads.get((number, chunk), ()):
                copy.wait()
        for half in range(2):
            lanes = slice(half * step, (half + 1) * step)
            spot = 2 * chunk + half
            out[spot] = mm(left[min(chunk, left.shape[0] - 1), :, lanes], right[min(chunk, right.shape[0] - 1)], TN).astype(BF16)
            tens = tensor ^ chunk
            outer = jnp.where(y_first == 1, tens, half)
            inside = jnp.where(y_first == 1, half, tens)

            @pl.when(outer != mine)
            def _():
                pltpu.make_async_copy(out.at[spot], send_ref.at[pl.ds(inside * step, step)], out_sems.at[spot]).start()

            @pl.when(outer == mine)
            def _():
                pltpu.make_async_copy(out.at[spot], keep_ref.at[pl.ds(inside * step, step)], out_sems.at[spot]).start()

    for spot in range(4):
        pltpu.make_async_copy(out.at[spot], send_ref.at[pl.ds(0, step)], out_sems.at[spot]).wait()


def weight_grad(own, far, left, right, y_first, first):
    _, rows, width = own.shape
    step = width // 2
    return call(
        lambda *refs: weight_grad_kernel((left, right), *refs),
        "weight_grad",
        [ANY, ANY],
        (own, far),
        [ANY, ANY],
        [pltpu.HBM((2 * step, width), BF16)] * 2,
        (1,),
        [y_first, first, lax.axis_index("tensor")],
        [
            pltpu.VMEM((1 + left[1], 2 * rows, width), BF16),
            pltpu.VMEM((1 + right[1], 2 * rows, width), BF16),
            pltpu.VMEM((4, step, width), BF16),
            pltpu.SemaphoreType.DMA((2, 2, 2)),
            pltpu.SemaphoreType.DMA((4,)),
        ],
        pins=(0, 1),
    )


def out_grad_kernel(own_ref, far_ref, other_ref, other_far_ref, right_ref, right_far_ref, own_out, other_out):
    count = right_ref.shape[1]

    def product(near, far):
        return (
            mm(near[...].reshape(count, -1), right_ref[0], TN)
            + mm(far[...].reshape(count, -1), right_far_ref[0], TN)
        ).astype(BF16)

    other_out[...] = product(other_ref, other_far_ref)
    own_out[...] = product(own_ref, far_ref)


def out_grad(sides, own, far, place_of):
    _, rows, width = own.shape
    head_width = sides[0][0].shape[3]
    shape = (head_width, width)
    right = pl.BlockSpec((1, rows, width), lambda i: (place_of, 0, 0))
    return call(
        out_grad_kernel,
        "out_grad",
        [pl.BlockSpec((1,) + a.shape[1:], lambda i, b=b: (b, 0, 0, 0)) for a, b in sides] + [right, right],
        (*[a for a, _ in sides], own, far),
        [VMEM, VMEM],
        [like(shape, BF16)] * 2,
        (1,),
        pins=tuple(range(6)),
    )


SHARED = 16


def padded(count):
    return -(-(SHARED + 2 * count) // 16) * 16


def put_vectors(ref, first, value):
    rows = value.shape[0]
    high = value.astype(BF16)
    low = (value - high.astype(F32)).astype(BF16)
    ref[first : first + rows] = high
    ref[first + rows : first + 2 * rows] = low
    return high.astype(F32) + low.astype(F32)


def get_vectors(ref, first, rows):
    return ref[first : first + rows].astype(F32) + ref[first + rows : first + 2 * rows].astype(F32)


def qkv_grad_kernel(place_ref, dqs_b, dqs_a, dk_ref, dv_ref, near_ref, far_ref, w_ref, out_ref, got_ref, parts_ref, feat_ref, send_ref, keep_ref, vec_ref):
    seqs, half_rows, _ = near_ref.shape
    rows = half_rows // 2
    width = dk_ref.shape[1]
    blocks = ((dqs_b, 0, near_ref, 0), (dqs_a, 0, near_ref, rows), (dqs_b, 1, far_ref, 0), (dqs_a, 1, far_ref, rows))

    def put(half, first, value):
        @pl.when(place_ref[0] == half)
        def _():
            keep_ref[first : first + width] = value

        @pl.when(place_ref[0] != half)
        def _():
            send_ref[first : first + width] = value

    for c, ref in ((1, dk_ref), (2, dv_ref)):
        grad = sum(
            mm(ref[s, :, :half_rows], near_ref[s]) + mm(ref[s, :, half_rows:], far_ref[s])
            for s in range(seqs)
        )
        put(1, (c - 1) * width, grad.astype(BF16))
    grad_q = sum(
        mm(dq[b, s], low[s, first : first + rows], TN)
        for dq, b, low, first in blocks
        for s in range(seqs)
    )
    put(0, 0, (out_ref[...].astype(F32) + got_ref[...].astype(F32)).astype(BF16))
    put(0, width, grad_q.astype(BF16))
    vec_ref[...] = jnp.zeros_like(vec_ref)
    vec_ref[0:6] = parts_ref[0:6]
    vec_ref[6:10] = parts_ref[8:12]
    ones = jnp.ones((8, rows), BF16)
    many = jnp.ones((8, 2 * half_rows), BF16)
    bias, back = [], 0.0
    for c in range(3):
        sums = []
        for s in range(seqs):
            if c == 0:
                sums.append(sum(mm(ones, dq[b, s]) for dq, b, _, _ in blocks)[0:1])
            else:
                sums.append(mm(many, (dk_ref, dv_ref)[c - 1][s], NT)[0:1])
        bias.append(sum(sums))
        sums = jnp.concatenate(sums)
        high = sums.astype(BF16).astype(F32)
        both = jnp.concatenate([high, sums - high]).astype(BF16)
        back = back + mm(both, w_ref[c])
    for s in range(seqs):
        vec_ref[SHARED + s : SHARED + s + 1] = parts_ref[6 + s : 7 + s] + back[s : s + 1] + back[seqs + s : seqs + s + 1]
    empty = jnp.zeros((1, vec_ref.shape[1] - 2 * width), F32)
    vec_ref[10:11] = jnp.concatenate([bias[0], bias[2], empty], axis=1)
    vec_ref[SHARED + seqs : SHARED + 2 * seqs] = feat_ref[...]
    vec_ref[...] = put_vectors(send_ref, 2 * width, vec_ref[...])


def qkv_grad(dqs_b, dqs_a, dk, dv, near, far, weights, out_own, out_got, parts, feats, mine):
    seqs, _, width = near.shape
    head_width = weights.shape[1]
    return call(
        qkv_grad_kernel,
        "qkv_grad",
        [VMEM] * 11,
        (dqs_b, dqs_a, dk, dv, near, far, weights, out_own, out_got, parts, feats),
        [VMEM] * 3,
        [
            like((2 * head_width + 2 * padded(seqs), width), BF16),
            pltpu.HBM((2 * head_width, width), BF16),
            like((padded(seqs), width), F32),
        ],
        (1,),
        [mine],
    )


def input_grad_kernel(dqs_b, dqs_a, dk_ref, dv_ref, w_ref, own_ref, y_ref, far_ref):
    seqs, width, columns = dk_ref.shape
    half_rows = columns // 2
    rows = half_rows // 2
    for half in (1, 0):
        for s in range(seqs):
            lanes = slice(half * half_rows, (half + 1) * half_rows)
            part = mm(dk_ref[s, :, lanes], w_ref[1], TN) + mm(dv_ref[s, :, lanes], w_ref[2], TN)
            own = part[:rows] + mm(dqs_b[half, s], w_ref[0])
            other = part[rows:] + mm(dqs_a[half, s], w_ref[0])
            if half == 0:
                own_ref[s] = own
                y_ref[s] = other.astype(BF16)
            else:
                far_ref[0, s] = own.astype(BF16)
                far_ref[1, s] = other.astype(BF16)


def input_grad(dqs_b, dqs_a, dk, dv, weights):
    seqs, head_width, columns = dk.shape
    width, rows = weights.shape[2], columns // 4
    return call(
        input_grad_kernel,
        "input_grad",
        [VMEM] * 5,
        (dqs_b, dqs_a, dk, dv, weights),
        [VMEM] * 3,
        [
            like((seqs, rows, width), F32),
            like((seqs, rows, width), BF16),
            like((2, seqs, rows, width), BF16),
        ],
    )


def input_cross_kernel(y_ref, got_ref, out_ref):
    out_ref[...] = (y_ref[...].astype(F32) + got_ref[0].astype(F32)).astype(BF16)


def input_cross(part, got):
    seqs, rows, width = part.shape
    block = pl.BlockSpec((1, rows, width), lambda s: (s, 0, 0))
    return call(
        input_cross_kernel,
        "input_cross",
        [block, pl.BlockSpec((1, 1, rows, width), lambda s: (1, s, 0, 0))],
        (part, got),
        block,
        like(part.shape, BF16),
        (seqs,),
    )


def input_total_kernel(pre_ref, own_ref, got_ref, cross_ref, out_ref):
    out_ref[0] = pre_ref[...] + (own_ref[0] + got_ref[0, 0].astype(F32)) + cross_ref[0].astype(F32)


def input_total(pre, own, got, cross):
    seqs, rows, width = own.shape
    block = pl.BlockSpec((1, rows, width), lambda s: (s, 0, 0))
    return call(
        input_total_kernel,
        "input_total",
        [pl.BlockSpec((rows, width), lambda s: (s, 0)), block, pl.BlockSpec((1, 1, rows, width), lambda s: (0, s, 0, 0)), block],
        (pre, own, got, cross),
        block,
        pltpu.HBM(own.shape, F32),
        (seqs,),
    )


def sinusoid(step_ids, feature_count):
    halfway = feature_count // 2
    frequency = jnp.exp(-math.log(10000.0) * jnp.arange(halfway, dtype=F32) / halfway)
    angles = step_ids.astype(F32)[:, None] * frequency[None, :]
    return jnp.concatenate([jnp.cos(angles), jnp.sin(angles)], axis=1)


def halved(value, mine):
    rows = value.shape[0] // 2
    return (
        lax.dynamic_slice_in_dim(value, (1 - mine) * rows, rows, 0),
        lax.dynamic_slice_in_dim(value, mine * rows, rows, 0),
    )


def split_kernel(mine_ref, keep_send, got_send, keep_keep, got_keep, send_ref, keep_ref):
    send_ref[...] = (keep_send[...].astype(F32) + got_send[...].astype(F32)).astype(BF16)
    keep_ref[...] = (keep_keep[...].astype(F32) + got_keep[...].astype(F32)).astype(BF16)


def add_split(keep, got, mine):
    rows, width = keep.shape
    blocks = 2 if rows % 64 == 0 else 1
    step = rows // 2 // blocks
    send = pl.BlockSpec((step, width), lambda i, m: ((1 - m[0]) * blocks + i, 0))
    stay = pl.BlockSpec((step, width), lambda i, m: (m[0] * blocks + i, 0))
    out = pl.BlockSpec((step, width), lambda i, m: (i, 0))
    if step % 8:
        total = (keep.astype(F32) + got.astype(F32)).astype(BF16)
        return halved(total, mine)
    return call(
        split_kernel,
        "add_split",
        [send, send, stay, stay],
        (keep, got, keep, got),
        [out, out],
        [like((rows // 2, width), BF16)] * 2,
        (blocks,),
        [mine],
    )


def add_kernel(left, right, out_ref):
    out_ref[...] = (left[...].astype(F32) + right[...].astype(F32)).astype(BF16)


def add(left, right):
    return call(add_kernel, "add", [VMEM, VMEM], (left, right), VMEM, like(left.shape, BF16))


def join_kernel(mine_ref, value_ref, got_ref, out_ref):
    @pl.when(pl.program_id(0) == mine_ref[0])
    def _():
        out_ref[...] = value_ref[...].astype(out_ref.dtype)

    @pl.when(pl.program_id(0) != mine_ref[0])
    def _():
        out_ref[...] = got_ref[...].astype(out_ref.dtype)


def join(value, got, mine, dtype=BF16):
    rows, width = value.shape
    if rows % 8:
        out = jnp.where(mine == 0, jnp.concatenate([value, got]), jnp.concatenate([got, value]))
        return out.astype(dtype)
    whole = pl.BlockSpec((rows, width), lambda i, m: (0, 0))
    return call(
        join_kernel,
        "join",
        [whole, whole],
        (value, got),
        pl.BlockSpec((rows, width), lambda i, m: (i, 0)),
        (pltpu.HBM if dtype == F32 else like)((2 * rows, width), dtype),
        (2,),
        [mine],
    )


def joined_vectors(count, mine, value, got, inner=None):
    pieces = [value[:SHARED] + got[:SHARED]]
    for first in (SHARED, SHARED + count):
        own, other = value[first : first + count], got[first : first + count]
        low, high = jnp.where(mine == 0, own, other), jnp.where(mine == 0, other, own)
        if inner is not None:
            middle = count // 2
            a, b = low[middle:], high[:middle]
            low = jnp.concatenate([low[:middle], jnp.where(inner == 1, b, a)])
            high = jnp.concatenate([jnp.where(inner == 1, a, b), high[middle:]])
        pieces += [low, high]
    rest = padded(2 * count) - SHARED - 4 * count
    return jnp.concatenate(pieces + [jnp.zeros((rest, value.shape[1]), F32)] * (rest > 0))


def small_join_kernel(mine_ref, value_ref, got_ref, out_ref, qkv_ref):
    first = mine_ref[0] == 0
    low = jnp.where(first, value_ref[...], got_ref[...]).astype(F32)
    high = jnp.where(first, got_ref[...], value_ref[...]).astype(F32)
    count = out_ref.shape[0]
    out_ref[...] = low[:count]
    qkv_ref[:count] = low[count:]
    qkv_ref[count:] = high


def joined_vectors(count, mine, value, got, inner=None):
    pieces = [value[:SHARED] + got[:SHARED]]
    for first in (SHARED, SHARED + count):
        own, other = value[first : first + count], got[first : first + count]
        low, high = jnp.where(mine == 0, own, other), jnp.where(mine == 0, other, own)
        if inner is not None:
            middle = count // 2
            a, b = low[middle:], high[:middle]
            low = jnp.concatenate([low[:middle], jnp.where(inner == 1, b, a)])
            high = jnp.concatenate([jnp.where(inner == 1, a, b), high[middle:]])
        pieces += [low, high]
    rest = padded(2 * count) - SHARED - 4 * count
    return jnp.concatenate(pieces + [jnp.zeros((rest, value.shape[1]), F32)] * (rest > 0))


def small_join_kernel(mine_ref, value_ref, got_ref, out_ref, qkv_ref):
    first = mine_ref[0] == 0
    low = jnp.where(first, value_ref[...], got_ref[...]).astype(F32)
    high = jnp.where(first, got_ref[...], value_ref[...]).astype(F32)
    count = out_ref.shape[0]
    out_ref[...] = low[:count]
    qkv_ref[:count] = low[count:]
    qkv_ref[count:] = high


def small_join(value, got, mine):
    rows, width = value.shape
    return call(
        small_join_kernel,
        "small_join",
        [VMEM, VMEM],
        (value, got),
        [VMEM, VMEM],
        [pltpu.HBM((rows // 2, width), F32), pltpu.HBM((rows // 2 * 3, width), F32)],
        (1,),
        [mine],
    )


def vector_kernel(count, mine_ref, value_ref, got_ref, out_ref):
    out_ref[...] = joined_vectors(count, mine_ref[0], value_ref[...], got_ref[...])


def vector_step(value, got, mine, count):
    return call(
        lambda *refs: vector_kernel(count, *refs),
        "vector_step",
        [VMEM, VMEM],
        (value, got),
        VMEM,
        like((padded(2 * count), value.shape[1]), F32),
        (1,),
        [mine],
    )


def small_kernel(count, last, mine_ref, keep_ref, got_ref, vec_ref, *outs):
    rows = keep_ref.shape[0]
    place_before, mine = mine_ref[0], mine_ref[1]
    vectors = joined_vectors(
        count, place_before, vec_ref[...], get_vectors(got_ref, rows, vec_ref.shape[0]), mine_ref[2] if last else None
    )

    def total(first, size):
        here = pl.ds(pl.multiple_of(first, 16), size)
        return (keep_ref[here].astype(F32) + got_ref[here].astype(F32)).astype(BF16)

    if last:
        outs[0][0:rows] = total(0, rows)
        outs[-1][...] = put_vectors(outs[0], rows, vectors)
    else:
        size = rows // 2
        outs[0][0:size] = total((1 - mine) * size, size)
        outs[-1][...] = put_vectors(outs[0], size, vectors)
        outs[1][...] = total(mine * size, size)


def small_step(keep, got, vectors, count, place_before, mine, last):
    rows, width = keep.shape
    after = padded(2 * count)
    size = rows if last else rows // 2
    out = call(
        lambda *refs: small_kernel(count, last, *refs),
        "small_step",
        [VMEM] * 3,
        (keep, got, vectors),
        [VMEM] * (2 if last else 3),
        [like((size + 2 * after, width), BF16)]
        + ([] if last else [like((size, width), BF16)])
        + [like((after, width), F32)],
        (1,),
        [place_before, mine, lax.axis_index("half")],
    )
    return (out[0], None, out[1]) if last else out


def small_end_kernel(count, mine_ref, value_ref, got_ref, vec_ref, out_ref, vec_out):
    rows = out_ref.shape[0]
    vec_out[...] = joined_vectors(count, mine_ref[0], vec_ref[...], get_vectors(got_ref, rows, vec_ref.shape[0]))
    out_ref[...] = (value_ref[0:rows].astype(F32) + got_ref[0:rows].astype(F32)).astype(BF16)


def small_end(value, got, vectors, count, mine):
    rows = value.shape[0] - 2 * vectors.shape[0]
    width = value.shape[1]
    return call(
        lambda *refs: small_end_kernel(count, *refs),
        "small_end",
        [VMEM] * 3,
        (value, got, vectors),
        [VMEM] * 2,
        [like((rows, width), BF16), like((padded(2 * count), width), F32)],
        (1,),
        [mine],
    )


def fold_kernel(first, second, chunks, value_ref, got_ref, out_ref):
    out_ref[...] = value_ref[...]
    out_ref[0:6] = value_ref[0:6] + got_ref[0:6]
    out_ref[6 : 6 + chunks] = value_ref[6 : 6 + chunks] + got_ref[6 + chunks : 6 + 2 * chunks]
    out_ref[first:second] = value_ref[first:second] + got_ref[first:second]


def fold(value, got, count, chunks):
    return call(
        lambda *refs: fold_kernel(SHARED, SHARED + count, chunks, *refs),
        "fold",
        [VMEM, VMEM],
        (value, got),
        VMEM,
        like(value.shape, F32),
    )


def quarters_kernel(spot_ref, up_ref, down_ref, up_out, down_out, sems):
    count = up_out.shape[0]
    here = pl.ds(pl.multiple_of(spot_ref[0] * count, 16), count)
    copies = [
        pltpu.make_async_copy(up_ref.at[here], up_out, sems.at[0]),
        pltpu.make_async_copy(down_ref.at[here], down_out, sems.at[1]),
    ]
    for copy in copies:
        copy.start()
    for copy in copies:
        copy.wait()


def quarters(up, down, spot):
    shape = (up.shape[0] // 4, up.shape[1])
    return call(
        quarters_kernel,
        "quarters",
        [ANY, ANY],
        (up, down),
        [ANY, ANY],
        [like(shape, BF16)] * 2,
        (1,),
        [spot],
        [pltpu.SemaphoreType.DMA((2,))],
    )


def per_device(
    inputs,
    cotangent,
    src_lengths,
    tgt_mask,
    timesteps,
    importance,
    w_qkv,
    b_qv,
    w_out,
    b_out,
    gain_one,
    shift_one,
    w_up,
    b_up,
    w_down,
    b_down,
    gain_two,
    shift_two,
    w_time1,
    time_bias1,
    w_time2,
    time_bias2,
):
    Order.token, Order.pinned = None, False
    half = lax.axis_index("half")
    tensor = lax.axis_index("tensor")
    seqs, half_rows, width = inputs.shape
    rows = half_rows // lax.axis_size("tensor")
    hidden = w_up.shape[1]
    head_width = w_qkv.shape[2]
    bits = lax.axis_size("dp").bit_length() - 1

    far = swap(inputs, "core")

    spread = [(0, 1), (1, 0)]

    up_quarter, down_quarter = quarters(w_up, w_down, 2 * place(*spread[1]) + place(*spread[0]))
    up_one = swap(up_quarter, "y")
    out_one = swap(w_out, "y")
    down_one = swap(down_quarter, "y")
    bias_one = swap(b_up, "y")
    up_core, down_core = hold(swap(w_up, "core"), swap(w_down, "core"))

    features = sinusoid(timesteps, w_time1.shape[0])
    time_sum = jnp.dot(features, w_time1, precision=HIGHEST) + time_bias1
    time_vec = jnp.dot(jax.nn.silu(time_sum), w_time2, precision=HIGHEST) + time_bias2

    feats = jnp.concatenate([time_sum, features], axis=1)
    feats = jnp.pad(feats, ((0, 0), (0, width - feats.shape[1])))

    def own_first(array):
        return jnp.concatenate(
            [
                lax.dynamic_slice_in_dim(array, tensor * rows, rows, 1),
                lax.dynamic_slice_in_dim(array, (1 - tensor) * rows, rows, 1),
            ],
            axis=1,
        )

    positions = jnp.arange(half_rows, dtype=jnp.int32)
    source_live = positions[None, :] < src_lengths[:, None]
    target_live = tgt_mask == 1
    near_live = own_first(jnp.where(half == 0, source_live, target_live))
    far_live = own_first(jnp.where(half == 0, target_live, source_live))
    allowed = jnp.concatenate([near_live, far_live], axis=1)
    mask = jnp.where(
        (jnp.arange(HEAD) == 0)[None, None, :] & ~allowed[:, :, None], MASKED, 0.0
    ).astype(BF16)

    w_turned = jnp.swapaxes(w_qkv, 1, 2)
    q_near, k_near, v_near, low_near = project(inputs, time_vec, w_turned, b_qv[0], b_qv[1], tensor, (feats, mask))
    far, bias_one = hold(far, bias_one)
    bias_core, bias_two = swap(b_up, "core"), swap(bias_one, "core")
    q_far, k_far, v_far, low_far = project(far, time_vec, w_turned, b_qv[0], b_qv[1], tensor)
    queries, keys, values = (q_near, q_far), (k_near, k_far), (v_near, v_far)

    up_one, bias_core, bias_two = hold(up_one, bias_core, bias_two)
    up_got = swap(up_one, *spread[0])
    att_y, sums_a, powers_a = attend(1, queries, keys, values, mask)
    got_y = swap(att_y, "y")
    (out_one,) = hold(out_one)
    out_core = swap(out_one, "core")
    up_one = join(up_one, up_got, place(*spread[0]))
    up_got = swap(up_one, *spread[1])
    down_one, out_core = hold(down_one, out_core)
    down_got = swap(down_one, *spread[0])
    att_own, sums_b, powers_b = attend(0, queries, keys, values, mask)
    got_h = swap(att_own, "core")
    down_one = join(down_one, down_got, place(*spread[0]))
    down_got = swap(down_one, *spread[1])
    got_y, got_h = hold(got_y, got_h)
    got_far, out_two = swap(got_y, "core"), swap(w_out, "core")
    up_one = join(up_one, up_got, place(*spread[1]))
    up_three = swap(up_one, "core")
    got_far, out_two, up_three = hold(got_far, out_two, up_three)
    down_one = join(down_one, down_got, place(*spread[1]))
    outs_w = [w_out, out_one, out_two, out_core]
    ups_w = [w_up, up_one, up_core, up_three]
    downs_w = [w_down, down_one, down_core, swap(down_one, "core")]
    ups_b = [b_up, bias_one, bias_core, bias_two]
    atts = ((att_own, 0), (got_y, 0), (got_h, 1), (got_far, 1))

    (
        parts,
        outputs,
        grad_pre,
        own,
        core,
        back_own,
        back_h,
        back_y,
    ) = rows_part(
        inputs,
        time_vec,
        cotangent,
        timesteps,
        importance,
        (b_out, gain_one, shift_one, b_down, gain_two, shift_two),
        ups_b,
        atts,
        outs_w,
        ups_w,
        downs_w,
        tensor,
    )
    back_h = swap(back_h, "core")
    back_y = swap(back_y, "y")
    back_h, core = hold(back_h, core)
    far_rows = swap(core, "core")

    down_steps = [(0, "y"), ("y", 0), (1,)]
    up_steps = [(0, 1), ("y",), (1, 0)]
    small_steps = [(0, 1), (1, 0)]
    dqs_b, dk, dv = attend_back(0, ((back_own, 0), (back_h, 0)), sums_b, powers_b, queries, keys, values)
    down_send, down_keep = weight_grad(own, far_rows, (0, True), (4, False), half, place(*down_steps[0]))
    down_got = swap(down_send, *down_steps[0])
    (back_y,) = hold(back_y)
    back_d = swap(back_y, "core")
    up_send, up_keep = weight_grad(own, far_rows, (5, False), (2, True), jnp.int32(0), place(*up_steps[0]))
    up_got = swap(up_send, *up_steps[0])
    out_own, out_other = out_grad(((att_own, 0), (att_own, 1), (got_y, 0), (got_y, 1)), own, far_rows, 6)
    out_got = swap(out_other, "y")
    def step(keep, got, steps, turn):
        send, keep = add_split(keep, got, place(*steps[turn]))
        return keep, swap(send, *steps[turn])

    def collect(value, got, dims, dtype=BF16):
        return join(value, got, place(*dims), dtype)

    down_keep, down_got = step(down_keep, down_got, down_steps, 1)
    dqs_a, dk, dv = attend_back(1, ((back_y, 0), (back_d, 1)), sums_a, powers_a, queries, keys, values, (dk, dv))
    down_keep, down_got = step(down_keep, down_got, down_steps, 2)
    small_send, small_keep, vectors = qkv_grad(
        dqs_b, dqs_a, dk, dv, low_near, low_far, w_turned, out_own, out_got, parts, feats, place(*small_steps[0])
    )
    small_got = swap(small_send, *small_steps[0])
    down = add(down_keep, down_got)
    down_got = swap(down, 2)
    up_keep, up_got = step(up_keep, up_got, up_steps, 1)
    dx_own, dx_y, dx_far = input_grad(dqs_b, dqs_a, dk, dv, w_turned)
    (dx_far,) = hold(dx_far)
    dx_got = swap(dx_far, "core")
    count = seqs
    small_send, small_keep, vectors = small_step(
        small_keep, small_got, vectors, count, place(*small_steps[0]), place(*small_steps[1]), False
    )
    small_got = swap(small_send, *small_steps[1])
    count *= 2
    down = add(down, down_got)
    down_steps, up_next = [(0,), (1,)], small_steps
    if bits == 3:
        down_got = swap(down, *down_steps[1])
    dx_cross = swap(input_cross(dx_y, dx_got), "y")
    up_keep, up_got = step(up_keep, up_got, up_steps, 2)
    small_send, _, vectors = small_step(
        small_keep, small_got, vectors, count, place(*small_steps[1]), place(2), True
    )
    small_got = swap(small_send, 2)
    count *= 2
    if bits == 3:
        down = collect(down, down_got, down_steps[1])
        down_got = swap(down, *down_steps[0])
    up = add(up_keep, up_got)
    up_got = swap(up, 2)
    if bits == 3:
        grad_w_down = collect(down, down_got, down_steps[0], F32)
    grad_inputs = input_total(grad_pre, dx_own, dx_got, dx_cross)
    small, vectors = small_end(small_send, small_got, vectors, count, place(2))
    count *= 2
    if bits > 3:
        up = add(up, up_got)
        for bit in range(3, bits):
            down, up, small = (add(v, swap(v, bit)) for v in (down, up, small))
            vectors = vector_step(vectors, swap(vectors, bit), bit_of(bit), count)
            count *= 2
        down = collect(down, swap(down, *down_steps[1]), down_steps[1])
        grad_w_down = collect(down, swap(down, *down_steps[0]), down_steps[0], F32)
    small_got = swap(small, *small_steps[1])
    vectors_got = swap(vectors, "core")
    if bits == 3:
        up = add(up, up_got)
    up_got = swap(up, *up_next[1])
    small = collect(small, small_got, small_steps[1])
    small_got = swap(small, *small_steps[0])
    vectors = fold(vectors, vectors_got, count, 2)
    vectors_got = swap(vectors, "y")
    up = collect(up, up_got, up_next[1])
    up_got = swap(up, *up_next[0])
    vectors = fold(vectors, vectors_got, count, 1)
    grad_w_out, qkv = small_join(small, small_got, place(*small_steps[0]))
    grad_w_qkv = jnp.swapaxes(qkv.reshape(3, head_width, width), 1, 2)
    grad_w_up = collect(up, up_got, up_next[0], F32)

    all_grad = vectors[SHARED : SHARED + count]
    all_sum = vectors[SHARED + count : SHARED + 2 * count, : time_sum.shape[1]]
    all_features = vectors[SHARED + count : SHARED + 2 * count, time_sum.shape[1] : time_sum.shape[1] + features.shape[1]]
    gate_of = jax.nn.sigmoid(all_sum)
    all_hidden = all_sum * gate_of
    grad_w_time2 = lax.dot_general(all_hidden, all_grad, TN, precision=HIGHEST)
    grad_hidden = lax.dot_general(all_grad, w_time2, NT, precision=HIGHEST)
    grad_hidden = grad_hidden * (gate_of * (1.0 + all_sum * (1.0 - gate_of)))
    grad_w_time1 = lax.dot_general(all_features, grad_hidden, TN, precision=HIGHEST)
    return (
        outputs,
        grad_inputs,
        grad_w_qkv,
        vectors[10, : 2 * head_width].reshape(2, head_width),
        grad_w_out,
        vectors[0],
        vectors[1],
        vectors[2],
        grad_w_up,
        vectors[6, :hidden],
        grad_w_down,
        vectors[3],
        vectors[4],
        vectors[5],
        grad_w_time1,
        jnp.sum(grad_hidden, axis=0),
        grad_w_time2,
        jnp.sum(all_grad, axis=0),
    )


def solution(mesh):
    in_specs = (
        P("dp", "half", None),
        P("dp", ("half", "tensor"), None),
        P("dp"),
        P("dp", None),
        P("dp"),
        P(),
        P(None, None, ("tensor", "half")),
        P(None, ("tensor", "half")),
        P(("tensor", "half"), None),
        P(),
        P(),
        P(),
        P(None, ("tensor", "half")),
        P(("tensor", "half")),
        P(("tensor", "half"), None),
        P(),
        P(),
        P(),
        P(),
        P(),
        P(),
        P(),
    )
    out_specs = (
        P("dp", ("half", "tensor"), None),
        P("dp", ("half", "tensor"), None),
        P(None, None, ("tensor", "half")),
        P(None, ("tensor", "half")),
        P(("tensor", "half"), None),
        P(),
        P(),
        P(),
        P(None, ("tensor", "half")),
        P(("tensor", "half")),
        P(("tensor", "half"), None),
        P(),
        P(),
        P(),
        P(),
        P(),
        P(),
        P(),
    )
    return jax.shard_map(
        per_device, mesh=mesh, in_specs=in_specs, out_specs=out_specs, check_vma=False
    )
```
